1024 devices in a mesh: row: 16 (over z), col: 32 (over x, y_hi, core), narrow: 2 (over y_lo).
Axes of the slice: x: 4, y: 8 (y_hi: 4, y_lo: 2; y = y_hi * 2 + y_lo), z: 16, core: 2. Of those that a mesh axis runs over, the one named last changes fastest.
Arguments:
- a_tiles: bfloat16 [12288, 12288], P('row', 'col'), may hold values from -0.375 to 0.375
- p_tiles: bfloat16 [12288, 3072], P('row'), may hold values from -0.4375 to 0.4375
- a_mask: int32 [64, 64], P('row', 'col'), may hold values 0 or 1
- p_mask: int32 [64, 16], P('row'), may hold values 0 or 1
Outputs:
- coarse: float32 [3072, 3072], P('row', ('col', 'narrow'))
The draws below stay inside these ranges and needn't reach their ends.
Inputs may be any that keep to these rules, and one draw needn't show every extreme that they name: `a_mask`: 0 or 1 for every block tile of the operator. `p_mask`: 0 or 1 for every block tile of the prolongator.
All inputs are finite; a program needn't handle non-finite values.
Results may differ from the reference program's by a relative error of at most 0.0003.
Values may be sent and summed in bfloat16 or wider, within the bound.
No kernel may reach another device: no remote copies, remote signals or barrier semaphores. Data moves between devices by JAX's collectives and lax.ppermute only.
A program may use at most 64 MiB of HBM per device.

```python
import jax
import jax.numpy as jnp
from jax import lax

TILE = 192
NB = 64
NF = 12288
NC = 16
NCF = 3072


def set_ends(values, rng, least, top_value):
    dims = values.shape
    index_at = [jax.random.randint(jax.random.fold_in(rng, axis), (), 0, dims[axis]) for axis in range(len(dims))]
    values = values.at[tuple(index_at)].set(least)
    longest = dims.index(max(dims))
    index_at[longest] = (index_at[longest] + 1) % dims[longest]
    return values.at[tuple(index_at)].set(top_value)


def block_levels(key, dims, shards, smallest, top_value):
    factor_of = 1.0
    for dim, shards_of in shards:
        heights = jax.random.uniform(jax.random.fold_in(jax.random.fold_in(key, 6), dim), (shards_of,), jnp.float32, smallest / len(shards), top_value / len(shards))
        factor_of = factor_of * jnp.repeat(jnp.exp(heights), dims[dim] // shards_of).reshape((-1,) + (1,) * (len(dims) - 1 - dim))
    return factor_of


def normal_values(stream_key, dims, spread, most, cuts=(), dtype=jnp.bfloat16):
    array = spread * jax.random.normal(stream_key, dims, jnp.float32)
    if cuts:
        array = array * block_levels(stream_key, dims, cuts, -0.22, 0.18)
    return jnp.clip(array, -most, most).astype(dtype)


def setup_inputs(seed: int = 0) -> dict:
    streams_of = jax.random.split(jax.random.key(seed), 5)
    a_tiles = normal_values(streams_of[0], (NF, NF), (NB * NB // 18) ** -0.5, 0.375, ((0, 16), (1, 32)))
    p_tiles = normal_values(streams_of[1], (NF, NCF), TILE ** -0.5, 0.4375, ((0, 16),))
    a_mask = set_ends((jax.random.randint(streams_of[2], (NB, NB), 0, 2) < 1).astype(jnp.int32), jax.random.fold_in(streams_of[2], 1), 0, 1)
    p_mask = set_ends((jax.random.randint(streams_of[3], (NB, NC), 0, 3) < 1).astype(jnp.int32), jax.random.fold_in(streams_of[3], 1), 0, 1)
    return {"a_tiles": a_tiles, "p_tiles": p_tiles, "a_mask": a_mask, "p_mask": p_mask}


def masked(tiles, mask):
    height, breadth = tiles.shape
    shaped = tiles.reshape(height // TILE, TILE, breadth // TILE, TILE)
    return (shaped * mask.astype(jnp.bfloat16)[:, None, :, None]).reshape(height, breadth)


def reference(a_tiles, p_tiles, a_mask, p_mask):
    a_masked = masked(a_tiles, a_mask)
    p_masked = masked(p_tiles, p_mask)
    product = jnp.dot(a_masked, p_masked, preferred_element_type=jnp.float32)
    return jnp.dot(p_masked.astype(jnp.float32).T, product, precision=lax.Precision.HIGHEST)
```

```python
import jax
import jax.numpy as jnp
from jax import lax
from jax.experimental import pallas as pl
from jax.experimental.pallas import tpu as pltpu
from jax.sharding import Mesh
from jax.sharding import PartitionSpec as P

TILE = 192
WIDE = 48
ROWS = 768
HALF = 384
FINE = 12288
COARSE = 3072
PLANES = 16
LIMIT = 32766.0
STEPS = 128.0
CODED = 80
VMEM = 48 * 1024 * 1024
F32 = jnp.float32
BF16 = jnp.bfloat16


def params():
    return pltpu.CompilerParams(vmem_limit_bytes=VMEM)


def dot_last(left, right):
    return lax.dot_general(left, right, (((1,), (1,)), ((), ())), preferred_element_type=F32)


def slice_kernel(place, mask, first, second, out):
    offset = place[1]
    tile = place[2]
    row = lax.broadcasted_iota(jnp.int32, (WIDE, 128), 0)
    lane = lax.broadcasted_iota(jnp.int32, (WIDE, 128), 1)
    pick_first = (lane == row + offset).astype(F32).astype(BF16)
    pick_second = (lane + 128 == row + offset).astype(F32).astype(BF16)
    picked = dot_last(pick_first, first[...]) + dot_last(pick_second, second[...])
    fine = lax.broadcasted_iota(jnp.int32, (1, ROWS), 1)
    present = jnp.zeros((1, ROWS), F32)
    for i in range(ROWS // TILE):
        inside = (fine >= i * TILE) & (fine < (i + 1) * TILE)
        present = jnp.where(inside, mask[i, tile].astype(F32), present)
    out[...] = (picked * present).astype(BF16)


def own_columns(p_tiles, p_mask, index):
    start = index * WIDE
    block = jnp.minimum(start // 128, COARSE // 128 - 2)
    place = jnp.stack([block, start - block * 128, start // TILE]).astype(jnp.int32)
    return pl.pallas_call(
        slice_kernel,
        out_shape=jax.ShapeDtypeStruct((WIDE, ROWS), BF16),
        grid_spec=pltpu.PrefetchScalarGridSpec(
            num_scalar_prefetch=2,
            grid=(1,),
            in_specs=[
                pl.BlockSpec((ROWS, 128), lambda g, place, mask: (0, place[0])),
                pl.BlockSpec((ROWS, 128), lambda g, place, mask: (0, place[0] + 1)),
            ],
            out_specs=pl.BlockSpec((WIDE, ROWS), lambda g, place, mask: (0, 0)),
        ),
        compiler_params=params(),
        name="own_columns",
    )(place, p_mask, p_tiles, p_tiles)


def mask_kernel(mask, tiles, out):
    width = tiles.shape[1]
    first = pl.program_id(0) * (width // TILE)
    lane = lax.broadcasted_iota(jnp.int32, (1, width), 1)
    for i in range(ROWS // TILE):
        present = jnp.zeros((1, width), F32)
        for k in range(width // TILE):
            inside = (lane >= k * TILE) & (lane < (k + 1) * TILE)
            present = jnp.where(inside, mask[i, first + k].astype(F32), present)
        rows = pl.ds(i * TILE, TILE)
        out[rows, :] = tiles[rows, :] * present.astype(BF16)


def masked(tiles, mask, width):
    height, breadth = tiles.shape
    return pl.pallas_call(
        mask_kernel,
        out_shape=jax.ShapeDtypeStruct((height, breadth), BF16),
        grid_spec=pltpu.PrefetchScalarGridSpec(
            num_scalar_prefetch=1,
            grid=(breadth // width,),
            in_specs=[pl.BlockSpec((height, width), lambda g, mask: (0, g))],
            out_specs=pl.BlockSpec((height, width), lambda g, mask: (0, g)),
        ),
        compiler_params=params(),
        name="masked_tiles",
    )(mask, tiles)


def product_kernel(place, columns, *refs):
    blocks, out = refs[:-1], refs[-1]
    total = jnp.zeros((4 * WIDE, ROWS), F32)
    for b, block in enumerate(blocks):
        plane = place[b]
        half = pl.multiple_of(place[8 + b] * HALF, HALF)
        left = columns[:, pl.ds(plane, 1), :, pl.ds(half, HALF)].reshape(4 * WIDE, HALF)
        total = total + dot_last(left, block[...])
    out[...] = total.reshape(4, WIDE, ROWS)


def product(columns, blocks, place):
    return pl.pallas_call(
        product_kernel,
        out_shape=jax.ShapeDtypeStruct((4, WIDE, ROWS), F32),
        in_specs=[pl.BlockSpec(memory_space=pltpu.SMEM)]
        + [pl.BlockSpec(memory_space=pltpu.VMEM)] * (1 + len(blocks)),
        out_specs=pl.BlockSpec(memory_space=pltpu.VMEM),
        compiler_params=params(),
        name="product",
    )(place, columns, *blocks)


def pack(values):
    tail = values[:, 128:]
    return jnp.concatenate(
        [values[:, :128], jnp.concatenate([tail[:24], tail[24:]], axis=1)], axis=0
    )


def coarse_kernel(parts, tiles, out, terms):
    @pl.when(pl.program_id(0) == 0)
    def _():
        whole = (parts[0] + parts[1]) + (parts[2] + parts[3])
        high = whole.astype(BF16)
        rest = whole - high.astype(F32)
        middle = rest.astype(BF16)
        low = (rest - middle.astype(F32)).astype(BF16)
        terms[...] = jnp.concatenate([high, middle, low], axis=0)

    full = jnp.dot(terms[...], tiles[...], preferred_element_type=F32)
    full = (full[2 * WIDE :] + full[WIDE : 2 * WIDE]) + full[:WIDE]
    for k in range(out.shape[0]):
        chunk = full[:, k * TILE : (k + 1) * TILE]
        most = jnp.maximum(jnp.max(jnp.abs(chunk), axis=0, keepdims=True), 1e-33)
        code = jnp.ceil(jnp.log2(most) * STEPS) + 1.0
        factor = LIMIT * jnp.exp2(code * (-1.0 / STEPS))
        values = pack(jnp.round(chunk * factor))
        scales = pack(jnp.broadcast_to(code, (WIDE, TILE)))
        coded = jnp.concatenate([values, scales[:1], scales[48:49], jnp.zeros((6, 128), F32)], axis=0)
        out[k] = coded.astype(jnp.int32).astype(jnp.int16)


def coarse_parts(parts, p_masked):
    width = COARSE // 4
    return pl.pallas_call(
        coarse_kernel,
        out_shape=jax.ShapeDtypeStruct((PLANES, CODED, 128), jnp.int16),
        grid=(4,),
        in_specs=[
            pl.BlockSpec((4, WIDE, ROWS), lambda g: (0, 0, 0)),
            pl.BlockSpec((ROWS, width), lambda g: (0, g)),
        ],
        out_specs=pl.BlockSpec((width // TILE, CODED, 128), lambda g: (g, 0, 0)),
        scratch_shapes=[pltpu.VMEM((3 * WIDE, ROWS), BF16)],
        compiler_params=params(),
        name="coarse_parts",
    )(parts, p_masked)


def sum_kernel(coded, out):
    total = jnp.zeros((72, 128), F32)
    for z in range(PLANES):
        block = coded[z].astype(jnp.int32).astype(F32)
        scale = jnp.exp2(block[72:80] * (1.0 / STEPS)) * (1.0 / LIMIT)
        factor = jnp.concatenate(
            [jnp.broadcast_to(scale[:1], (48, 128)), jnp.broadcast_to(scale[1:2], (24, 128))], axis=0
        )
        total = total + block[:72] * factor
    out[:, :128] = total[:48]
    out[:24, 128:] = total[48:, :64]
    out[24:, 128:] = total[48:, 64:]


def summed(coded):
    return pl.pallas_call(
        sum_kernel,
        out_shape=jax.ShapeDtypeStruct((WIDE, TILE), F32),
        in_specs=[pl.BlockSpec(memory_space=pltpu.VMEM)],
        out_specs=pl.BlockSpec(memory_space=pltpu.VMEM),
        compiler_params=params(),
        name="summed",
    )(coded)


def along_y(near):
    pairs = []
    for y in range(8):
        source = (y + near) % 8 if y % 2 else (y - near) % 8
        for core in range(2):
            pairs.append((((source // 2) * 2 + core) * 2 + source % 2, ((y // 2) * 2 + core) * 2 + y % 2))
    return pairs


def local(a_tiles, p_tiles, a_mask, p_mask):
    yh, core, yl = lax.axis_index("yh"), lax.axis_index("core"), lax.axis_index("yl")
    index = ((lax.axis_index("x") * 4 + yh) * 2 + core) * 2 + yl

    mine = own_columns(p_tiles, p_mask, index)
    gathered = lax.all_gather(mine, ("zh", "zl"))

    a_tiles, mine = lax.optimization_barrier((a_tiles, mine))
    own = masked(a_tiles, a_mask, HALF)
    ys = ("yh", "core", "yl")
    sign = 2 * yl - 1
    blocks = [own] + [lax.ppermute(own, ys, along_y(d)) for d in (1, -2, 3)]
    planes = [yh, yh + sign, yh - sign, yh + 2]
    blocks = blocks + [lax.ppermute(block, "core", [(0, 1), (1, 0)]) for block in blocks]
    planes = jnp.stack(planes + planes) % 4
    halves = jnp.stack([core] * 4 + [1 - core] * 4)
    place = jnp.concatenate([planes, halves]).astype(jnp.int32)

    p_tiles, own = lax.optimization_barrier((p_tiles, own))
    p_masked = masked(p_tiles, p_mask, COARSE // 4)

    columns = lax.all_to_all(gathered, "x", 0, 0, tiled=True).reshape(4, 4, WIDE, ROWS)
    parts = lax.all_to_all(product(columns, blocks, place), "x", 0, 0, tiled=True)
    coded = lax.all_to_all(coarse_parts(parts, p_masked), ("zh", "zl"), 0, 0, tiled=True)
    return summed(coded).T


def solution(mesh):
    fine = Mesh(mesh.devices.reshape(4, 4, 4, 4, 2, 2), ("zh", "zl", "x", "yh", "core", "yl"))
    z, col = ("zh", "zl"), ("x", "yh", "core")
    return jax.shard_map(
        local,
        mesh=fine,
        in_specs=(P(z, col), P(z, None), P(z, col), P(z, None)),
        out_specs=P(z, col + ("yl",)),
        check_vma=False,
    )
```

```python
import jax
import jax.numpy as jnp
from jax import lax
from jax.experimental import pallas as pl
from jax.experimental.pallas import tpu as pltpu
from jax.sharding import Mesh
from jax.sharding import PartitionSpec as P

TILE = 192
WIDE = 48
ROWS = 768
HALF = 384
FINE = 12288
COARSE = 3072
PLANES = 16
LIMIT = 32766.0
STEPS = 128.0
CODED = 80
VMEM = 48 * 1024 * 1024
MOST_VMEM = 62 * 1024 * 1024
SWAP = [(0, 1), (1, 0)]
F32 = jnp.float32
BF16 = jnp.bfloat16


def params():
    return pltpu.CompilerParams(vmem_limit_bytes=VMEM)


def dot_last(left, right):
    return lax.dot_general(left, right, (((1,), (1,)), ((), ())), preferred_element_type=F32)


def slice_kernel(place, mask, *refs):
    views, out = refs[:4], refs[4]
    row = lax.broadcasted_iota(jnp.int32, (WIDE, 128), 0)
    lane = lax.broadcasted_iota(jnp.int32, (WIDE, 128), 1)
    pick_first = (lane == row + place[1]).astype(F32).astype(BF16)
    pick_second = (lane + 128 == row + place[1]).astype(F32).astype(BF16)
    fine = lax.broadcasted_iota(jnp.int32, (1, ROWS), 1)
    for n in range(2):
        first, second = views[2 * n], views[2 * n + 1]
        picked = dot_last(pick_first, first[...]) + dot_last(pick_second, second[...])
        present = jnp.zeros((1, ROWS), F32)
        for i in range(ROWS // TILE):
            inside = (fine >= i * TILE) & (fine < (i + 1) * TILE)
            present = jnp.where(inside, mask[i, place[2] + 4 * n].astype(F32), present)
        out[n] = (picked * present).astype(BF16)


def two_slices(p_tiles, p_mask, first, rest):
    start = rest * WIDE
    block = jnp.minimum(start // 128, 4)
    place = jnp.stack([6 * first + block, start - block * 128, 4 * first + start // TILE])

    def view(shift):
        return pl.BlockSpec((ROWS, 128), lambda g, place, mask: (0, place[0] + shift))

    return pl.pallas_call(
        slice_kernel,
        out_shape=jax.ShapeDtypeStruct((2, WIDE, ROWS), BF16),
        grid_spec=pltpu.PrefetchScalarGridSpec(
            num_scalar_prefetch=2,
            grid=(1,),
            in_specs=[view(0), view(1), view(6), view(7)],
            out_specs=pl.BlockSpec((2, WIDE, ROWS), lambda g, place, mask: (0, 0, 0)),
        ),
        compiler_params=pltpu.CompilerParams(vmem_limit_bytes=MOST_VMEM),
        name="two_slices",
    )(place.astype(jnp.int32), p_mask, p_tiles, p_tiles, p_tiles, p_tiles)


def mask_kernel(mask, tiles, out):
    width = tiles.shape[1]
    first = pl.program_id(0) * (width // TILE)
    lane = lax.broadcasted_iota(jnp.int32, (1, width), 1)
    for i in range(ROWS // TILE):
        present = jnp.zeros((1, width), F32)
        for k in range(width // TILE):
            inside = (lane >= k * TILE) & (lane < (k + 1) * TILE)
            present = jnp.where(inside, mask[i, first + k].astype(F32), present)
        rows = pl.ds(i * TILE, TILE)
        out[rows, :] = tiles[rows, :] * present.astype(BF16)


def masked(tiles, mask, width):
    height, breadth = tiles.shape
    return pl.pallas_call(
        mask_kernel,
        out_shape=jax.ShapeDtypeStruct((height, breadth), BF16),
        grid_spec=pltpu.PrefetchScalarGridSpec(
            num_scalar_prefetch=1,
            grid=(breadth // width,),
            in_specs=[pl.BlockSpec((height, width), lambda g, mask: (0, g))],
            out_specs=pl.BlockSpec((height, width), lambda g, mask: (0, g)),
        ),
        compiler_params=params(),
        name="masked_tiles",
    )(mask, tiles)


def collect_kernel(place, near, far, whole, lower, upper):
    @pl.when(place[0] < 2)
    def _():
        lower[...], upper[...] = near[...], far[...]

    @pl.when(place[0] >= 2)
    def _():
        lower[...], upper[...] = far[...], near[...]

    whole[:2], whole[2:] = lower[...], upper[...]


def collect(near, far, zh):
    return pl.pallas_call(
        collect_kernel,
        out_shape=[jax.ShapeDtypeStruct((n, WIDE, ROWS), BF16) for n in (4, 2, 2)],
        in_specs=[pl.BlockSpec(memory_space=pltpu.SMEM)]
        + [pl.BlockSpec(memory_space=pltpu.VMEM)] * 2,
        out_specs=[pl.BlockSpec(memory_space=pltpu.VMEM)] * 3,
        compiler_params=params(),
        name="collect",
    )(zh.reshape(1).astype(jnp.int32), near, far)


def product_kernel(place, slab, above, below, lower, upper, *refs):
    blocks, out, columns = refs[:-2], refs[-2], refs[-1]
    zl = place[16]
    columns[(zl + 2) % 4] = slab[...]
    columns[(zl + 3) % 4] = above[...]
    columns[(zl + 1) % 4] = below[...]
    columns[zl, :2] = lower[...]
    columns[zl, 2:] = upper[...]
    total = jnp.zeros((4 * WIDE, ROWS), F32)
    for b, block in enumerate(blocks):
        half = pl.multiple_of(place[8 + b] * HALF, HALF)
        left = columns[place[b], :, :, pl.ds(half, HALF)].reshape(4 * WIDE, HALF)
        total = total + dot_last(left, block[...])
    out[...] = total.reshape(4, WIDE, ROWS)


def product(slabs, blocks, place):
    return pl.pallas_call(
        product_kernel,
        out_shape=jax.ShapeDtypeStruct((4, WIDE, ROWS), F32),
        in_specs=[pl.BlockSpec(memory_space=pltpu.SMEM)]
        + [pl.BlockSpec(memory_space=pltpu.VMEM)] * (len(slabs) + len(blocks)),
        out_specs=pl.BlockSpec(memory_space=pltpu.VMEM),
        scratch_shapes=[pltpu.VMEM((4, 4, WIDE, ROWS), BF16)],
        compiler_params=params(),
        name="product",
    )(place, *slabs, *blocks)


def pack(values):
    tail = values[:, 128:]
    return jnp.concatenate(
        [values[:, :128], jnp.concatenate([tail[:24], tail[24:]], axis=1)], axis=0
    )


def coarse_kernel(mask, parts, tiles, out, terms, present):
    @pl.when(pl.program_id(0) == 0)
    def _():
        whole = (parts[0] + parts[1]) + (parts[2] + parts[3])
        high = whole.astype(BF16)
        rest = whole - high.astype(F32)
        middle = rest.astype(BF16)
        low = (rest - middle.astype(F32)).astype(BF16)
        terms[...] = jnp.concatenate([high, middle, low], axis=0)

    mask_kernel(mask, tiles, present)
    full = jnp.dot(terms[...], present[...], preferred_element_type=F32)
    full = (full[2 * WIDE :] + full[WIDE : 2 * WIDE]) + full[:WIDE]
    for k in range(out.shape[0]):
        chunk = full[:, k * TILE : (k + 1) * TILE]
        most = jnp.maximum(jnp.max(jnp.abs(chunk), axis=0, keepdims=True), 1e-33)
        code = jnp.ceil(jnp.log2(most) * STEPS) + 1.0
        factor = LIMIT * jnp.exp2(code * (-1.0 / STEPS))
        values = pack(jnp.round(chunk * factor))
        scales = pack(jnp.broadcast_to(code, (WIDE, TILE)))
        coded = jnp.concatenate([values, scales[:1], scales[48:49], jnp.zeros((6, 128), F32)], axis=0)
        out[k] = coded.astype(jnp.int32).astype(jnp.int16)


def coarse_parts(parts, p_tiles, p_mask):
    width = COARSE // 4
    return pl.pallas_call(
        coarse_kernel,
        out_shape=jax.ShapeDtypeStruct((PLANES, CODED, 128), jnp.int16),
        grid_spec=pltpu.PrefetchScalarGridSpec(
            num_scalar_prefetch=1,
            grid=(4,),
            in_specs=[
                pl.BlockSpec((4, WIDE, ROWS), lambda g, mask: (0, 0, 0)),
                pl.BlockSpec((ROWS, width), lambda g, mask: (0, g)),
            ],
            out_specs=pl.BlockSpec((width // TILE, CODED, 128), lambda g, mask: (g, 0, 0)),
            scratch_shapes=[pltpu.VMEM((3 * WIDE, ROWS), BF16), pltpu.VMEM((ROWS, width), BF16)],
        ),
        compiler_params=params(),
        name="coarse_parts",
    )(p_mask, parts, p_tiles)


def sum_kernel(coded, out):
    total = jnp.zeros((72, 128), F32)
    for z in range(PLANES):
        block = coded[z].astype(jnp.int32).astype(F32)
        scale = jnp.exp2(block[72:80] * (1.0 / STEPS)) * (1.0 / LIMIT)
        factor = jnp.concatenate(
            [jnp.broadcast_to(scale[:1], (48, 128)), jnp.broadcast_to(scale[1:2], (24, 128))], axis=0
        )
        total = total + block[:72] * factor
    out[:, :128] = total[:48]
    out[:24, 128:] = total[48:, :64]
    out[24:, 128:] = total[48:, 64:]


def summed(coded):
    return pl.pallas_call(
        sum_kernel,
        out_shape=jax.ShapeDtypeStruct((WIDE, TILE), F32),
        in_specs=[pl.BlockSpec(memory_space=pltpu.VMEM)],
        out_specs=pl.BlockSpec(memory_space=pltpu.VMEM),
        compiler_params=params(),
        name="summed",
    )(coded)


def along_y(near):
    pairs = []
    for y in range(8):
        source = (y + near) % 8 if y % 2 else (y - near) % 8
        for core in range(2):
            pairs.append((((source // 2) * 2 + core) * 2 + source % 2, ((y // 2) * 2 + core) * 2 + y % 2))
    return pairs


def swapped(turn):
    return [
        ((zh * 4 + zl) * 4 + x, ((x + turn) % 4 * 4 + (zl + 2) % 4) * 4 + zh)
        for zh in range(4)
        for zl in range(4)
        for x in range(4)
    ]


def around(near):
    return [((z + near) % PLANES, z) for z in range(PLANES)]


def local(a_tiles, p_tiles, a_mask, p_mask):
    zh, zl, x = lax.axis_index("zh"), lax.axis_index("zl"), lax.axis_index("x")
    yh, core, yl = lax.axis_index("yh"), lax.axis_index("core"), lax.axis_index("yl")
    z, ys = ("zh", "zl"), ("yh", "core", "yl")

    mine = two_slices(p_tiles, p_mask, x // 2 * 2, (yh * 2 + core) * 2 + yl)
    near, far = [lax.ppermute(mine, z + ("x",), swapped(turn)) for turn in (0, 2)]
    a_tiles, mine = lax.optimization_barrier((a_tiles, mine))
    own = masked(a_tiles, a_mask, HALF)
    first, second = [lax.ppermute(own, ys, along_y(near_by)) for near_by in (1, -2)]
    other = [lax.ppermute(own, "core", SWAP)]

    slab, lower, upper = collect(near, far, zh)
    slab, lower, upper, own, first, second, other = lax.optimization_barrier(
        (slab, lower, upper, own, first, second, other)
    )
    slabs = [slab, lax.ppermute(slab, z, around(1)), lax.ppermute(slab, z, around(-1))]
    slabs += [lax.ppermute(lower, z, around(2)), lax.ppermute(upper, z, around(-2))]
    third = lax.ppermute(own, ys, along_y(3))
    other += [lax.ppermute(block, "core", SWAP) for block in (first, second, third)]

    sign = 2 * yl - 1
    blocks = [own, first, second, third] + other
    planes = [yh, yh + sign, yh - sign, yh + 2]
    planes = jnp.stack(planes + planes) % 4
    halves = jnp.stack([core] * 4 + [1 - core] * 4)
    place = jnp.concatenate([planes, halves, zl.reshape(1)]).astype(jnp.int32)

    parts = lax.all_to_all(product(slabs, blocks, place), "x", 0, 0, tiled=True)
    coded = lax.all_to_all(coarse_parts(parts, p_tiles, p_mask), z, 0, 0, tiled=True)
    return summed(coded).T


def solution(mesh):
    fine = Mesh(mesh.devices.reshape(4, 4, 4, 4, 2, 2), ("zh", "zl", "x", "yh", "core", "yl"))
    z, col = ("zh", "zl"), ("x", "yh", "core")
    return jax.shard_map(
        local,
        mesh=fine,
        in_specs=(P(z, col), P(z, None), P(z, col), P(z, None)),
        out_specs=P(z, col + ("yl",)),
        check_vma=False,
    )
```

```python
import jax
import jax.numpy as jnp
from jax import lax
from jax.experimental import pallas as pl
from jax.experimental.pallas import tpu as pltpu
from jax.sharding import Mesh
from jax.sharding import PartitionSpec as P

TILE = 192
WIDE = 48
ROWS = 768
HALF = 384
FINE = 12288
COARSE = 3072
PLANES = 16
LIMIT = 32766.0
STEPS = 128.0
CODED = 80
VMEM = 48 * 1024 * 1024
MOST_VMEM = 62 * 1024 * 1024
SWAP = [(0, 1), (1, 0)]
F32 = jnp.float32
BF16 = jnp.bfloat16


def params():
    return pltpu.CompilerParams(vmem_limit_bytes=VMEM)


def dot_last(left, right):
    return lax.dot_general(left, right, (((1,), (1,)), ((), ())), preferred_element_type=F32)


def slice_kernel(place, mask, *refs):
    views, out = refs[:4], refs[4]
    row = lax.broadcasted_iota(jnp.int32, (WIDE, 128), 0)
    lane = lax.broadcasted_iota(jnp.int32, (WIDE, 128), 1)
    pick_first = (lane == row + place[1]).astype(F32).astype(BF16)
    pick_second = (lane + 128 == row + place[1]).astype(F32).astype(BF16)
    fine = lax.broadcasted_iota(jnp.int32, (1, ROWS), 1)
    for n in range(2):
        first, second = views[2 * n], views[2 * n + 1]
        picked = dot_last(pick_first, first[...]) + dot_last(pick_second, second[...])
        present = jnp.zeros((1, ROWS), F32)
        for i in range(ROWS // TILE):
            inside = (fine >= i * TILE) & (fine < (i + 1) * TILE)
            present = jnp.where(inside, mask[i, place[2] + 4 * n].astype(F32), present)
        out[n] = (picked * present).astype(BF16)


def two_slices(p_tiles, p_mask, first, rest):
    start = rest * WIDE
    block = jnp.minimum(start // 128, 4)
    place = jnp.stack([6 * first + block, start - block * 128, 4 * first + start // TILE])

    def view(shift):
        return pl.BlockSpec((ROWS, 128), lambda g, place, mask: (0, place[0] + shift))

    return pl.pallas_call(
        slice_kernel,
        out_shape=jax.ShapeDtypeStruct((2, WIDE, ROWS), BF16),
        grid_spec=pltpu.PrefetchScalarGridSpec(
            num_scalar_prefetch=2,
            grid=(1,),
            in_specs=[view(0), view(1), view(6), view(7)],
            out_specs=pl.BlockSpec((2, WIDE, ROWS), lambda g, place, mask: (0, 0, 0)),
        ),
        compiler_params=pltpu.CompilerParams(vmem_limit_bytes=MOST_VMEM),
        name="two_slices",
    )(place.astype(jnp.int32), p_mask, p_tiles, p_tiles, p_tiles, p_tiles)


def mask_kernel(mask, tiles, out):
    width = tiles.shape[1]
    first = pl.program_id(0) * (width // TILE)
    lane = lax.broadcasted_iota(jnp.int32, (1, width), 1)
    for i in range(ROWS // TILE):
        present = jnp.zeros((1, width), F32)
        for k in range(width // TILE):
            inside = (lane >= k * TILE) & (lane < (k + 1) * TILE)
            present = jnp.where(inside, mask[i, first + k].astype(F32), present)
        rows = pl.ds(i * TILE, TILE)
        out[rows, :] = tiles[rows, :] * present.astype(BF16)


def masked(tiles, mask, width):
    height, breadth = tiles.shape
    return pl.pallas_call(
        mask_kernel,
        out_shape=jax.ShapeDtypeStruct((height, breadth), BF16),
        grid_spec=pltpu.PrefetchScalarGridSpec(
            num_scalar_prefetch=1,
            grid=(breadth // width,),
            in_specs=[pl.BlockSpec((height, width), lambda g, mask: (0, g))],
            out_specs=pl.BlockSpec((height, width), lambda g, mask: (0, g)),
        ),
        compiler_params=params(),
        name="masked_tiles",
    )(mask, tiles)


def collect_kernel(place, near, far, whole, lower, upper):
    @pl.when(place[0] < 2)
    def _():
        lower[...], upper[...] = near[...], far[...]

    @pl.when(place[0] >= 2)
    def _():
        lower[...], upper[...] = far[...], near[...]

    whole[:2], whole[2:] = lower[...], upper[...]


def collect(near, far, zh):
    return pl.pallas_call(
        collect_kernel,
        out_shape=[jax.ShapeDtypeStruct((n, WIDE, ROWS), BF16) for n in (4, 2, 2)],
        in_specs=[pl.BlockSpec(memory_space=pltpu.SMEM)]
        + [pl.BlockSpec(memory_space=pltpu.VMEM)] * 2,
        out_specs=[pl.BlockSpec(memory_space=pltpu.VMEM)] * 3,
        compiler_params=params(),
        name="collect",
    )(zh.reshape(1).astype(jnp.int32), near, far)


def product_kernel(place, slab, above, below, lower, upper, *refs):
    blocks, out, columns = refs[:-2], refs[-2], refs[-1]
    zl = place[16]
    columns[(zl + 2) % 4] = slab[...]
    columns[(zl + 3) % 4] = above[...]
    columns[(zl + 1) % 4] = below[...]
    columns[zl, :2] = lower[...]
    columns[zl, 2:] = upper[...]
    total = jnp.zeros((4 * WIDE, ROWS), F32)
    for b, block in enumerate(blocks):
        half = pl.multiple_of(place[8 + b] * HALF, HALF)
        left = columns[place[b], :, :, pl.ds(half, HALF)].reshape(4 * WIDE, HALF)
        total = total + dot_last(left, block[...])
    out[...] = total.reshape(4, WIDE, ROWS)


def product(slabs, blocks, place):
    return pl.pallas_call(
        product_kernel,
        out_shape=jax.ShapeDtypeStruct((4, WIDE, ROWS), F32),
        in_specs=[pl.BlockSpec(memory_space=pltpu.SMEM)]
        + [pl.BlockSpec(memory_space=pltpu.VMEM)] * (len(slabs) + len(blocks)),
        out_specs=pl.BlockSpec(memory_space=pltpu.VMEM),
        scratch_shapes=[pltpu.VMEM((4, 4, WIDE, ROWS), BF16)],
        compiler_params=params(),
        name="product",
    )(place, *slabs, *blocks)


def pack(values):
    tail = values[:, 128:]
    return jnp.concatenate(
        [values[:, :128], jnp.concatenate([tail[:24], tail[24:]], axis=1)], axis=0
    )


def coarse_kernel(mask, parts, tiles, out, terms, present):
    @pl.when(pl.program_id(0) == 0)
    def _():
        whole = (parts[0] + parts[1]) + (parts[2] + parts[3])
        high = whole.astype(BF16)
        rest = whole - high.astype(F32)
        middle = rest.astype(BF16)
        low = (rest - middle.astype(F32)).astype(BF16)
        terms[...] = jnp.concatenate([high, middle, low], axis=0)

    mask_kernel(mask, tiles, present)
    full = jnp.dot(terms[...], present[...], preferred_element_type=F32)
    full = (full[2 * WIDE :] + full[WIDE : 2 * WIDE]) + full[:WIDE]
    for k in range(out.shape[0]):
        chunk = full[:, k * TILE : (k + 1) * TILE]
        most = jnp.maximum(jnp.max(jnp.abs(chunk), axis=0, keepdims=True), 1e-33)
        code = jnp.ceil(jnp.log2(most) * STEPS) + 1.0
        factor = LIMIT * jnp.exp2(code * (-1.0 / STEPS))
        values = pack(jnp.round(chunk * factor))
        scales = pack(jnp.broadcast_to(code, (WIDE, TILE)))
        coded = jnp.concatenate([values, scales[:1], scales[48:49], jnp.zeros((6, 128), F32)], axis=0)
        out[k] = coded.astype(jnp.int32).astype(jnp.int16)


def coarse_parts(parts, p_tiles, p_mask):
    width = COARSE // 4
    return pl.pallas_call(
        coarse_kernel,
        out_shape=jax.ShapeDtypeStruct((PLANES, CODED, 128), jnp.int16),
        grid_spec=pltpu.PrefetchScalarGridSpec(
            num_scalar_prefetch=1,
            grid=(4,),
            in_specs=[
                pl.BlockSpec((4, WIDE, ROWS), lambda g, mask: (0, 0, 0)),
                pl.BlockSpec((ROWS, width), lambda g, mask: (0, g)),
            ],
            out_specs=pl.BlockSpec((width // TILE, CODED, 128), lambda g, mask: (g, 0, 0)),
            scratch_shapes=[pltpu.VMEM((3 * WIDE, ROWS), BF16), pltpu.VMEM((ROWS, width), BF16)],
        ),
        compiler_params=params(),
        name="coarse_parts",
    )(p_mask, parts, p_tiles)


def sum_kernel(coded, out):
    total = jnp.zeros((72, 128), F32)
    for z in range(PLANES):
        block = coded[z].astype(jnp.int32).astype(F32)
        scale = jnp.exp2(block[72:80] * (1.0 / STEPS)) * (1.0 / LIMIT)
        factor = jnp.concatenate(
            [jnp.broadcast_to(scale[:1], (48, 128)), jnp.broadcast_to(scale[1:2], (24, 128))], axis=0
        )
        total = total + block[:72] * factor
    out[:, :128] = total[:48]
    out[:24, 128:] = total[48:, :64]
    out[24:, 128:] = total[48:, 64:]


def summed(coded):
    return pl.pallas_call(
        sum_kernel,
        out_shape=jax.ShapeDtypeStruct((WIDE, TILE), F32),
        in_specs=[pl.BlockSpec(memory_space=pltpu.VMEM)],
        out_specs=pl.BlockSpec(memory_space=pltpu.VMEM),
        compiler_params=params(),
        name="summed",
    )(coded)


def along_y(near):
    pairs = []
    for y in range(8):
        source = (y + near) % 8 if y % 2 else (y - near) % 8
        for core in range(2):
            pairs.append((((source // 2) * 2 + core) * 2 + source % 2, ((y // 2) * 2 + core) * 2 + y % 2))
    return pairs


def swapped(turn):
    return [
        ((zh * 4 + zl) * 4 + x, ((x + turn) % 4 * 4 + (zl + 2) % 4) * 4 + zh)
        for zh in range(4)
        for zl in range(4)
        for x in range(4)
    ]


def around(near):
    return [((z + near) % PLANES, z) for z in range(PLANES)]


def local(a_tiles, p_tiles, a_mask, p_mask):
    zh, zl, x = lax.axis_index("zh"), lax.axis_index("zl"), lax.axis_index("x")
    yh, core, yl = lax.axis_index("yh"), lax.axis_index("core"), lax.axis_index("yl")
    z, ys = ("zh", "zl"), ("yh", "core", "yl")

    mine = two_slices(p_tiles, p_mask, x // 2 * 2, (yh * 2 + core) * 2 + yl)
    near, far = [lax.ppermute(mine, z + ("x",), swapped(turn)) for turn in (0, 2)]
    a_tiles, mine = lax.optimization_barrier((a_tiles, mine))
    own = masked(a_tiles, a_mask, HALF)
    blocks = [own] + [lax.ppermute(own, ys, along_y(near_by)) for near_by in (1, -2, 3)]

    slab, lower, upper = collect(near, far, zh)
    slab, lower, upper, blocks = lax.optimization_barrier((slab, lower, upper, blocks))
    beside = [lax.ppermute(slab, z, around(1)), lax.ppermute(slab, z, around(-1))]
    halves = [lax.ppermute(lower, z, around(2)), lax.ppermute(upper, z, around(-2))]
    halves, blocks = lax.optimization_barrier((halves, blocks))
    blocks += [lax.ppermute(block, "core", SWAP) for block in blocks]
    slabs = [slab] + beside + halves

    sign = 2 * yl - 1
    planes = [yh, yh + sign, yh - sign, yh + 2]
    planes = jnp.stack(planes + planes) % 4
    halves = jnp.stack([core] * 4 + [1 - core] * 4)
    place = jnp.concatenate([planes, halves, zl.reshape(1)]).astype(jnp.int32)

    parts = lax.all_to_all(product(slabs, blocks, place), "x", 0, 0, tiled=True)
    coded = lax.all_to_all(coarse_parts(parts, p_tiles, p_mask), z, 0, 0, tiled=True)
    return summed(coded).T


def solution(mesh):
    fine = Mesh(mesh.devices.reshape(4, 4, 4, 4, 2, 2), ("zh", "zl", "x", "yh", "core", "yl"))
    z, col = ("zh", "zl"), ("x", "yh", "core")
    return jax.shard_map(
        local,
        mesh=fine,
        in_specs=(P(z, col), P(z, None), P(z, col), P(z, None)),
        out_specs=P(z, col + ("yl",)),
        check_vma=False,
    )
```

```python
import jax
import jax.numpy as jnp
from jax import lax
from jax.experimental import pallas as pl
from jax.experimental.pallas import tpu as pltpu
from jax.sharding import Mesh
from jax.sharding import PartitionSpec as P

TILE = 192
WIDE = 48
ROWS = 768
HALF = 384
COARSE = 3072
PLANES = 16
LIMIT = 32766.0
STEPS = 128.0
LEAST = 1e-33
CODED = 80
VMEM = 48 * 1024 * 1024
MOST_VMEM = 62 * 1024 * 1024
F32 = jnp.float32
BF16 = jnp.bfloat16


def params():
    return pltpu.CompilerParams(vmem_limit_bytes=VMEM)


def dot_last(left, right):
    return lax.dot_general(left, right, (((1,), (1,)), ((), ())), preferred_element_type=F32)


def stripes_kernel(place, mask, window, out):
    core, tile, yl = place[0], 2 * place[1], place[2]
    row = lax.broadcasted_iota(jnp.int32, (WIDE, HALF), 0)
    lane = lax.broadcasted_iota(jnp.int32, (WIDE, HALF), 1)
    picks = [(lane == row + (2 * s + yl) * WIDE).astype(F32).astype(BF16) for s in range(4)]
    picked = dot_last(jnp.concatenate(picks, axis=0), window[...])
    fine = lax.broadcasted_iota(jnp.int32, (1, HALF), 1)
    for n in range(2):
        upper, lower = mask[2 * core, tile + n], mask[2 * core + 1, tile + n]
        present = jnp.where(fine < TILE, upper.astype(F32), lower.astype(F32))
        rows = slice(2 * WIDE * n, 2 * WIDE * (n + 1))
        out[rows, :] = (picked[rows] * present).astype(BF16)


def stripes(p_tiles, p_mask, core, half, yl):
    place = jnp.stack([core, half, yl]).astype(jnp.int32)
    return pl.pallas_call(
        stripes_kernel,
        out_shape=jax.ShapeDtypeStruct((4 * WIDE, HALF), BF16),
        grid_spec=pltpu.PrefetchScalarGridSpec(
            num_scalar_prefetch=2,
            grid=(1,),
            in_specs=[pl.BlockSpec((HALF, HALF), lambda g, place, mask: (place[0], place[1]))],
            out_specs=pl.BlockSpec((4 * WIDE, HALF), lambda g, place, mask: (0, 0)),
        ),
        compiler_params=pltpu.CompilerParams(vmem_limit_bytes=MOST_VMEM),
        name="stripes",
    )(place, p_mask, p_tiles)


def mask_rows(mask, tiles, out, first):
    width = tiles.shape[1]
    lane = lax.broadcasted_iota(jnp.int32, (1, width), 1)
    for i in range(ROWS // TILE):
        present = jnp.zeros((1, width), F32)
        for k in range(width // TILE):
            inside = (lane >= k * TILE) & (lane < (k + 1) * TILE)
            present = jnp.where(inside, mask(i, first + k).astype(F32), present)
        rows = slice(i * TILE, (i + 1) * TILE)
        out[rows, :] = tiles[rows, :] * present.astype(BF16)


def operator_kernel(mask, tiles, out):
    mask_rows(lambda i, k: mask[k, i], tiles, out, 0)


def masked_operator(a_tiles, a_mask):
    return pl.pallas_call(
        operator_kernel,
        out_shape=jax.ShapeDtypeStruct(a_tiles.shape, BF16),
        in_specs=[pl.BlockSpec(memory_space=pltpu.SMEM), pl.BlockSpec(memory_space=pltpu.VMEM)],
        out_specs=pl.BlockSpec(memory_space=pltpu.VMEM),
        compiler_params=params(),
        name="masked_operator",
    )(a_mask.T, a_tiles)


def collect_kernel(place, near, far, whole, lower, upper):
    @pl.when(place[0] < 2)
    def _():
        lower[...], upper[...] = near[...], far[...]

    @pl.when(place[0] >= 2)
    def _():
        lower[...], upper[...] = far[...], near[...]

    whole[: 4 * WIDE], whole[4 * WIDE :] = lower[...], upper[...]


def collect(near, far, zh):
    return pl.pallas_call(
        collect_kernel,
        out_shape=[jax.ShapeDtypeStruct((n * WIDE, HALF), BF16) for n in (8, 4, 4)],
        in_specs=[pl.BlockSpec(memory_space=pltpu.SMEM)]
        + [pl.BlockSpec(memory_space=pltpu.VMEM)] * 2,
        out_specs=[pl.BlockSpec(memory_space=pltpu.VMEM)] * 3,
        compiler_params=params(),
        name="collect",
    )(zh.reshape(1).astype(jnp.int32), near, far)


def product_kernel(place, slab, above, below, lower, upper, own, after, before, across, out, columns):
    zl, x, core = place[0], place[1], place[2]
    for y in range(4):
        rows = pl.ds(pl.multiple_of((2 * y + core) * WIDE, WIDE), WIDE)
        half = pl.ds(pl.multiple_of((2 * (y % 2) + core) * WIDE, WIDE), WIDE)
        into = slice(y * WIDE, (y + 1) * WIDE)
        columns[zl, into] = slab[rows, :]
        columns[(zl + 1) % 4, into] = above[rows, :]
        columns[(zl + 3) % 4, into] = below[rows, :]
        columns[(zl + 2) % 4, into] = (lower if y < 2 else upper)[half, :]
    total = dot_last(columns[x], own[...]) + dot_last(columns[(x + 1) % 4], after[...])
    total = total + dot_last(columns[(x + 3) % 4], before[...])
    total = total + dot_last(columns[(x + 2) % 4], across[...])
    out[...] = total.reshape(4, WIDE, ROWS)


def product(slabs, blocks, zl, x, core):
    place = jnp.stack([zl, x, core]).astype(jnp.int32)
    return pl.pallas_call(
        product_kernel,
        out_shape=jax.ShapeDtypeStruct((4, WIDE, ROWS), F32),
        in_specs=[pl.BlockSpec(memory_space=pltpu.SMEM)]
        + [pl.BlockSpec(memory_space=pltpu.VMEM)] * (len(slabs) + len(blocks)),
        out_specs=pl.BlockSpec(memory_space=pltpu.VMEM),
        scratch_shapes=[pltpu.VMEM((4, 4 * WIDE, HALF), BF16)],
        compiler_params=params(),
        name="product",
    )(place, *slabs, *blocks)


def scale_code(most):
    return jnp.ceil(jnp.log2(jnp.maximum(most, LEAST)) * STEPS) + 1.0


def encode_kernel(mine, theirs, out):
    lane = lax.broadcasted_iota(jnp.int32, (WIDE, 128), 1)
    for n in range(4):
        codes = jnp.zeros((WIDE, 128), F32)
        for g in range(ROWS // 128):
            lanes = slice(g * 128, (g + 1) * 128)
            values = mine[n, :, lanes] + theirs[n, :, lanes]
            code = scale_code(jnp.max(jnp.abs(values), axis=1, keepdims=True))
            values = jnp.round(values * (LIMIT * jnp.exp2(code * (-1.0 / STEPS))))
            out[n, :, lanes] = values.astype(jnp.int32).astype(jnp.int16)
            codes = jnp.where(lane == g, code, codes)
        out[n, :, ROWS:] = codes.astype(jnp.int32).astype(jnp.int16)


def encode(mine, theirs):
    return pl.pallas_call(
        encode_kernel,
        out_shape=jax.ShapeDtypeStruct((4, WIDE, ROWS + 128), jnp.int16),
        in_specs=[pl.BlockSpec(memory_space=pltpu.VMEM)] * 2,
        out_specs=pl.BlockSpec(memory_space=pltpu.VMEM),
        compiler_params=params(),
        name="encode",
    )(mine, theirs)


def decoded_sum(coded):
    groups = []
    scales = [
        jnp.exp2(coded[n, :, ROWS:].astype(jnp.int32).astype(F32) * (1.0 / STEPS)) * (1.0 / LIMIT)
        for n in range(4)
    ]
    for g in range(ROWS // 128):
        lanes = slice(g * 128, (g + 1) * 128)
        terms = [
            coded[n, :, lanes].astype(jnp.int32).astype(F32) * scales[n][:, g : g + 1]
            for n in range(4)
        ]
        groups.append((terms[0] + terms[1]) + (terms[2] + terms[3]))
    return jnp.concatenate(groups, axis=1)


def pack(values):
    tail = values[:, 128:]
    return jnp.concatenate(
        [values[:, :128], jnp.concatenate([tail[:24], tail[24:]], axis=1)], axis=0
    )


def coarse_kernel(mask, parts, tiles, out, terms, present):
    @pl.when(pl.program_id(0) == 0)
    def _():
        whole = decoded_sum(parts)
        high = whole.astype(BF16)
        rest = whole - high.astype(F32)
        middle = rest.astype(BF16)
        low = (rest - middle.astype(F32)).astype(BF16)
        terms[...] = jnp.concatenate([high, middle, low], axis=0)

    first = pl.program_id(0) * (tiles.shape[1] // TILE)
    mask_rows(lambda i, k: mask[i, k], tiles, present, first)
    full = jnp.dot(terms[...], present[...], preferred_element_type=F32)
    full = (full[2 * WIDE :] + full[WIDE : 2 * WIDE]) + full[:WIDE]
    for k in range(out.shape[0]):
        chunk = full[:, k * TILE : (k + 1) * TILE]
        code = scale_code(jnp.max(jnp.abs(chunk), axis=0, keepdims=True))
        factor = LIMIT * jnp.exp2(code * (-1.0 / STEPS))
        values = pack(jnp.round(chunk * factor))
        scales = pack(jnp.broadcast_to(code, (WIDE, TILE)))
        coded = jnp.concatenate([values, scales[:1], scales[48:49], jnp.zeros((6, 128), F32)], axis=0)
        out[k] = coded.astype(jnp.int32).astype(jnp.int16)


def coarse_parts(parts, p_tiles, p_mask):
    width = COARSE // 4
    return pl.pallas_call(
        coarse_kernel,
        out_shape=jax.ShapeDtypeStruct((PLANES, CODED, 128), jnp.int16),
        grid_spec=pltpu.PrefetchScalarGridSpec(
            num_scalar_prefetch=1,
            grid=(4,),
            in_specs=[
                pl.BlockSpec((4, WIDE, ROWS + 128), lambda g, mask: (0, 0, 0)),
                pl.BlockSpec((ROWS, width), lambda g, mask: (0, g)),
            ],
            out_specs=pl.BlockSpec((width // TILE, CODED, 128), lambda g, mask: (g, 0, 0)),
            scratch_shapes=[pltpu.VMEM((3 * WIDE, ROWS), BF16), pltpu.VMEM((ROWS, width), BF16)],
        ),
        compiler_params=params(),
        name="coarse_parts",
    )(p_mask, parts, p_tiles)


def sum_kernel(coded, out):
    total = jnp.zeros((72, 128), F32)
    for z in range(PLANES):
        block = coded[z].astype(jnp.int32).astype(F32)
        scale = jnp.exp2(block[72:80] * (1.0 / STEPS)) * (1.0 / LIMIT)
        factor = jnp.concatenate(
            [jnp.broadcast_to(scale[:1], (48, 128)), jnp.broadcast_to(scale[1:2], (24, 128))], axis=0
        )
        total = total + block[:72] * factor
    out[:, :128] = total[:48]
    out[:24, 128:] = total[48:, :64]
    out[24:, 128:] = total[48:, 64:]


def summed(coded):
    return pl.pallas_call(
        sum_kernel,
        out_shape=jax.ShapeDtypeStruct((WIDE, TILE), F32),
        in_specs=[pl.BlockSpec(memory_space=pltpu.VMEM)],
        out_specs=pl.BlockSpec(memory_space=pltpu.VMEM),
        compiler_params=params(),
        name="summed",
    )(coded)


def swapped(turn):
    return [
        ((zh * 4 + zl) * 4 + yh, ((yh + turn) % 4 * 4 + zh) * 4 + zl)
        for zh in range(4)
        for zl in range(4)
        for yh in range(4)
    ]


def around(size, near):
    return [((i + near) % size, i) for i in range(size)]


def local(a_tiles, p_tiles, a_mask, p_mask):
    zh, zl, x = lax.axis_index("zh"), lax.axis_index("zl"), lax.axis_index("x")
    yh, core, yl = lax.axis_index("yh"), lax.axis_index("core"), lax.axis_index("yl")
    z = ("zh", "zl")

    mine = stripes(p_tiles, p_mask, core, 2 * x + yh // 2, yl)
    near, far = [lax.ppermute(mine, z + ("yh",), swapped(turn)) for turn in (0, 2)]
    a_tiles, mine = lax.optimization_barrier((a_tiles, mine))
    own = masked_operator(a_tiles, a_mask)
    after, before = [lax.ppermute(own, "x", around(4, turn)) for turn in (1, -1)]

    slab, lower, upper, own, after, before = lax.optimization_barrier(
        (*collect(near, far, zh), own, after, before)
    )
    slabs = [slab, *[lax.ppermute(slab, z, around(PLANES, turn)) for turn in (1, -1)]]
    slabs += [lax.ppermute(lower, z, around(PLANES, 2)), lax.ppermute(upper, z, around(PLANES, -2))]
    blocks = [own, after, before, lax.ppermute(after, "x", around(4, 1))]

    theirs = lax.ppermute(product(slabs, blocks, zl, x, 1 - core), "core", [(0, 1), (1, 0)])
    coded = encode(product(slabs, blocks, zl, x, core), theirs)
    coded = lax.all_to_all(coded, "yh", 0, 0, tiled=True)
    coded = lax.all_to_all(coarse_parts(coded, p_tiles, p_mask), z, 0, 0, tiled=True)
    return summed(coded).T


def solution(mesh):
    fine = Mesh(mesh.devices.reshape(4, 4, 4, 4, 2, 2), ("zh", "zl", "x", "yh", "core", "yl"))
    z, col = ("zh", "zl"), ("x", "yh", "core")
    return jax.shard_map(
        local,
        mesh=fine,
        in_specs=(P(z, col), P(z, None), P(z, col), P(z, None)),
        out_specs=P(z, col + ("yl",)),
        check_vma=False,
    )
```

```python
import jax
import jax.numpy as jnp
from jax import lax
from jax.experimental import pallas as pl
from jax.experimental.pallas import tpu as pltpu
from jax.sharding import Mesh
from jax.sharding import PartitionSpec as P

TILE = 192
WIDE = 48
ROWS = 768
HALF = 384
COARSE = 3072
PLANES = 16
LIMIT = 32766.0
STEPS = 128.0
LEAST = 1e-33
CODED = 80
VMEM = 48 * 1024 * 1024
MOST_VMEM = 62 * 1024 * 1024
F32 = jnp.float32
BF16 = jnp.bfloat16


def params():
    return pltpu.CompilerParams(vmem_limit_bytes=VMEM)


def dot_last(left, right):
    return lax.dot_general(left, right, (((1,), (1,)), ((), ())), preferred_element_type=F32)


def stripes_kernel(place, mask, window, out):
    core, tile, yl = place[0], 4 * place[1], place[2]
    row = lax.broadcasted_iota(jnp.int32, (WIDE, HALF), 0)
    lane = lax.broadcasted_iota(jnp.int32, (WIDE, HALF), 1)
    picks = [(lane == row + (2 * s + yl) * WIDE).astype(F32).astype(BF16) for s in range(4)]
    pick = jnp.concatenate(picks, axis=0)
    fine = lax.broadcasted_iota(jnp.int32, (1, HALF), 1)
    for n in range(4):
        if n % 2 == 0:
            picked = dot_last(pick, window[:, n * TILE : n * TILE + HALF])
        upper, lower = mask[2 * core, tile + n], mask[2 * core + 1, tile + n]
        present = jnp.where(fine < TILE, upper.astype(F32), lower.astype(F32))
        part = picked[: 2 * WIDE] if n % 2 == 0 else picked[2 * WIDE :]
        out[2 * WIDE * n : 2 * WIDE * (n + 1), :] = (part * present).astype(BF16)


def stripes(p_tiles, p_mask, core, x, yl):
    place = jnp.stack([core, x, yl]).astype(jnp.int32)
    return pl.pallas_call(
        stripes_kernel,
        out_shape=jax.ShapeDtypeStruct((8 * WIDE, HALF), BF16),
        grid_spec=pltpu.PrefetchScalarGridSpec(
            num_scalar_prefetch=2,
            grid=(1,),
            in_specs=[pl.BlockSpec((HALF, 2 * HALF), lambda g, place, mask: (place[0], place[1]))],
            out_specs=pl.BlockSpec((8 * WIDE, HALF), lambda g, place, mask: (0, 0)),
        ),
        compiler_params=pltpu.CompilerParams(vmem_limit_bytes=MOST_VMEM),
        name="stripes",
    )(place, p_mask, p_tiles)


def mask_rows(mask, tiles, out, first):
    width = tiles.shape[1]
    lane = lax.broadcasted_iota(jnp.int32, (1, width), 1)
    for i in range(ROWS // TILE):
        present = jnp.zeros((1, width), F32)
        for k in range(width // TILE):
            inside = (lane >= k * TILE) & (lane < (k + 1) * TILE)
            present = jnp.where(inside, mask(i, first + k).astype(F32), present)
        rows = slice(i * TILE, (i + 1) * TILE)
        out[rows, :] = tiles[rows, :] * present.astype(BF16)


def operator_kernel(mask, tiles, out):
    mask_rows(lambda i, k: mask[k, i], tiles, out, 0)


def masked_operator(a_tiles, a_mask):
    return pl.pallas_call(
        operator_kernel,
        out_shape=jax.ShapeDtypeStruct(a_tiles.shape, BF16),
        in_specs=[pl.BlockSpec(memory_space=pltpu.SMEM), pl.BlockSpec(memory_space=pltpu.VMEM)],
        out_specs=pl.BlockSpec(memory_space=pltpu.VMEM),
        compiler_params=params(),
        name="masked_operator",
    )(a_mask.T, a_tiles)


def product_kernel(place, *refs):
    slabs, blocks, out, columns = refs[:4], refs[4:8], refs[8], refs[9]
    first, x, core = place[0], place[1], place[2]
    for n, slab in enumerate(slabs):
        for y in range(4):
            rows = pl.ds(pl.multiple_of((2 * y + core) * WIDE, WIDE), WIDE)
            columns[(first + n) % 4, y * WIDE : (y + 1) * WIDE] = slab[rows, :]
    total = dot_last(columns[x], blocks[0][...])
    for n in range(1, 4):
        total = total + dot_last(columns[(x + n) % 4], blocks[n][...])
    out[...] = total.reshape(4, WIDE, ROWS)


def product(slabs, blocks, first, x, core):
    place = jnp.stack([first, x, core]).astype(jnp.int32)
    return pl.pallas_call(
        product_kernel,
        out_shape=jax.ShapeDtypeStruct((4, WIDE, ROWS), F32),
        in_specs=[pl.BlockSpec(memory_space=pltpu.SMEM)] + [pl.BlockSpec(memory_space=pltpu.VMEM)] * 8,
        out_specs=pl.BlockSpec(memory_space=pltpu.VMEM),
        scratch_shapes=[pltpu.VMEM((4, 4 * WIDE, HALF), BF16)],
        compiler_params=params(),
        name="product",
    )(place, *slabs, *blocks)


def scale_code(most):
    return jnp.ceil(jnp.log2(jnp.maximum(most, LEAST)) * STEPS) + 1.0


def encode_kernel(mine, theirs, out):
    lane = lax.broadcasted_iota(jnp.int32, (WIDE, 128), 1)
    for n in range(4):
        codes = jnp.zeros((WIDE, 128), F32)
        for g in range(ROWS // 128):
            lanes = slice(g * 128, (g + 1) * 128)
            values = mine[n, :, lanes] + theirs[n, :, lanes]
            code = scale_code(jnp.max(jnp.abs(values), axis=1, keepdims=True))
            values = jnp.round(values * (LIMIT * jnp.exp2(code * (-1.0 / STEPS))))
            out[n, :, lanes] = values.astype(jnp.int32).astype(jnp.int16)
            codes = jnp.where(lane == g, code, codes)
        out[n, :, ROWS:] = codes.astype(jnp.int32).astype(jnp.int16)


def encode(mine, theirs):
    return pl.pallas_call(
        encode_kernel,
        out_shape=jax.ShapeDtypeStruct((4, WIDE, ROWS + 128), jnp.int16),
        in_specs=[pl.BlockSpec(memory_space=pltpu.VMEM)] * 2,
        out_specs=pl.BlockSpec(memory_space=pltpu.VMEM),
        compiler_params=params(),
        name="encode",
    )(mine, theirs)


def decoded_sum(coded):
    groups = []
    scales = [
        jnp.exp2(coded[n, :, ROWS:].astype(jnp.int32).astype(F32) * (1.0 / STEPS)) * (1.0 / LIMIT)
        for n in range(4)
    ]
    for g in range(ROWS // 128):
        lanes = slice(g * 128, (g + 1) * 128)
        terms = [
            coded[n, :, lanes].astype(jnp.int32).astype(F32) * scales[n][:, g : g + 1]
            for n in range(4)
        ]
        groups.append((terms[0] + terms[1]) + (terms[2] + terms[3]))
    return jnp.concatenate(groups, axis=1)


def pack(values):
    tail = values[:, 128:]
    return jnp.concatenate(
        [values[:, :128], jnp.concatenate([tail[:24], tail[24:]], axis=1)], axis=0
    )


def coarse_kernel(mask, parts, tiles, out, terms, present):
    @pl.when(pl.program_id(0) == 0)
    def _():
        whole = decoded_sum(parts)
        high = whole.astype(BF16)
        rest = whole - high.astype(F32)
        middle = rest.astype(BF16)
        low = (rest - middle.astype(F32)).astype(BF16)
        terms[...] = jnp.concatenate([high, middle, low], axis=0)

    first = pl.program_id(0) * (tiles.shape[1] // TILE)
    mask_rows(lambda i, k: mask[i, k], tiles, present, first)
    full = jnp.dot(terms[...], present[...], preferred_element_type=F32)
    full = (full[2 * WIDE :] + full[WIDE : 2 * WIDE]) + full[:WIDE]
    for k in range(out.shape[0]):
        chunk = full[:, k * TILE : (k + 1) * TILE]
        code = scale_code(jnp.max(jnp.abs(chunk), axis=0, keepdims=True))
        factor = LIMIT * jnp.exp2(code * (-1.0 / STEPS))
        values = pack(jnp.round(chunk * factor))
        scales = pack(jnp.broadcast_to(code, (WIDE, TILE)))
        coded = jnp.concatenate([values, scales[:1], scales[48:49], jnp.zeros((6, 128), F32)], axis=0)
        out[k] = coded.astype(jnp.int32).astype(jnp.int16)


def coarse_parts(parts, p_tiles, p_mask):
    width = COARSE // 4
    return pl.pallas_call(
        coarse_kernel,
        out_shape=jax.ShapeDtypeStruct((PLANES, CODED, 128), jnp.int16),
        grid_spec=pltpu.PrefetchScalarGridSpec(
            num_scalar_prefetch=1,
            grid=(4,),
            in_specs=[
                pl.BlockSpec((4, WIDE, ROWS + 128), lambda g, mask: (0, 0, 0)),
                pl.BlockSpec((ROWS, width), lambda g, mask: (0, g)),
            ],
            out_specs=pl.BlockSpec((width // TILE, CODED, 128), lambda g, mask: (g, 0, 0)),
            scratch_shapes=[pltpu.VMEM((3 * WIDE, ROWS), BF16), pltpu.VMEM((ROWS, width), BF16)],
        ),
        compiler_params=params(),
        name="coarse_parts",
    )(p_mask, parts, p_tiles)


def sum_kernel(coded, out):
    total = jnp.zeros((72, 128), F32)
    for z in range(PLANES):
        block = coded[z].astype(jnp.int32).astype(F32)
        scale = jnp.exp2(block[72:80] * (1.0 / STEPS)) * (1.0 / LIMIT)
        factor = jnp.concatenate(
            [jnp.broadcast_to(scale[:1], (48, 128)), jnp.broadcast_to(scale[1:2], (24, 128))], axis=0
        )
        total = total + block[:72] * factor
    out[:, :128] = total[:48]
    out[:24, 128:] = total[48:, :64]
    out[24:, 128:] = total[48:, 64:]


def summed(coded):
    return pl.pallas_call(
        sum_kernel,
        out_shape=jax.ShapeDtypeStruct((WIDE, TILE), F32),
        in_specs=[pl.BlockSpec(memory_space=pltpu.VMEM)],
        out_specs=pl.BlockSpec(memory_space=pltpu.VMEM),
        compiler_params=params(),
        name="summed",
    )(coded)


def shift(yh):
    return yh // 2 * 2


def spread():
    pairs = []
    for source in range(4**3 * 4):
        zh, zl, yh, core, yl = source // 64, source // 16 % 4, source // 4 % 4, source // 2 % 2, source % 2
        target = ((yh + core + 2 * yl) % 4 * 4 + (zh + shift(zl)) % 4) * 4 + zl
        pairs.append((source, (target * 2 + core) * 2 + yl))
    return pairs


def around(size, near):
    return [((i + near) % size, i) for i in range(size)]


def local(a_tiles, p_tiles, a_mask, p_mask):
    zh, zl, x = lax.axis_index("zh"), lax.axis_index("zl"), lax.axis_index("x")
    yh, core, yl = lax.axis_index("yh"), lax.axis_index("core"), lax.axis_index("yl")
    z = ("zh", "zl")

    mine = stripes(p_tiles, p_mask, core, x, yl)
    slab = lax.ppermute(mine, z + ("yh", "core", "yl"), spread())
    first = (zl - shift(yh)) % 4
    a_tiles, mine = lax.optimization_barrier((a_tiles, mine))
    own = masked_operator(a_tiles, a_mask)
    after, before = [lax.ppermute(own, "x", around(4, turn)) for turn in (1, -1)]

    slab, own, after, before = lax.optimization_barrier((slab, own, after, before))
    slabs = [slab] + [lax.ppermute(slab, z, around(PLANES, turn)) for turn in (1, 2, -1)]
    blocks = [own, after, lax.ppermute(after, "x", around(4, 1)), before]

    theirs = lax.ppermute(product(slabs, blocks, first, x, 1 - core), "core", [(0, 1), (1, 0)])
    coded = encode(product(slabs, blocks, first, x, core), theirs)
    coded = lax.all_to_all(coded, "yh", 0, 0, tiled=True)
    coded = lax.all_to_all(coarse_parts(coded, p_tiles, p_mask), z, 0, 0, tiled=True)
    return summed(coded).T


def solution(mesh):
    fine = Mesh(mesh.devices.reshape(4, 4, 4, 4, 2, 2), ("zh", "zl", "x", "yh", "core", "yl"))
    z, col = ("zh", "zl"), ("x", "yh", "core")
    return jax.shard_map(
        local,
        mesh=fine,
        in_specs=(P(z, col), P(z, None), P(z, col), P(z, None)),
        out_specs=P(z, col + ("yl",)),
        check_vma=False,
    )
```

```python
import functools

import jax
import jax.numpy as jnp
from jax import lax
from jax.experimental import pallas as pl
from jax.experimental.pallas import tpu as pltpu
from jax.sharding import Mesh
from jax.sharding import PartitionSpec as P

TILE = 192
WIDE = 48
ROWS = 768
HALF = 384
COARSE = 3072
PLANES = 16
LIMIT = 32766.0
STEPS = 128.0
EMPTY = 16
LEAST = 1e-33
CODED = 80
VMEM = 16 * 1024 * 1024
MOST_VMEM = 62 * 1024 * 1024
F32 = jnp.float32
BF16 = jnp.bfloat16


def params():
    return pltpu.CompilerParams(vmem_limit_bytes=VMEM)


def dot_last(left, right):
    return lax.dot_general(left, right, (((1,), (1,)), ((), ())), preferred_element_type=F32)


def stripes_kernel(mask, tiles, out, window, arrived):
    core, x, yl = lax.axis_index("core"), lax.axis_index("x"), lax.axis_index("yl")
    copies = []
    for n in range(2):
        rows = pl.ds(pl.multiple_of(core * HALF, HALF), HALF)
        columns = pl.ds(pl.multiple_of((2 * x + n) * HALF, HALF), HALF)
        copies.append(pltpu.make_async_copy(tiles.at[rows, columns], window.at[n], arrived.at[n]))
        copies[n].start()
    row = lax.broadcasted_iota(jnp.int32, (WIDE, HALF), 0)
    lane = lax.broadcasted_iota(jnp.int32, (WIDE, HALF), 1)
    picks = [(lane == row + (2 * s + yl) * WIDE).astype(F32).astype(BF16) for s in range(4)]
    pick = jnp.concatenate(picks, axis=0)
    fine = lax.broadcasted_iota(jnp.int32, (1, HALF), 1)
    out[8 * WIDE :, :] = jnp.zeros((EMPTY, HALF), BF16)
    for n in range(2):
        copies[n].wait()
        picked = dot_last(pick, window[n])
        for m in range(2):
            tile = 4 * x + 2 * n + m
            upper, lower = mask[2 * core, tile], mask[2 * core + 1, tile]
            present = jnp.where(fine < TILE, upper.astype(F32), lower.astype(F32))
            part = picked[2 * WIDE * m : 2 * WIDE * (m + 1)]
            first = 2 * WIDE * (2 * n + m)
            out[first : first + 2 * WIDE, :] = (part * present).astype(BF16)


def stripes(p_tiles, p_mask):
    return pl.pallas_call(
        stripes_kernel,
        out_shape=jax.ShapeDtypeStruct((8 * WIDE + EMPTY, HALF), BF16),
        in_specs=[pl.BlockSpec(memory_space=pltpu.SMEM), pl.BlockSpec(memory_space=pltpu.HBM)],
        out_specs=pl.BlockSpec(memory_space=pltpu.VMEM),
        scratch_shapes=[pltpu.VMEM((2, HALF, HALF), BF16), pltpu.SemaphoreType.DMA((2,))],
        compiler_params=pltpu.CompilerParams(vmem_limit_bytes=MOST_VMEM),
        name="stripes",
    )(p_mask, p_tiles)


def mask_rows(mask, tiles, out, first):
    height, width = tiles.shape
    lane = lax.broadcasted_iota(jnp.int32, (1, width), 1)
    for i in range(height // TILE):
        present = jnp.zeros((1, width), F32)
        for k in range(width // TILE):
            inside = (lane >= k * TILE) & (lane < (k + 1) * TILE)
            present = jnp.where(inside, mask(i, first + k).astype(F32), present)
        rows = slice(i * TILE, (i + 1) * TILE)
        out[rows, :] = tiles[rows, :] * present.astype(BF16)


def operator_kernel(mask, tiles, upper, lower):
    for half, out in enumerate((upper, lower)):
        rows = tiles[half * HALF : (half + 1) * HALF, :]
        mask_rows(lambda i, k: mask[k, 2 * half + i], rows, out, 0)


def masked_operator(a_tiles, a_mask):
    return pl.pallas_call(
        operator_kernel,
        out_shape=[jax.ShapeDtypeStruct((HALF, HALF), BF16)] * 2,
        in_specs=[pl.BlockSpec(memory_space=pltpu.SMEM), pl.BlockSpec(memory_space=pltpu.VMEM)],
        out_specs=[pl.BlockSpec(memory_space=pltpu.VMEM)] * 2,
        compiler_params=params(),
        name="masked_operator",
    )(a_mask.T, a_tiles)


def product_kernel(other, *refs):
    slabs, blocks, out, columns = refs[:4], refs[4:12], refs[12], refs[13]
    x, zl, yh = lax.axis_index("x"), lax.axis_index("zl"), lax.axis_index("yh")
    first = zl + 4 - shift(yh)
    core = (lax.axis_index("core") + other) % 2
    for n, slab in enumerate(slabs):
        for y in range(4):
            rows = pl.ds(pl.multiple_of((2 * y + core) * WIDE, WIDE), WIDE)
            columns[(first + n) % 4, y * WIDE : (y + 1) * WIDE] = slab[rows, :]
    for half in range(2):
        total = dot_last(columns[x], blocks[half][...])
        for n in range(1, 4):
            total = total + dot_last(columns[(x + n) % 4], blocks[2 * n + half][...])
        out[:, :, half * HALF : (half + 1) * HALF] = total.reshape(4, WIDE, HALF)


def product(slabs, blocks, other):
    return pl.pallas_call(
        functools.partial(product_kernel, other),
        out_shape=jax.ShapeDtypeStruct((4, WIDE, ROWS), F32),
        in_specs=[pl.BlockSpec(memory_space=pltpu.VMEM)] * 12,
        out_specs=pl.BlockSpec(memory_space=pltpu.VMEM),
        scratch_shapes=[pltpu.VMEM((4, 4 * WIDE, HALF), BF16)],
        compiler_params=params(),
        name="product_for_other" if other else "product",
    )(*slabs, *blocks)


def scale_code(most):
    return jnp.ceil(jnp.log2(jnp.maximum(most, LEAST)) * STEPS) + 1.0


def encode_kernel(mine, theirs, out):
    lane = lax.broadcasted_iota(jnp.int32, (WIDE, 128), 1)
    for n in range(4):
        codes = jnp.zeros((WIDE, 128), F32)
        for g in range(ROWS // 128):
            lanes = slice(g * 128, (g + 1) * 128)
            values = mine[n, :, lanes] + theirs[n, :, lanes]
            code = scale_code(jnp.max(jnp.abs(values), axis=1, keepdims=True))
            values = jnp.round(values * (LIMIT * jnp.exp2(code * (-1.0 / STEPS))))
            out[n, :, lanes] = values.astype(jnp.int32).astype(jnp.int16)
            codes = jnp.where(lane == g, code, codes)
        out[n, :, ROWS:] = codes.astype(jnp.int32).astype(jnp.int16)


def encode(mine, theirs):
    return pl.pallas_call(
        encode_kernel,
        out_shape=jax.ShapeDtypeStruct((4, WIDE, ROWS + 128), jnp.int16),
        in_specs=[pl.BlockSpec(memory_space=pltpu.VMEM)] * 2,
        out_specs=pl.BlockSpec(memory_space=pltpu.VMEM),
        compiler_params=params(),
        name="encode",
    )(mine, theirs)


def decoded_sum(coded):
    groups = []
    scales = [
        jnp.exp2(coded[n, :, ROWS:].astype(jnp.int32).astype(F32) * (1.0 / STEPS)) * (1.0 / LIMIT)
        for n in range(4)
    ]
    for g in range(ROWS // 128):
        lanes = slice(g * 128, (g + 1) * 128)
        terms = [
            coded[n, :, lanes].astype(jnp.int32).astype(F32) * scales[n][:, g : g + 1]
            for n in range(4)
        ]
        groups.append((terms[0] + terms[1]) + (terms[2] + terms[3]))
    return jnp.concatenate(groups, axis=1)


def pack(values):
    tail = values[:, 128:]
    return jnp.concatenate(
        [values[:, :128], jnp.concatenate([tail[:24], tail[24:]], axis=1)], axis=0
    )


def coarse_kernel(mask, parts, tiles, out, terms, present):
    @pl.when(pl.program_id(0) == 0)
    def _():
        whole = decoded_sum(parts)
        high = whole.astype(BF16)
        rest = whole - high.astype(F32)
        middle = rest.astype(BF16)
        low = (rest - middle.astype(F32)).astype(BF16)
        terms[...] = jnp.concatenate([high, middle, low], axis=0)

    first = pl.program_id(0) * (tiles.shape[1] // TILE)
    mask_rows(lambda i, k: mask[i, k], tiles, present, first)
    full = jnp.dot(terms[...], present[...], preferred_element_type=F32)
    full = (full[2 * WIDE :] + full[WIDE : 2 * WIDE]) + full[:WIDE]
    for k in range(out.shape[0]):
        chunk = full[:, k * TILE : (k + 1) * TILE]
        code = scale_code(jnp.max(jnp.abs(chunk), axis=0, keepdims=True))
        factor = LIMIT * jnp.exp2(code * (-1.0 / STEPS))
        values = pack(jnp.round(chunk * factor))
        scales = pack(jnp.broadcast_to(code, (WIDE, TILE)))
        coded = jnp.concatenate([values, scales[:1], scales[48:49], jnp.zeros((6, 128), F32)], axis=0)
        out[k] = coded.astype(jnp.int32).astype(jnp.int16)


def coarse_parts(parts, p_tiles, p_mask):
    width = COARSE // 4
    return pl.pallas_call(
        coarse_kernel,
        out_shape=jax.ShapeDtypeStruct((PLANES, CODED, 128), jnp.int16),
        grid_spec=pltpu.PrefetchScalarGridSpec(
            num_scalar_prefetch=1,
            grid=(4,),
            in_specs=[
                pl.BlockSpec((4, WIDE, ROWS + 128), lambda g, mask: (0, 0, 0)),
                pl.BlockSpec((ROWS, width), lambda g, mask: (0, g)),
            ],
            out_specs=pl.BlockSpec((width // TILE, CODED, 128), lambda g, mask: (g, 0, 0)),
            scratch_shapes=[pltpu.VMEM((3 * WIDE, ROWS), BF16), pltpu.VMEM((ROWS, width), BF16)],
        ),
        compiler_params=params(),
        name="coarse_parts",
    )(p_mask, parts, p_tiles)


def sum_kernel(coded, out):
    total = jnp.zeros((72, 128), F32)
    for z in range(PLANES):
        block = coded[z].astype(jnp.int32).astype(F32)
        scale = jnp.exp2(block[72:80] * (1.0 / STEPS)) * (1.0 / LIMIT)
        factor = jnp.concatenate(
            [jnp.broadcast_to(scale[:1], (48, 128)), jnp.broadcast_to(scale[1:2], (24, 128))], axis=0
        )
        total = total + block[:72] * factor
    out[:, :128] = total[:48]
    out[:24, 128:] = total[48:, :64]
    out[24:, 128:] = total[48:, 64:]


def summed(coded):
    return pl.pallas_call(
        sum_kernel,
        out_shape=jax.ShapeDtypeStruct((WIDE, TILE), F32),
        in_specs=[pl.BlockSpec(memory_space=pltpu.VMEM)],
        out_specs=pl.BlockSpec(memory_space=pltpu.VMEM),
        compiler_params=params(),
        name="summed",
    )(coded)


def shift(yh):
    return yh // 2 * 2


def spread():
    pairs = []
    for source in range(4**3 * 4):
        zh, zl, yh, core, yl = source // 64, source // 16 % 4, source // 4 % 4, source // 2 % 2, source % 2
        target = ((yh + core + 2 * yl) % 4 * 4 + (zh + shift(zl)) % 4) * 4 + zl
        pairs.append((source, (target * 2 + core) * 2 + yl))
    return pairs


def around(size, near):
    return [((i + near) % size, i) for i in range(size)]


def local(a_tiles, p_tiles, a_mask, p_mask):
    z = ("zh", "zl")
    mine = stripes(p_tiles, p_mask)
    slab = lax.ppermute(mine, z + ("yh", "core", "yl"), spread())
    a_tiles, mine = lax.optimization_barrier((a_tiles, mine))
    own = masked_operator(a_tiles, a_mask)
    after = [lax.ppermute(half, "x", around(4, 1)) for half in own]
    before = [lax.ppermute(half, "x", around(4, -1)) for half in own]

    slab, own, after, before = lax.optimization_barrier((slab, own, after, before))
    slabs = [slab] + [lax.ppermute(slab, z, around(PLANES, turn)) for turn in (1, 2, -1)]
    across = [
        lax.ppermute(after[0], "x", around(4, 1)),
        lax.ppermute(before[1], "x", around(4, -1)),
    ]
    blocks = [*own, *after, *across, *before]

    theirs = lax.ppermute(product(slabs, blocks, 1), "core", [(0, 1), (1, 0)])
    coded = encode(product(slabs, blocks, 0), theirs)
    coded = lax.all_to_all(coded, "yh", 0, 0, tiled=True)
    coded = lax.all_to_all(coarse_parts(coded, p_tiles, p_mask), z, 0, 0, tiled=True)
    return summed(coded).T


def solution(mesh):
    fine = Mesh(mesh.devices.reshape(4, 4, 4, 4, 2, 2), ("zh", "zl", "x", "yh", "core", "yl"))
    z, col = ("zh", "zl"), ("x", "yh", "core")
    return jax.shard_map(
        local,
        mesh=fine,
        in_specs=(P(z, col), P(z, None), P(z, col), P(z, None)),
        out_specs=P(z, col + ("yl",)),
        check_vma=False,
    )
```

```python
import functools

import jax
import jax.numpy as jnp
from jax import lax
from jax.experimental import pallas as pl
from jax.experimental.pallas import tpu as pltpu
from jax.sharding import Mesh
from jax.sharding import PartitionSpec as P

TILE = 192
WIDE = 48
ROWS = 768
HALF = 384
COARSE = 3072
PLANES = 16
LIMIT = 32766.0
STEPS = 128.0
EMPTY = 16
LEAST = 1e-33
CODED = 80
VMEM = 16 * 1024 * 1024
MOST_VMEM = 62 * 1024 * 1024
F32 = jnp.float32
BF16 = jnp.bfloat16


def params():
    return pltpu.CompilerParams(vmem_limit_bytes=VMEM)


def dot_last(left, right):
    return lax.dot_general(left, right, (((1,), (1,)), ((), ())), preferred_element_type=F32)


def stripes_kernel(mask, tiles, out, window, arrived):
    core, x = lax.axis_index("core"), lax.axis_index("x")
    yl, _ = y_target(lax.axis_index("zl"), lax.axis_index("yh"), lax.axis_index("yl"))
    copies = []
    for n in range(2):
        rows = pl.ds(pl.multiple_of(core * HALF, HALF), HALF)
        columns = pl.ds(pl.multiple_of((2 * x + n) * HALF, HALF), HALF)
        copies.append(pltpu.make_async_copy(tiles.at[rows, columns], window.at[n], arrived.at[n]))
        copies[n].start()
    row = lax.broadcasted_iota(jnp.int32, (WIDE, HALF), 0)
    lane = lax.broadcasted_iota(jnp.int32, (WIDE, HALF), 1)
    picks = [(lane == row + (2 * s + yl) * WIDE).astype(F32).astype(BF16) for s in range(4)]
    pick = jnp.concatenate(picks, axis=0)
    fine = lax.broadcasted_iota(jnp.int32, (1, HALF), 1)
    out[8 * WIDE :, :] = jnp.zeros((EMPTY, HALF), BF16)
    for n in range(2):
        copies[n].wait()
        picked = dot_last(pick, window[n])
        for m in range(2):
            tile = 4 * x + 2 * n + m
            upper, lower = mask[2 * core, tile], mask[2 * core + 1, tile]
            present = jnp.where(fine < TILE, upper.astype(F32), lower.astype(F32))
            part = picked[2 * WIDE * m : 2 * WIDE * (m + 1)]
            first = 2 * WIDE * (2 * n + m)
            out[first : first + 2 * WIDE, :] = (part * present).astype(BF16)


def stripes(p_tiles, p_mask):
    return pl.pallas_call(
        stripes_kernel,
        out_shape=jax.ShapeDtypeStruct((8 * WIDE + EMPTY, HALF), BF16),
        in_specs=[pl.BlockSpec(memory_space=pltpu.SMEM), pl.BlockSpec(memory_space=pltpu.HBM)],
        out_specs=pl.BlockSpec(memory_space=pltpu.VMEM),
        scratch_shapes=[pltpu.VMEM((2, HALF, HALF), BF16), pltpu.SemaphoreType.DMA((2,))],
        compiler_params=pltpu.CompilerParams(vmem_limit_bytes=MOST_VMEM),
        name="stripes",
    )(p_mask, p_tiles)


def mask_rows(mask, tiles, out, first):
    height, width = tiles.shape
    lane = lax.broadcasted_iota(jnp.int32, (1, width), 1)
    for i in range(height // TILE):
        present = jnp.zeros((1, width), F32)
        for k in range(width // TILE):
            inside = (lane >= k * TILE) & (lane < (k + 1) * TILE)
            present = jnp.where(inside, mask(i, first + k).astype(F32), present)
        rows = slice(i * TILE, (i + 1) * TILE)
        out[rows, :] = tiles[rows, :] * present.astype(BF16)


def operator_kernel(mask, tiles, upper, lower):
    for half, out in enumerate((upper, lower)):
        rows = tiles[half * HALF : (half + 1) * HALF, :]
        mask_rows(lambda i, k: mask[k, 2 * half + i], rows, out, 0)


def masked_operator(a_tiles, a_mask):
    return pl.pallas_call(
        operator_kernel,
        out_shape=[jax.ShapeDtypeStruct((HALF, HALF), BF16)] * 2,
        in_specs=[pl.BlockSpec(memory_space=pltpu.SMEM), pl.BlockSpec(memory_space=pltpu.VMEM)],
        out_specs=[pl.BlockSpec(memory_space=pltpu.VMEM)] * 2,
        compiler_params=params(),
        name="masked_operator",
    )(a_mask.T, a_tiles)


def product_kernel(other, *refs):
    slabs, blocks, out, columns = refs[:4], refs[4:12], refs[12], refs[13]
    x, zl = lax.axis_index("x"), lax.axis_index("zl")
    core = (lax.axis_index("core") + other) % 2
    for n, slab in enumerate(slabs):
        for y in range(4):
            rows = pl.ds(pl.multiple_of((2 * y + core) * WIDE, WIDE), WIDE)
            columns[(zl + n) % 4, y * WIDE : (y + 1) * WIDE] = slab[rows, :]
    for half in range(2):
        total = dot_last(columns[x], blocks[half][...])
        for n in range(1, 4):
            total = total + dot_last(columns[(x + n) % 4], blocks[2 * n + half][...])
        out[:, :, half * HALF : (half + 1) * HALF] = total.reshape(4, WIDE, HALF)


def product(slabs, blocks, other):
    return pl.pallas_call(
        functools.partial(product_kernel, other),
        out_shape=jax.ShapeDtypeStruct((4, WIDE, ROWS), F32),
        in_specs=[pl.BlockSpec(memory_space=pltpu.VMEM)] * 12,
        out_specs=pl.BlockSpec(memory_space=pltpu.VMEM),
        scratch_shapes=[pltpu.VMEM((4, 4 * WIDE, HALF), BF16)],
        compiler_params=params(),
        name="product_for_other" if other else "product",
    )(*slabs, *blocks)


def scale_code(most):
    return jnp.ceil(jnp.log2(jnp.maximum(most, LEAST)) * STEPS) + 1.0


def encode_kernel(mine, theirs, out):
    lane = lax.broadcasted_iota(jnp.int32, (WIDE, 128), 1)
    for n in range(4):
        codes = jnp.zeros((WIDE, 128), F32)
        for g in range(ROWS // 128):
            lanes = slice(g * 128, (g + 1) * 128)
            values = mine[n, :, lanes] + theirs[n, :, lanes]
            code = scale_code(jnp.max(jnp.abs(values), axis=1, keepdims=True))
            values = jnp.round(values * (LIMIT * jnp.exp2(code * (-1.0 / STEPS))))
            out[n, :, lanes] = values.astype(jnp.int32).astype(jnp.int16)
            codes = jnp.where(lane == g, code, codes)
        out[n, :, ROWS:] = codes.astype(jnp.int32).astype(jnp.int16)


def encode(mine, theirs):
    return pl.pallas_call(
        encode_kernel,
        out_shape=jax.ShapeDtypeStruct((4, WIDE, ROWS + 128), jnp.int16),
        in_specs=[pl.BlockSpec(memory_space=pltpu.VMEM)] * 2,
        out_specs=pl.BlockSpec(memory_space=pltpu.VMEM),
        compiler_params=params(),
        name="encode",
    )(mine, theirs)


def decoded_sum(coded):
    groups = []
    scales = [
        jnp.exp2(coded[n, :, ROWS:].astype(jnp.int32).astype(F32) * (1.0 / STEPS)) * (1.0 / LIMIT)
        for n in range(4)
    ]
    for g in range(ROWS // 128):
        lanes = slice(g * 128, (g + 1) * 128)
        terms = [
            coded[n, :, lanes].astype(jnp.int32).astype(F32) * scales[n][:, g : g + 1]
            for n in range(4)
        ]
        groups.append((terms[0] + terms[1]) + (terms[2] + terms[3]))
    return jnp.concatenate(groups, axis=1)


def pack(values):
    tail = values[:, 128:]
    return jnp.concatenate(
        [values[:, :128], jnp.concatenate([tail[:24], tail[24:]], axis=1)], axis=0
    )


def coarse_kernel(mask, parts, tiles, out, terms, present):
    @pl.when(pl.program_id(0) == 0)
    def _():
        whole = decoded_sum(parts)
        high = whole.astype(BF16)
        rest = whole - high.astype(F32)
        middle = rest.astype(BF16)
        low = (rest - middle.astype(F32)).astype(BF16)
        terms[...] = jnp.concatenate([high, middle, low], axis=0)

    first = pl.program_id(0) * (tiles.shape[1] // TILE)
    mask_rows(lambda i, k: mask[i, k], tiles, present, first)
    full = jnp.dot(terms[...], present[...], preferred_element_type=F32)
    full = (full[2 * WIDE :] + full[WIDE : 2 * WIDE]) + full[:WIDE]
    for k in range(out.shape[0]):
        chunk = full[:, k * TILE : (k + 1) * TILE]
        code = scale_code(jnp.max(jnp.abs(chunk), axis=0, keepdims=True))
        factor = LIMIT * jnp.exp2(code * (-1.0 / STEPS))
        values = pack(jnp.round(chunk * factor))
        scales = pack(jnp.broadcast_to(code, (WIDE, TILE)))
        coded = jnp.concatenate([values, scales[:1], scales[48:49], jnp.zeros((6, 128), F32)], axis=0)
        out[k] = coded.astype(jnp.int32).astype(jnp.int16)


def coarse_parts(parts, p_tiles, p_mask):
    width = COARSE // 4
    return pl.pallas_call(
        coarse_kernel,
        out_shape=jax.ShapeDtypeStruct((PLANES, CODED, 128), jnp.int16),
        grid_spec=pltpu.PrefetchScalarGridSpec(
            num_scalar_prefetch=1,
            grid=(4,),
            in_specs=[
                pl.BlockSpec((4, WIDE, ROWS + 128), lambda g, mask: (0, 0, 0)),
                pl.BlockSpec((ROWS, width), lambda g, mask: (0, g)),
            ],
            out_specs=pl.BlockSpec((width // TILE, CODED, 128), lambda g, mask: (g, 0, 0)),
            scratch_shapes=[pltpu.VMEM((3 * WIDE, ROWS), BF16), pltpu.VMEM((ROWS, width), BF16)],
        ),
        compiler_params=params(),
        name="coarse_parts",
    )(p_mask, parts, p_tiles)


def sum_kernel(coded, out):
    total = jnp.zeros((72, 128), F32)
    for z in range(PLANES):
        block = coded[z].astype(jnp.int32).astype(F32)
        scale = jnp.exp2(block[72:80] * (1.0 / STEPS)) * (1.0 / LIMIT)
        factor = jnp.concatenate(
            [jnp.broadcast_to(scale[:1], (48, 128)), jnp.broadcast_to(scale[1:2], (24, 128))], axis=0
        )
        total = total + block[:72] * factor
    out[:, :128] = total[:48]
    out[:24, 128:] = total[48:, :64]
    out[24:, 128:] = total[48:, 64:]


def summed(coded):
    return pl.pallas_call(
        sum_kernel,
        out_shape=jax.ShapeDtypeStruct((WIDE, TILE), F32),
        in_specs=[pl.BlockSpec(memory_space=pltpu.VMEM)],
        out_specs=pl.BlockSpec(memory_space=pltpu.VMEM),
        compiler_params=params(),
        name="summed",
    )(coded)


def y_target(zl, yh, yl):
    turn = (2 * yh + yl + 8 - 2 * zl) % 8
    far = (turn + 3) // 4 % 2
    return far, far * (turn - 1) + (1 - far) * ((8 - turn) % 8)


def spread():
    pairs = []
    for source in range(4**3 * 4):
        zh, zl, yh, core, yl = source // 64, source // 16 % 4, source // 4 % 4, source // 2 % 2, source % 2
        target_yl, rank = y_target(zl, yh, yl)
        target = ((rank + 2 * core + zl) % 4 * 4 + zh) * 4 + zl
        pairs.append((source, (target * 2 + core) * 2 + target_yl))
    return pairs


def around(size, near):
    return [((i + near) % size, i) for i in range(size)]


def local(a_tiles, p_tiles, a_mask, p_mask):
    z = ("zh", "zl")
    mine = stripes(p_tiles, p_mask)
    slab = lax.ppermute(mine, z + ("yh", "core", "yl"), spread())
    a_tiles, mine = lax.optimization_barrier((a_tiles, mine))
    own = masked_operator(a_tiles, a_mask)
    after = [lax.ppermute(half, "x", around(4, 1)) for half in own]
    before = [lax.ppermute(half, "x", around(4, -1)) for half in own]

    slab, own, after, before = lax.optimization_barrier((slab, own, after, before))
    slabs = [slab] + [lax.ppermute(slab, z, around(PLANES, turn)) for turn in (1, 2, -1)]
    across = [
        lax.ppermute(after[0], "x", around(4, 1)),
        lax.ppermute(before[1], "x", around(4, -1)),
    ]
    blocks = [*own, *after, *across, *before]

    theirs = lax.ppermute(product(slabs, blocks, 1), "core", [(0, 1), (1, 0)])
    coded = encode(product(slabs, blocks, 0), theirs)
    coded = lax.all_to_all(coded, "yh", 0, 0, tiled=True)
    coded = lax.all_to_all(coarse_parts(coded, p_tiles, p_mask), z, 0, 0, tiled=True)
    return summed(coded).T


def solution(mesh):
    fine = Mesh(mesh.devices.reshape(4, 4, 4, 4, 2, 2), ("zh", "zl", "x", "yh", "core", "yl"))
    z, col = ("zh", "zl"), ("x", "yh", "core")
    return jax.shard_map(
        local,
        mesh=fine,
        in_specs=(P(z, col), P(z, None), P(z, col), P(z, None)),
        out_specs=P(z, col + ("yl",)),
        check_vma=False,
    )
```

```python
import functools

import jax
import jax.numpy as jnp
from jax import lax
from jax.experimental import pallas as pl
from jax.experimental.pallas import tpu as pltpu
from jax.sharding import Mesh
from jax.sharding import PartitionSpec as P

TILE = 192
WIDE = 48
ROWS = 768
HALF = 384
COARSE = 3072
PLANES = 16
LIMIT = 32766.0
STEPS = 128.0
EMPTY = 16
LEAST = 1e-33
CODED = 80
VMEM = 16 * 1024 * 1024
MOST_VMEM = 57 * 1024 * 1024
F32 = jnp.float32
BF16 = jnp.bfloat16


def params():
    return pltpu.CompilerParams(vmem_limit_bytes=VMEM)


def dot_last(left, right):
    return lax.dot_general(left, right, (((1,), (1,)), ((), ())), preferred_element_type=F32)


def stripes_kernel(mask_in, tiles, out, window, mask, arrived, mask_arrived):
    core, x = lax.axis_index("core"), lax.axis_index("x")
    yl, _ = y_target(lax.axis_index("zl"), lax.axis_index("yh"), lax.axis_index("yl"))
    mask_copy = pltpu.make_async_copy(mask_in, mask, mask_arrived)
    mask_copy.start()
    copies = []
    for n in range(2):
        rows = pl.ds(pl.multiple_of(core * HALF, HALF), HALF)
        columns = pl.ds(pl.multiple_of((2 * x + n) * HALF, HALF), HALF)
        copies.append(pltpu.make_async_copy(tiles.at[rows, columns], window.at[n], arrived.at[n]))
        copies[n].start()
    row = lax.broadcasted_iota(jnp.int32, (WIDE, HALF), 0)
    lane = lax.broadcasted_iota(jnp.int32, (WIDE, HALF), 1)
    picks = [(lane == row + (2 * s + yl) * WIDE).astype(F32).astype(BF16) for s in range(4)]
    pick = jnp.concatenate(picks, axis=0)
    fine = lax.broadcasted_iota(jnp.int32, (1, HALF), 1)
    out[8 * WIDE :, :] = jnp.zeros((EMPTY, HALF), BF16)
    mask_copy.wait()
    for n in range(2):
        copies[n].wait()
        picked = dot_last(pick, window[n])
        for m in range(2):
            tile = 4 * x + 2 * n + m
            upper, lower = mask[2 * core, tile], mask[2 * core + 1, tile]
            present = jnp.where(fine < TILE, upper.astype(F32), lower.astype(F32))
            part = picked[2 * WIDE * m : 2 * WIDE * (m + 1)]
            first = 2 * WIDE * (2 * n + m)
            out[first : first + 2 * WIDE, :] = (part * present).astype(BF16)


def stripes(p_tiles, p_mask):
    return pl.pallas_call(
        stripes_kernel,
        out_shape=jax.ShapeDtypeStruct((8 * WIDE + EMPTY, HALF), BF16),
        in_specs=[pl.BlockSpec(memory_space=pl.ANY)] * 2,
        out_specs=pl.BlockSpec(memory_space=pltpu.VMEM),
        scratch_shapes=[
            pltpu.VMEM((2, HALF, HALF), BF16),
            pltpu.SMEM(p_mask.shape, jnp.int32),
            pltpu.SemaphoreType.DMA((2,)),
            pltpu.SemaphoreType.DMA,
        ],
        compiler_params=pltpu.CompilerParams(vmem_limit_bytes=MOST_VMEM),
        name="stripes",
    )(p_mask, p_tiles)


def mask_rows(mask, tiles, out, first):
    height, width = tiles.shape
    lane = lax.broadcasted_iota(jnp.int32, (1, width), 1)
    for i in range(height // TILE):
        present = jnp.zeros((1, width), F32)
        for k in range(width // TILE):
            inside = (lane >= k * TILE) & (lane < (k + 1) * TILE)
            present = jnp.where(inside, mask(i, first + k).astype(F32), present)
        rows = slice(i * TILE, (i + 1) * TILE)
        out[rows, :] = tiles[rows, :] * present.astype(BF16)


def operator_kernel(mask, tiles, upper, lower):
    for half, out in enumerate((upper, lower)):
        rows = tiles[half * HALF : (half + 1) * HALF, :]
        mask_rows(lambda i, k: mask[k, 2 * half + i], rows, out, 0)


def masked_operator(a_tiles, a_mask):
    return pl.pallas_call(
        operator_kernel,
        out_shape=[jax.ShapeDtypeStruct((HALF, HALF), BF16)] * 2,
        in_specs=[pl.BlockSpec(memory_space=pltpu.SMEM), pl.BlockSpec(memory_space=pltpu.VMEM)],
        out_specs=[pl.BlockSpec(memory_space=pltpu.VMEM)] * 2,
        compiler_params=params(),
        name="masked_operator",
    )(a_mask.T, a_tiles)


def product_kernel(other, *refs):
    slabs, blocks, out, columns = refs[:4], refs[4:12], refs[12], refs[13]
    x, zl = lax.axis_index("x"), lax.axis_index("zl")
    core = (lax.axis_index("core") + other) % 2
    for n, slab in enumerate(slabs):
        for y in range(4):
            rows = pl.ds(pl.multiple_of((2 * y + core) * WIDE, WIDE), WIDE)
            columns[(zl + n) % 4, y * WIDE : (y + 1) * WIDE] = slab[rows, :]
    for half in range(2):
        total = dot_last(columns[x], blocks[half][...])
        for n in range(1, 4):
            total = total + dot_last(columns[(x + n) % 4], blocks[2 * n + half][...])
        out[:, :, half * HALF : (half + 1) * HALF] = total.reshape(4, WIDE, HALF)


def product(slabs, blocks, other):
    return pl.pallas_call(
        functools.partial(product_kernel, other),
        out_shape=jax.ShapeDtypeStruct((4, WIDE, ROWS), F32),
        in_specs=[pl.BlockSpec(memory_space=pltpu.VMEM)] * 12,
        out_specs=pl.BlockSpec(memory_space=pltpu.VMEM),
        scratch_shapes=[pltpu.VMEM((4, 4 * WIDE, HALF), BF16)],
        compiler_params=params(),
        name="product_for_other" if other else "product",
    )(*slabs, *blocks)


def scale_code(most):
    return jnp.ceil(jnp.log2(jnp.maximum(most, LEAST)) * STEPS) + 1.0


def encode_kernel(mine, theirs, out):
    lane = lax.broadcasted_iota(jnp.int32, (WIDE, 128), 1)
    for n in range(4):
        codes = jnp.zeros((WIDE, 128), F32)
        for g in range(ROWS // 128):
            lanes = slice(g * 128, (g + 1) * 128)
            values = mine[n, :, lanes] + theirs[n, :, lanes]
            code = scale_code(jnp.max(jnp.abs(values), axis=1, keepdims=True))
            values = jnp.round(values * (LIMIT * jnp.exp2(code * (-1.0 / STEPS))))
            out[n, :, lanes] = values.astype(jnp.int32).astype(jnp.int16)
            codes = jnp.where(lane == g, code, codes)
        out[n, :, ROWS:] = codes.astype(jnp.int32).astype(jnp.int16)


def encode(mine, theirs):
    return pl.pallas_call(
        encode_kernel,
        out_shape=jax.ShapeDtypeStruct((4, WIDE, ROWS + 128), jnp.int16),
        in_specs=[pl.BlockSpec(memory_space=pltpu.VMEM)] * 2,
        out_specs=pl.BlockSpec(memory_space=pltpu.VMEM),
        compiler_params=params(),
        name="encode",
    )(mine, theirs)


def decoded_sum(coded):
    groups = []
    scales = [
        jnp.exp2(coded[n, :, ROWS:].astype(jnp.int32).astype(F32) * (1.0 / STEPS)) * (1.0 / LIMIT)
        for n in range(4)
    ]
    for g in range(ROWS // 128):
        lanes = slice(g * 128, (g + 1) * 128)
        terms = [
            coded[n, :, lanes].astype(jnp.int32).astype(F32) * scales[n][:, g : g + 1]
            for n in range(4)
        ]
        groups.append((terms[0] + terms[1]) + (terms[2] + terms[3]))
    return jnp.concatenate(groups, axis=1)


def pack(values):
    tail = values[:, 128:]
    return jnp.concatenate(
        [values[:, :128], jnp.concatenate([tail[:24], tail[24:]], axis=1)], axis=0
    )


def coarse_kernel(mask, parts, tiles, out, terms, present):
    @pl.when(pl.program_id(0) == 0)
    def _():
        whole = decoded_sum(parts)
        high = whole.astype(BF16)
        rest = whole - high.astype(F32)
        middle = rest.astype(BF16)
        low = (rest - middle.astype(F32)).astype(BF16)
        terms[...] = jnp.concatenate([high, middle, low], axis=0)

    first = pl.program_id(0) * (tiles.shape[1] // TILE)
    mask_rows(lambda i, k: mask[i, k], tiles, present, first)
    full = jnp.dot(terms[...], present[...], preferred_element_type=F32)
    full = (full[2 * WIDE :] + full[WIDE : 2 * WIDE]) + full[:WIDE]
    for k in range(out.shape[0]):
        chunk = full[:, k * TILE : (k + 1) * TILE]
        code = scale_code(jnp.max(jnp.abs(chunk), axis=0, keepdims=True))
        factor = LIMIT * jnp.exp2(code * (-1.0 / STEPS))
        values = pack(jnp.round(chunk * factor))
        scales = pack(jnp.broadcast_to(code, (WIDE, TILE)))
        coded = jnp.concatenate([values, scales[:1], scales[48:49], jnp.zeros((6, 128), F32)], axis=0)
        out[k] = coded.astype(jnp.int32).astype(jnp.int16)


def coarse_parts(parts, p_tiles, p_mask):
    width = COARSE // 4
    return pl.pallas_call(
        coarse_kernel,
        out_shape=jax.ShapeDtypeStruct((PLANES, CODED, 128), jnp.int16),
        grid_spec=pltpu.PrefetchScalarGridSpec(
            num_scalar_prefetch=1,
            grid=(4,),
            in_specs=[
                pl.BlockSpec((4, WIDE, ROWS + 128), lambda g, mask: (0, 0, 0)),
                pl.BlockSpec((ROWS, width), lambda g, mask: (0, g)),
            ],
            out_specs=pl.BlockSpec((width // TILE, CODED, 128), lambda g, mask: (g, 0, 0)),
            scratch_shapes=[pltpu.VMEM((3 * WIDE, ROWS), BF16), pltpu.VMEM((ROWS, width), BF16)],
        ),
        compiler_params=params(),
        name="coarse_parts",
    )(p_mask, parts, p_tiles)


def sum_kernel(coded, out):
    total = jnp.zeros((72, 128), F32)
    for z in range(PLANES):
        block = coded[z].astype(jnp.int32).astype(F32)
        scale = jnp.exp2(block[72:80] * (1.0 / STEPS)) * (1.0 / LIMIT)
        factor = jnp.concatenate(
            [jnp.broadcast_to(scale[:1], (48, 128)), jnp.broadcast_to(scale[1:2], (24, 128))], axis=0
        )
        total = total + block[:72] * factor
    out[:, :128] = total[:48]
    out[:24, 128:] = total[48:, :64]
    out[24:, 128:] = total[48:, 64:]


def summed(coded):
    return pl.pallas_call(
        sum_kernel,
        out_shape=jax.ShapeDtypeStruct((WIDE, TILE), F32),
        in_specs=[pl.BlockSpec(memory_space=pltpu.VMEM)],
        out_specs=pl.BlockSpec(memory_space=pltpu.VMEM),
        compiler_params=params(),
        name="summed",
    )(coded)


def y_target(zl, yh, yl):
    turn = (2 * yh + yl + 8 - 2 * zl) % 8
    far = (turn + 3) // 4 % 2
    return far, far * (turn - 1) + (1 - far) * ((8 - turn) % 8)


def spread():
    pairs = []
    for source in range(4**3 * 4):
        zh, zl, yh, core, yl = source // 64, source // 16 % 4, source // 4 % 4, source // 2 % 2, source % 2
        target_yl, rank = y_target(zl, yh, yl)
        target = ((rank + 2 * core + zl) % 4 * 4 + zh) * 4 + zl
        pairs.append((source, (target * 2 + core) * 2 + target_yl))
    return pairs


def around(size, near):
    return [((i + near) % size, i) for i in range(size)]


def two_away():
    near = [2, -2]
    return [
        ((i + near[core]) % PLANES * 2 + core, i * 2 + core) for i in range(PLANES) for core in range(2)
    ]


def local(a_tiles, p_tiles, a_mask, p_mask):
    z = ("zh", "zl")
    mine = stripes(p_tiles, p_mask)
    slab = lax.ppermute(mine, z + ("yh", "core", "yl"), spread())
    a_tiles, mine = lax.optimization_barrier((a_tiles, mine))
    own = masked_operator(a_tiles, a_mask)
    after = [lax.ppermute(half, "x", around(4, 1)) for half in own]
    before = [lax.ppermute(half, "x", around(4, -1)) for half in own]

    slab, own, after, before = lax.optimization_barrier((slab, own, after, before))
    above, below = [lax.ppermute(slab, z, around(PLANES, turn)) for turn in (1, -1)]
    slabs = [slab, above, lax.ppermute(slab, z + ("core",), two_away()), below]
    across = [
        lax.ppermute(after[0], "x", around(4, 1)),
        lax.ppermute(before[1], "x", around(4, -1)),
    ]
    blocks = [*own, *after, *across, *before]

    theirs = lax.ppermute(product(slabs, blocks, 1), "core", [(0, 1), (1, 0)])
    coded = encode(product(slabs, blocks, 0), theirs)
    coded = lax.all_to_all(coded, "yh", 0, 0, tiled=True)
    coded = lax.all_to_all(coarse_parts(coded, p_tiles, p_mask), z, 0, 0, tiled=True)
    return summed(coded).T


def solution(mesh):
    fine = Mesh(mesh.devices.reshape(4, 4, 4, 4, 2, 2), ("zh", "zl", "x", "yh", "core", "yl"))
    z, col = ("zh", "zl"), ("x", "yh", "core")
    return jax.shard_map(
        local,
        mesh=fine,
        in_specs=(P(z, col), P(z, None), P(z, col), P(z, None)),
        out_specs=P(z, col + ("yl",)),
        check_vma=False,
    )
```

```python
import functools

import jax
import jax.numpy as jnp
from jax import lax
from jax.experimental import pallas as pl
from jax.experimental.pallas import tpu as pltpu
from jax.sharding import Mesh
from jax.sharding import PartitionSpec as P

TILE = 192
WIDE = 48
ROWS = 768
HALF = 384
COARSE = 3072
PLANES = 16
LIMIT = 32766.0
STEPS = 128.0
EMPTY = 16
LEAST = 1e-33
CODED = 80
VMEM = 16 * 1024 * 1024
MOST_VMEM = 57 * 1024 * 1024
F32 = jnp.float32
BF16 = jnp.bfloat16


def params():
    return pltpu.CompilerParams(vmem_limit_bytes=VMEM)


def dot_last(left, right):
    return lax.dot_general(left, right, (((1,), (1,)), ((), ())), preferred_element_type=F32)


def stripes_kernel(mask_in, tiles, out, window, mask, arrived, mask_arrived):
    core, x = lax.axis_index("core"), lax.axis_index("x")
    yl, _ = y_target(lax.axis_index("zl"), lax.axis_index("yh"), lax.axis_index("yl"))
    mask_copy = pltpu.make_async_copy(mask_in, mask, mask_arrived)
    mask_copy.start()
    copies = []
    for n in range(2):
        rows = pl.ds(pl.multiple_of(core * HALF, HALF), HALF)
        columns = pl.ds(pl.multiple_of((2 * x + n) * HALF, HALF), HALF)
        copies.append(pltpu.make_async_copy(tiles.at[rows, columns], window.at[n], arrived.at[n]))
        copies[n].start()
    row = lax.broadcasted_iota(jnp.int32, (WIDE, HALF), 0)
    lane = lax.broadcasted_iota(jnp.int32, (WIDE, HALF), 1)
    picks = [(lane == row + (2 * s + yl) * WIDE).astype(F32).astype(BF16) for s in range(4)]
    pick = jnp.concatenate(picks, axis=0)
    fine = lax.broadcasted_iota(jnp.int32, (1, HALF), 1)
    out[8 * WIDE :, :] = jnp.zeros((EMPTY, HALF), BF16)
    mask_copy.wait()
    for n in range(2):
        copies[n].wait()
        picked = dot_last(pick, window[n])
        for m in range(2):
            tile = 4 * x + 2 * n + m
            upper, lower = mask[2 * core, tile], mask[2 * core + 1, tile]
            present = jnp.where(fine < TILE, upper.astype(F32), lower.astype(F32))
            part = picked[2 * WIDE * m : 2 * WIDE * (m + 1)]
            first = 2 * WIDE * (2 * n + m)
            out[first : first + 2 * WIDE, :] = (part * present).astype(BF16)


def stripes(p_tiles, p_mask):
    return pl.pallas_call(
        stripes_kernel,
        out_shape=jax.ShapeDtypeStruct((8 * WIDE + EMPTY, HALF), BF16),
        in_specs=[pl.BlockSpec(memory_space=pl.ANY)] * 2,
        out_specs=pl.BlockSpec(memory_space=pltpu.VMEM),
        scratch_shapes=[
            pltpu.VMEM((2, HALF, HALF), BF16),
            pltpu.SMEM(p_mask.shape, jnp.int32),
            pltpu.SemaphoreType.DMA((2,)),
            pltpu.SemaphoreType.DMA,
        ],
        compiler_params=pltpu.CompilerParams(vmem_limit_bytes=MOST_VMEM),
        name="stripes",
    )(p_mask, p_tiles)


def mask_rows(mask, tiles, out, first):
    height, width = tiles.shape
    lane = lax.broadcasted_iota(jnp.int32, (1, width), 1)
    for i in range(height // TILE):
        present = jnp.zeros((1, width), F32)
        for k in range(width // TILE):
            inside = (lane >= k * TILE) & (lane < (k + 1) * TILE)
            present = jnp.where(inside, mask(i, first + k).astype(F32), present)
        rows = slice(i * TILE, (i + 1) * TILE)
        out[rows, :] = tiles[rows, :] * present.astype(BF16)


def operator_kernel(mask, tiles, upper, lower):
    for half, out in enumerate((upper, lower)):
        rows = tiles[half * HALF : (half + 1) * HALF, :]
        mask_rows(lambda i, k: mask[k, 2 * half + i], rows, out, 0)


def masked_operator(a_tiles, a_mask):
    return pl.pallas_call(
        operator_kernel,
        out_shape=[jax.ShapeDtypeStruct((HALF, HALF), BF16)] * 2,
        in_specs=[pl.BlockSpec(memory_space=pltpu.SMEM), pl.BlockSpec(memory_space=pltpu.VMEM)],
        out_specs=[pl.BlockSpec(memory_space=pltpu.VMEM)] * 2,
        compiler_params=params(),
        name="masked_operator",
    )(a_mask.T, a_tiles)


def product_kernel(other, *refs):
    slabs, blocks, out, columns = refs[:4], refs[4:12], refs[12], refs[13]
    x, zl = lax.axis_index("x"), lax.axis_index("zl")
    core = (lax.axis_index("core") + other) % 2
    for n, slab in enumerate(slabs):
        for y in range(4):
            rows = pl.ds(pl.multiple_of((2 * y + core) * WIDE, WIDE), WIDE)
            columns[(zl + n) % 4, y * WIDE : (y + 1) * WIDE] = slab[rows, :]
    for half in range(2):
        total = dot_last(columns[x], blocks[half][...])
        for n in range(1, 4):
            total = total + dot_last(columns[(x + n) % 4], blocks[2 * n + half][...])
        out[:, :, half * HALF : (half + 1) * HALF] = total.reshape(4, WIDE, HALF)


def product(slabs, blocks, other):
    return pl.pallas_call(
        functools.partial(product_kernel, other),
        out_shape=jax.ShapeDtypeStruct((4, WIDE, ROWS), F32),
        in_specs=[pl.BlockSpec(memory_space=pltpu.VMEM)] * 12,
        out_specs=pl.BlockSpec(memory_space=pltpu.VMEM),
        scratch_shapes=[pltpu.VMEM((4, 4 * WIDE, HALF), BF16)],
        compiler_params=params(),
        name="product_for_other" if other else "product",
    )(*slabs, *blocks)


def scale_code(most):
    return jnp.ceil(jnp.log2(jnp.maximum(most, LEAST)) * STEPS) + 1.0


def encode_kernel(mine, theirs, out):
    lane = lax.broadcasted_iota(jnp.int32, (WIDE, 128), 1)
    for n in range(4):
        codes = jnp.zeros((WIDE, 128), F32)
        for g in range(ROWS // 128):
            lanes = slice(g * 128, (g + 1) * 128)
            values = mine[n, :, lanes] + theirs[n, :, lanes]
            code = scale_code(jnp.max(jnp.abs(values), axis=1, keepdims=True))
            values = jnp.round(values * (LIMIT * jnp.exp2(code * (-1.0 / STEPS))))
            out[n, :, lanes] = values.astype(jnp.int32).astype(jnp.int16)
            codes = jnp.where(lane == g, code, codes)
        out[n, :, ROWS:] = codes.astype(jnp.int32).astype(jnp.int16)


def encode(mine, theirs):
    return pl.pallas_call(
        encode_kernel,
        out_shape=jax.ShapeDtypeStruct((4, WIDE, ROWS + 128), jnp.int16),
        in_specs=[pl.BlockSpec(memory_space=pltpu.VMEM)] * 2,
        out_specs=pl.BlockSpec(memory_space=pltpu.VMEM),
        compiler_params=params(),
        name="encode",
    )(mine, theirs)


def decoded_sum(coded):
    groups = []
    scales = [
        jnp.exp2(coded[n, :, ROWS:].astype(jnp.int32).astype(F32) * (1.0 / STEPS)) * (1.0 / LIMIT)
        for n in range(4)
    ]
    for g in range(ROWS // 128):
        lanes = slice(g * 128, (g + 1) * 128)
        terms = [
            coded[n, :, lanes].astype(jnp.int32).astype(F32) * scales[n][:, g : g + 1]
            for n in range(4)
        ]
        groups.append((terms[0] + terms[1]) + (terms[2] + terms[3]))
    return jnp.concatenate(groups, axis=1)


def pack(values):
    tail = values[:, 128:]
    return jnp.concatenate(
        [values[:, :128], jnp.concatenate([tail[:24], tail[24:]], axis=1)], axis=0
    )


def coarse_kernel(mask, parts, tiles, out, terms, present):
    @pl.when(pl.program_id(0) == 0)
    def _():
        whole = decoded_sum(parts)
        high = whole.astype(BF16)
        rest = whole - high.astype(F32)
        middle = rest.astype(BF16)
        low = (rest - middle.astype(F32)).astype(BF16)
        terms[...] = jnp.concatenate([high, middle, low], axis=0)

    first = pl.program_id(0) * (tiles.shape[1] // TILE)
    mask_rows(lambda i, k: mask[i, k], tiles, present, first)
    full = jnp.dot(terms[...], present[...], preferred_element_type=F32)
    full = (full[2 * WIDE :] + full[WIDE : 2 * WIDE]) + full[:WIDE]
    for k in range(out.shape[0]):
        chunk = full[:, k * TILE : (k + 1) * TILE]
        code = scale_code(jnp.max(jnp.abs(chunk), axis=0, keepdims=True))
        factor = LIMIT * jnp.exp2(code * (-1.0 / STEPS))
        values = pack(jnp.round(chunk * factor))
        scales = pack(jnp.broadcast_to(code, (WIDE, TILE)))
        coded = jnp.concatenate([values, scales[:1], scales[48:49], jnp.zeros((6, 128), F32)], axis=0)
        out[k] = coded.astype(jnp.int32).astype(jnp.int16)


def coarse_parts(parts, p_tiles, p_mask):
    width = COARSE // 4
    return pl.pallas_call(
        coarse_kernel,
        out_shape=jax.ShapeDtypeStruct((PLANES, CODED, 128), jnp.int16),
        grid_spec=pltpu.PrefetchScalarGridSpec(
            num_scalar_prefetch=1,
            grid=(4,),
            in_specs=[
                pl.BlockSpec((4, WIDE, ROWS + 128), lambda g, mask: (0, 0, 0)),
                pl.BlockSpec((ROWS, width), lambda g, mask: (0, g)),
            ],
            out_specs=pl.BlockSpec((width // TILE, CODED, 128), lambda g, mask: (g, 0, 0)),
            scratch_shapes=[pltpu.VMEM((3 * WIDE, ROWS), BF16), pltpu.VMEM((ROWS, width), BF16)],
        ),
        compiler_params=params(),
        name="coarse_parts",
    )(p_mask, parts, p_tiles)


def sum_kernel(coded, out):
    total = jnp.zeros((72, 128), F32)
    for z in range(PLANES):
        block = coded[z].astype(jnp.int32).astype(F32)
        scale = jnp.exp2(block[72:80] * (1.0 / STEPS)) * (1.0 / LIMIT)
        factor = jnp.concatenate(
            [jnp.broadcast_to(scale[:1], (48, 128)), jnp.broadcast_to(scale[1:2], (24, 128))], axis=0
        )
        total = total + block[:72] * factor
    out[:, :128] = total[:48]
    out[:24, 128:] = total[48:, :64]
    out[24:, 128:] = total[48:, 64:]


def summed(coded):
    return pl.pallas_call(
        sum_kernel,
        out_shape=jax.ShapeDtypeStruct((WIDE, TILE), F32),
        in_specs=[pl.BlockSpec(memory_space=pltpu.VMEM)],
        out_specs=pl.BlockSpec(memory_space=pltpu.VMEM),
        compiler_params=params(),
        name="summed",
    )(coded)


def y_target(zl, yh, yl):
    turn = (2 * yh + yl + 8 - 2 * zl) % 8
    far = (turn + 3) // 4 % 2
    return far, far * (turn - 1) + (1 - far) * ((8 - turn) % 8)


def spread():
    pairs = []
    for source in range(4**3 * 4):
        zh, zl, yh, core, yl = source // 64, source // 16 % 4, source // 4 % 4, source // 2 % 2, source % 2
        target_yl, rank = y_target(zl, yh, yl)
        target = ((rank + 2 * core + zl) % 4 * 4 + zh) * 4 + zl
        pairs.append((source, (target * 2 + core) * 2 + target_yl))
    return pairs


def around(size, near):
    return [((i + near) % size, i) for i in range(size)]


def two_away():
    near = [2, -2]
    return [
        ((i + near[core]) % PLANES * 2 + core, i * 2 + core) for i in range(PLANES) for core in range(2)
    ]


def local(a_tiles, p_tiles, a_mask, p_mask):
    z = ("zh", "zl")
    mine = stripes(p_tiles, p_mask)
    slab = lax.ppermute(mine, z + ("yh", "core", "yl"), spread())
    a_tiles, mine = lax.optimization_barrier((a_tiles, mine))
    own = masked_operator(a_tiles, a_mask)
    after = [lax.ppermute(half, "x", around(4, 1)) for half in own]
    before = [lax.ppermute(half, "x", around(4, -1)) for half in own]

    above, below = [lax.ppermute(slab, z, around(PLANES, turn)) for turn in (1, -1)]
    slabs = [slab, above, lax.ppermute(slab, z + ("core",), two_away()), below]
    across = [
        lax.ppermute(after[0], "x", around(4, 1)),
        lax.ppermute(before[1], "x", around(4, -1)),
    ]
    blocks = [*own, *after, *across, *before]

    theirs = lax.ppermute(product(slabs, blocks, 1), "core", [(0, 1), (1, 0)])
    coded = encode(product(slabs, blocks, 0), theirs)
    coded = lax.all_to_all(coded, "yh", 0, 0, tiled=True)
    coded = lax.all_to_all(coarse_parts(coded, p_tiles, p_mask), z, 0, 0, tiled=True)
    return summed(coded).T


def solution(mesh):
    fine = Mesh(mesh.devices.reshape(4, 4, 4, 4, 2, 2), ("zh", "zl", "x", "yh", "core", "yl"))
    z, col = ("zh", "zl"), ("x", "yh", "core")
    return jax.shard_map(
        local,
        mesh=fine,
        in_specs=(P(z, col), P(z, None), P(z, col), P(z, None)),
        out_specs=P(z, col + ("yl",)),
        check_vma=False,
    )
```

```python
import functools

import jax
import jax.numpy as jnp
from jax import lax
from jax.experimental import pallas as pl
from jax.experimental.pallas import tpu as pltpu
from jax.sharding import Mesh
from jax.sharding import PartitionSpec as P

TILE = 192
WIDE = 48
ROWS = 768
HALF = 384
COARSE = 3072
PLANES = 16
LIMIT = 32766.0
STEPS = 128.0
EMPTY = 16
LEAST = 1e-33
GROUPS = ROWS // 128
CODED = 80
VMEM = 16 * 1024 * 1024
MOST_VMEM = 57 * 1024 * 1024
F32 = jnp.float32
BF16 = jnp.bfloat16


def params():
    return pltpu.CompilerParams(vmem_limit_bytes=VMEM)


def dot_last(left, right):
    return lax.dot_general(left, right, (((1,), (1,)), ((), ())), preferred_element_type=F32)


def stripes_kernel(mask_in, tiles, out, window, mask, arrived, mask_arrived):
    core, x = lax.axis_index("core"), lax.axis_index("x")
    yl, _ = y_target(lax.axis_index("zl"), lax.axis_index("yh"), lax.axis_index("yl"))
    mask_copy = pltpu.make_async_copy(mask_in, mask, mask_arrived)
    mask_copy.start()
    copies = []
    for n in range(2):
        rows = pl.ds(pl.multiple_of(core * HALF, HALF), HALF)
        columns = pl.ds(pl.multiple_of((2 * x + n) * HALF, HALF), HALF)
        copies.append(pltpu.make_async_copy(tiles.at[rows, columns], window.at[n], arrived.at[n]))
        copies[n].start()
    row = lax.broadcasted_iota(jnp.int32, (WIDE, HALF), 0)
    lane = lax.broadcasted_iota(jnp.int32, (WIDE, HALF), 1)
    picks = [(lane == row + (2 * s + yl) * WIDE).astype(F32).astype(BF16) for s in range(4)]
    pick = jnp.concatenate(picks, axis=0)
    fine = lax.broadcasted_iota(jnp.int32, (1, HALF), 1)
    out[8 * WIDE :, :] = jnp.zeros((EMPTY, HALF), BF16)
    mask_copy.wait()
    for n in range(2):
        copies[n].wait()
        picked = dot_last(pick, window[n])
        for m in range(2):
            tile = 4 * x + 2 * n + m
            upper, lower = mask[2 * core, tile], mask[2 * core + 1, tile]
            present = jnp.where(fine < TILE, upper.astype(F32), lower.astype(F32))
            part = picked[2 * WIDE * m : 2 * WIDE * (m + 1)]
            first = 2 * WIDE * (2 * n + m)
            out[first : first + 2 * WIDE, :] = (part * present).astype(BF16)


def stripes(p_tiles, p_mask):
    return pl.pallas_call(
        stripes_kernel,
        out_shape=jax.ShapeDtypeStruct((8 * WIDE + EMPTY, HALF), BF16),
        in_specs=[pl.BlockSpec(memory_space=pl.ANY)] * 2,
        out_specs=pl.BlockSpec(memory_space=pltpu.VMEM),
        scratch_shapes=[
            pltpu.VMEM((2, HALF, HALF), BF16),
            pltpu.SMEM(p_mask.shape, jnp.int32),
            pltpu.SemaphoreType.DMA((2,)),
            pltpu.SemaphoreType.DMA,
        ],
        compiler_params=pltpu.CompilerParams(vmem_limit_bytes=MOST_VMEM),
        name="stripes",
    )(p_mask, p_tiles)


def mask_rows(mask, tiles, out, first):
    height, width = tiles.shape
    lane = lax.broadcasted_iota(jnp.int32, (1, width), 1)
    for i in range(height // TILE):
        present = jnp.zeros((1, width), F32)
        for k in range(width // TILE):
            inside = (lane >= k * TILE) & (lane < (k + 1) * TILE)
            present = jnp.where(inside, mask(i, first + k).astype(F32), present)
        rows = slice(i * TILE, (i + 1) * TILE)
        out[rows, :] = tiles[rows, :] * present.astype(BF16)


def operator_kernel(mask, tiles, upper, lower):
    for half, out in enumerate((upper, lower)):
        rows = tiles[half * HALF : (half + 1) * HALF, :]
        mask_rows(lambda i, k: mask[k, 2 * half + i], rows, out, 0)


def masked_operator(a_tiles, a_mask):
    return pl.pallas_call(
        operator_kernel,
        out_shape=[jax.ShapeDtypeStruct((HALF, HALF), BF16)] * 2,
        in_specs=[pl.BlockSpec(memory_space=pltpu.SMEM), pl.BlockSpec(memory_space=pltpu.VMEM)],
        out_specs=[pl.BlockSpec(memory_space=pltpu.VMEM)] * 2,
        compiler_params=params(),
        name="masked_operator",
    )(a_mask.T, a_tiles)


def trim_kernel(padded, out):
    out[...] = padded[: 8 * WIDE, :]


def trim(padded):
    return pl.pallas_call(
        trim_kernel,
        out_shape=jax.ShapeDtypeStruct((8 * WIDE, HALF), BF16),
        in_specs=[pl.BlockSpec(memory_space=pltpu.VMEM)],
        out_specs=pl.BlockSpec(memory_space=pltpu.VMEM),
        compiler_params=params(),
        name="trim",
    )(padded)


def product_kernel(other, *refs):
    slabs, blocks, out, columns = refs[:4], refs[4:12], refs[12], refs[13]
    x, zl = lax.axis_index("x"), lax.axis_index("zl")
    core = (lax.axis_index("core") + other) % 2
    for n, slab in enumerate(slabs):
        for y in range(4):
            rows = pl.ds(pl.multiple_of((2 * y + core) * WIDE, WIDE), WIDE)
            columns[(zl + n) % 4, y * WIDE : (y + 1) * WIDE] = slab[rows, :]
    for half in range(2):
        total = dot_last(columns[x], blocks[half][...])
        for n in range(1, 4):
            total = total + dot_last(columns[(x + n) % 4], blocks[2 * n + half][...])
        out[:, :, half * HALF : (half + 1) * HALF] = total.reshape(4, WIDE, HALF)


def product(slabs, blocks, other):
    return pl.pallas_call(
        functools.partial(product_kernel, other),
        out_shape=jax.ShapeDtypeStruct((4, WIDE, ROWS), F32),
        in_specs=[pl.BlockSpec(memory_space=pltpu.VMEM)] * 12,
        out_specs=pl.BlockSpec(memory_space=pltpu.VMEM),
        scratch_shapes=[pltpu.VMEM((4, 4 * WIDE, HALF), BF16)],
        compiler_params=params(),
        name="product_for_other" if other else "product",
    )(*slabs, *blocks)


def scale_code(most):
    return jnp.ceil(jnp.log2(jnp.maximum(most, LEAST)) * STEPS) + 1.0


def encode_kernel(mine, theirs, out):
    for n in range(4):
        codes = []
        for g in range(GROUPS):
            lanes = slice(g * 128, (g + 1) * 128)
            values = mine[n, :, lanes] + theirs[n, :, lanes]
            codes.append(scale_code(jnp.max(jnp.abs(values), axis=0, keepdims=True)))
            values = jnp.round(values * (LIMIT * jnp.exp2(codes[g] * (-1.0 / STEPS))))
            out[n, g * WIDE : (g + 1) * WIDE, :] = values.astype(jnp.int32).astype(jnp.int16)
        codes = jnp.concatenate(codes + [jnp.zeros((8 - GROUPS, 128), F32)], axis=0)
        out[n, GROUPS * WIDE :, :] = codes.astype(jnp.int32).astype(jnp.int16)


def encode(mine, theirs):
    return pl.pallas_call(
        encode_kernel,
        out_shape=jax.ShapeDtypeStruct((4, GROUPS * WIDE + 8, 128), jnp.int16),
        in_specs=[pl.BlockSpec(memory_space=pltpu.VMEM)] * 2,
        out_specs=pl.BlockSpec(memory_space=pltpu.VMEM),
        compiler_params=params(),
        name="encode",
    )(mine, theirs)


def decoded_sum(coded):
    total = [jnp.zeros((WIDE, 128), F32)] * GROUPS
    for n in range(4):
        codes = coded[n, GROUPS * WIDE :, :].astype(jnp.int32).astype(F32)
        scales = jnp.exp2(codes * (1.0 / STEPS)) * (1.0 / LIMIT)
        for g in range(GROUPS):
            values = coded[n, g * WIDE : (g + 1) * WIDE, :].astype(jnp.int32).astype(F32)
            total[g] = total[g] + values * scales[g : g + 1]
    return jnp.concatenate(total, axis=1)


def pack(values):
    tail = values[:, 128:]
    return jnp.concatenate(
        [values[:, :128], jnp.concatenate([tail[:24], tail[24:]], axis=1)], axis=0
    )


def coarse_kernel(mask, parts, tiles, out, present):
    whole = decoded_sum(parts)
    high = whole.astype(BF16)
    terms = jnp.concatenate([high, (whole - high.astype(F32)).astype(BF16)], axis=0)
    width = present.shape[1]
    for n in range(COARSE // width):
        first = n * (width // TILE)
        block = tiles.at[:, n * width : (n + 1) * width]
        mask_rows(lambda i, k: mask[i, k], block, present, first)
        full = jnp.dot(terms, present[...], preferred_element_type=F32)
        full = full[:WIDE] + full[WIDE:]
        for k in range(width // TILE):
            chunk = full[:, k * TILE : (k + 1) * TILE]
            code = scale_code(jnp.max(jnp.abs(chunk), axis=0, keepdims=True))
            factor = LIMIT * jnp.exp2(code * (-1.0 / STEPS))
            values = pack(jnp.round(chunk * factor))
            scales = pack(jnp.broadcast_to(code, (WIDE, TILE)))
            empty = jnp.zeros((6, 128), F32)
            coded = jnp.concatenate([values, scales[:1], scales[48:49], empty], axis=0)
            out[first + k] = coded.astype(jnp.int32).astype(jnp.int16)


def coarse_parts(parts, p_tiles, p_mask):
    vmem = pl.BlockSpec(memory_space=pltpu.VMEM)
    return pl.pallas_call(
        coarse_kernel,
        out_shape=jax.ShapeDtypeStruct((PLANES, CODED, 128), jnp.int16),
        in_specs=[pl.BlockSpec(memory_space=pltpu.SMEM), vmem, vmem],
        out_specs=vmem,
        scratch_shapes=[pltpu.VMEM((ROWS, COARSE // 4), BF16)],
        compiler_params=params(),
        name="coarse_parts",
    )(p_mask, parts, p_tiles)


def sum_kernel(coded, out):
    total = jnp.zeros((72, 128), F32)
    for z in range(PLANES):
        block = coded[z].astype(jnp.int32).astype(F32)
        scale = jnp.exp2(block[72:80] * (1.0 / STEPS)) * (1.0 / LIMIT)
        factor = jnp.concatenate(
            [jnp.broadcast_to(scale[:1], (48, 128)), jnp.broadcast_to(scale[1:2], (24, 128))], axis=0
        )
        total = total + block[:72] * factor
    out[:, :128] = total[:48]
    out[:24, 128:] = total[48:, :64]
    out[24:, 128:] = total[48:, 64:]


def summed(coded):
    return pl.pallas_call(
        sum_kernel,
        out_shape=jax.ShapeDtypeStruct((WIDE, TILE), F32),
        in_specs=[pl.BlockSpec(memory_space=pltpu.VMEM)],
        out_specs=pl.BlockSpec(memory_space=pltpu.VMEM),
        compiler_params=params(),
        name="summed",
    )(coded)


def y_target(zl, yh, yl):
    turn = (2 * yh + yl + 8 - 2 * zl) % 8
    far = (turn + 3) // 4 % 2
    return far, far * (turn - 1) + (1 - far) * ((8 - turn) % 8)


def spread():
    pairs = []
    for source in range(4**3 * 4):
        zh, zl, yh, core, yl = source // 64, source // 16 % 4, source // 4 % 4, source // 2 % 2, source % 2
        target_yl, rank = y_target(zl, yh, yl)
        target = ((rank + 2 * core + zl) % 4 * 4 + zh) * 4 + zl
        pairs.append((source, (target * 2 + core) * 2 + target_yl))
    return pairs


def around(size, near):
    return [((i + near) % size, i) for i in range(size)]


def two_away():
    near = [2, -2]
    return [
        ((i + near[core]) % PLANES * 2 + core, i * 2 + core) for i in range(PLANES) for core in range(2)
    ]


def local(a_tiles, p_tiles, a_mask, p_mask):
    z = ("zh", "zl")
    mine = stripes(p_tiles, p_mask)
    slab = trim(lax.ppermute(mine, z + ("yh", "core", "yl"), spread()))
    a_tiles, mine = lax.optimization_barrier((a_tiles, mine))
    own = masked_operator(a_tiles, a_mask)
    after = [lax.ppermute(half, "x", around(4, 1)) for half in own]
    before = [lax.ppermute(half, "x", around(4, -1)) for half in own]

    above, below = [lax.ppermute(slab, z, around(PLANES, turn)) for turn in (1, -1)]
    slabs = [slab, above, lax.ppermute(slab, z + ("core",), two_away()), below]
    across = [
        lax.ppermute(after[0], "x", around(4, 1)),
        lax.ppermute(before[1], "x", around(4, -1)),
    ]
    blocks = [*own, *after, *across, *before]

    theirs = lax.ppermute(product(slabs, blocks, 1), "core", [(0, 1), (1, 0)])
    coded = encode(product(slabs, blocks, 0), theirs)
    coded = lax.all_to_all(coded, "yh", 0, 0, tiled=True)
    coded = lax.all_to_all(coarse_parts(coded, p_tiles, p_mask), z, 0, 0, tiled=True)
    return summed(coded).T


def solution(mesh):
    fine = Mesh(mesh.devices.reshape(4, 4, 4, 4, 2, 2), ("zh", "zl", "x", "yh", "core", "yl"))
    z, col = ("zh", "zl"), ("x", "yh", "core")
    return jax.shard_map(
        local,
        mesh=fine,
        in_specs=(P(z, col), P(z, None), P(z, col), P(z, None)),
        out_specs=P(z, col + ("yl",)),
        check_vma=False,
    )
```

```python
import functools

import jax
import jax.numpy as jnp
from jax import lax
from jax.experimental import pallas as pl
from jax.experimental.pallas import tpu as pltpu
from jax.sharding import Mesh
from jax.sharding import PartitionSpec as P

TILE = 192
WIDE = 48
ROWS = 768
HALF = 384
COARSE = 3072
PLANES = 16
LIMIT = 32766.0
STEPS = 128.0
EMPTY = 16
LEAST = 1e-33
GROUPS = ROWS // 128
CODED = 80
VMEM = 16 * 1024 * 1024
MOST_VMEM = 57 * 1024 * 1024
F32 = jnp.float32
BF16 = jnp.bfloat16


def params():
    return pltpu.CompilerParams(vmem_limit_bytes=VMEM)


def dot_last(left, right):
    return lax.dot_general(left, right, (((1,), (1,)), ((), ())), preferred_element_type=F32)


def stripes_kernel(mask_in, tiles, out, window, mask, arrived, mask_arrived):
    core, x = lax.axis_index("core"), lax.axis_index("x")
    yl, _ = y_target(lax.axis_index("zl"), lax.axis_index("yh"), lax.axis_index("yl"))
    mask_copy = pltpu.make_async_copy(mask_in, mask, mask_arrived)
    mask_copy.start()
    copies = []
    for n in range(2):
        rows = pl.ds(pl.multiple_of(core * HALF, HALF), HALF)
        columns = pl.ds(pl.multiple_of((2 * x + n) * HALF, HALF), HALF)
        copies.append(pltpu.make_async_copy(tiles.at[rows, columns], window.at[n], arrived.at[n]))
        copies[n].start()
    row = lax.broadcasted_iota(jnp.int32, (WIDE, HALF), 0)
    lane = lax.broadcasted_iota(jnp.int32, (WIDE, HALF), 1)
    picks = [(lane == row + (2 * s + yl) * WIDE).astype(F32).astype(BF16) for s in range(4)]
    pick = jnp.concatenate(picks, axis=0)
    fine = lax.broadcasted_iota(jnp.int32, (1, HALF), 1)
    out[8 * WIDE :, :] = jnp.zeros((EMPTY, HALF), BF16)
    mask_copy.wait()
    for n in range(2):
        copies[n].wait()
        picked = dot_last(pick, window[n])
        for m in range(2):
            tile = 4 * x + 2 * n + m
            upper, lower = mask[2 * core, tile], mask[2 * core + 1, tile]
            present = jnp.where(fine < TILE, upper.astype(F32), lower.astype(F32))
            part = picked[2 * WIDE * m : 2 * WIDE * (m + 1)]
            first = 2 * WIDE * (2 * n + m)
            out[first : first + 2 * WIDE, :] = (part * present).astype(BF16)


def stripes(p_tiles, p_mask):
    return pl.pallas_call(
        stripes_kernel,
        out_shape=jax.ShapeDtypeStruct((8 * WIDE + EMPTY, HALF), BF16),
        in_specs=[pl.BlockSpec(memory_space=pl.ANY)] * 2,
        out_specs=pl.BlockSpec(memory_space=pltpu.VMEM),
        scratch_shapes=[
            pltpu.VMEM((2, HALF, HALF), BF16),
            pltpu.SMEM(p_mask.shape, jnp.int32),
            pltpu.SemaphoreType.DMA((2,)),
            pltpu.SemaphoreType.DMA,
        ],
        compiler_params=pltpu.CompilerParams(vmem_limit_bytes=MOST_VMEM),
        name="stripes",
    )(p_mask, p_tiles)


def mask_rows(mask, tiles, out, first):
    height, width = tiles.shape
    lane = lax.broadcasted_iota(jnp.int32, (1, width), 1)
    for i in range(height // TILE):
        present = jnp.zeros((1, width), F32)
        for k in range(width // TILE):
            inside = (lane >= k * TILE) & (lane < (k + 1) * TILE)
            present = jnp.where(inside, mask(i, first + k).astype(F32), present)
        rows = slice(i * TILE, (i + 1) * TILE)
        out[rows, :] = tiles[rows, :] * present.astype(BF16)


def operator_kernel(mask, tiles, upper, lower):
    for half, out in enumerate((upper, lower)):
        rows = tiles[half * HALF : (half + 1) * HALF, :]
        mask_rows(lambda i, k: mask[k, 2 * half + i], rows, out, 0)


def masked_operator(a_tiles, a_mask):
    return pl.pallas_call(
        operator_kernel,
        out_shape=[jax.ShapeDtypeStruct((HALF, HALF), BF16)] * 2,
        in_specs=[pl.BlockSpec(memory_space=pltpu.SMEM), pl.BlockSpec(memory_space=pltpu.VMEM)],
        out_specs=[pl.BlockSpec(memory_space=pltpu.VMEM)] * 2,
        compiler_params=params(),
        name="masked_operator",
    )(a_mask.T, a_tiles)


def trim_kernel(padded, out):
    out[...] = padded[: 8 * WIDE, :]


def trim(padded):
    return pl.pallas_call(
        trim_kernel,
        out_shape=jax.ShapeDtypeStruct((8 * WIDE, HALF), BF16),
        in_specs=[pl.BlockSpec(memory_space=pltpu.VMEM)],
        out_specs=pl.BlockSpec(memory_space=pltpu.VMEM),
        compiler_params=params(),
        name="trim",
    )(padded)


def product_kernel(other, *refs):
    slabs, blocks, out, columns = refs[:4], refs[4:12], refs[12], refs[13]
    x, zl = lax.axis_index("x"), lax.axis_index("zl")
    core = (lax.axis_index("core") + other) % 2
    for n, slab in zip((0, 1, 3, 2), slabs):
        for y in range(4):
            rows = pl.ds(pl.multiple_of((2 * y + core) * WIDE, WIDE), WIDE)
            columns[(zl + n) % 4, y * WIDE : (y + 1) * WIDE] = slab[rows, :]
    for half in range(2):
        total = dot_last(columns[x], blocks[half][...])
        for n in range(1, 4):
            total = total + dot_last(columns[(x + n) % 4], blocks[2 * n + half][...])
        out[:, :, half * HALF : (half + 1) * HALF] = total.reshape(4, WIDE, HALF)


def product(slabs, blocks, other):
    return pl.pallas_call(
        functools.partial(product_kernel, other),
        out_shape=jax.ShapeDtypeStruct((4, WIDE, ROWS), F32),
        in_specs=[pl.BlockSpec(memory_space=pltpu.VMEM)] * 12,
        out_specs=pl.BlockSpec(memory_space=pltpu.VMEM),
        scratch_shapes=[pltpu.VMEM((4, 4 * WIDE, HALF), BF16)],
        compiler_params=params(),
        name="product_for_other" if other else "product",
    )(*slabs, *blocks)


def scale_code(most):
    return jnp.ceil(jnp.log2(jnp.maximum(most, LEAST)) * STEPS) + 1.0


def encode_kernel(mine, theirs, out):
    for n in range(4):
        codes = []
        for g in range(GROUPS):
            lanes = slice(g * 128, (g + 1) * 128)
            values = mine[n, :, lanes] + theirs[n, :, lanes]
            codes.append(scale_code(jnp.max(jnp.abs(values), axis=0, keepdims=True)))
            values = jnp.round(values * (LIMIT * jnp.exp2(codes[g] * (-1.0 / STEPS))))
            out[n, g * WIDE : (g + 1) * WIDE, :] = values.astype(jnp.int32).astype(jnp.int16)
        codes = jnp.concatenate(codes + [jnp.zeros((8 - GROUPS, 128), F32)], axis=0)
        out[n, GROUPS * WIDE :, :] = codes.astype(jnp.int32).astype(jnp.int16)


def encode(mine, theirs):
    return pl.pallas_call(
        encode_kernel,
        out_shape=jax.ShapeDtypeStruct((4, GROUPS * WIDE + 8, 128), jnp.int16),
        in_specs=[pl.BlockSpec(memory_space=pltpu.VMEM)] * 2,
        out_specs=pl.BlockSpec(memory_space=pltpu.VMEM),
        compiler_params=params(),
        name="encode",
    )(mine, theirs)


def decoded_sum(coded):
    total = [jnp.zeros((WIDE, 128), F32)] * GROUPS
    for n in range(4):
        codes = coded[n, GROUPS * WIDE :, :].astype(jnp.int32).astype(F32)
        scales = jnp.exp2(codes * (1.0 / STEPS)) * (1.0 / LIMIT)
        for g in range(GROUPS):
            values = coded[n, g * WIDE : (g + 1) * WIDE, :].astype(jnp.int32).astype(F32)
            total[g] = total[g] + values * scales[g : g + 1]
    return jnp.concatenate(total, axis=1)


def pack(values):
    tail = values[:, 128:]
    return jnp.concatenate(
        [values[:, :128], jnp.concatenate([tail[:24], tail[24:]], axis=1)], axis=0
    )


def coarse_kernel(mask, parts, tiles, out, present):
    whole = decoded_sum(parts)
    high = whole.astype(BF16)
    terms = jnp.concatenate([high, (whole - high.astype(F32)).astype(BF16)], axis=0)
    width = present.shape[1]
    for n in range(COARSE // width):
        first = n * (width // TILE)
        block = tiles.at[:, n * width : (n + 1) * width]
        mask_rows(lambda i, k: mask[i, k], block, present, first)
        full = jnp.dot(terms, present[...], preferred_element_type=F32)
        full = full[:WIDE] + full[WIDE:]
        for k in range(width // TILE):
            chunk = full[:, k * TILE : (k + 1) * TILE]
            code = scale_code(jnp.max(jnp.abs(chunk), axis=0, keepdims=True))
            factor = LIMIT * jnp.exp2(code * (-1.0 / STEPS))
            values = pack(jnp.round(chunk * factor))
            scales = pack(jnp.broadcast_to(code, (WIDE, TILE)))
            empty = jnp.zeros((6, 128), F32)
            coded = jnp.concatenate([values, scales[:1], scales[48:49], empty], axis=0)
            out[first + k] = coded.astype(jnp.int32).astype(jnp.int16)


def coarse_parts(parts, p_tiles, p_mask):
    vmem = pl.BlockSpec(memory_space=pltpu.VMEM)
    return pl.pallas_call(
        coarse_kernel,
        out_shape=jax.ShapeDtypeStruct((PLANES, CODED, 128), jnp.int16),
        in_specs=[pl.BlockSpec(memory_space=pltpu.SMEM), vmem, vmem],
        out_specs=vmem,
        scratch_shapes=[pltpu.VMEM((ROWS, COARSE // 4), BF16)],
        compiler_params=params(),
        name="coarse_parts",
    )(p_mask, parts, p_tiles)


def sum_kernel(coded, out):
    total = jnp.zeros((72, 128), F32)
    for z in range(PLANES):
        block = coded[z].astype(jnp.int32).astype(F32)
        scale = jnp.exp2(block[72:80] * (1.0 / STEPS)) * (1.0 / LIMIT)
        factor = jnp.concatenate(
            [jnp.broadcast_to(scale[:1], (48, 128)), jnp.broadcast_to(scale[1:2], (24, 128))], axis=0
        )
        total = total + block[:72] * factor
    out[:, :128] = total[:48]
    out[:24, 128:] = total[48:, :64]
    out[24:, 128:] = total[48:, 64:]


def summed(coded):
    return pl.pallas_call(
        sum_kernel,
        out_shape=jax.ShapeDtypeStruct((WIDE, TILE), F32),
        in_specs=[pl.BlockSpec(memory_space=pltpu.VMEM)],
        out_specs=pl.BlockSpec(memory_space=pltpu.VMEM),
        compiler_params=params(),
        name="summed",
    )(coded)


def y_target(zl, yh, yl):
    turn = (2 * yh + yl + 8 - 2 * zl) % 8
    far = (turn + 3) // 4 % 2
    return far, far * (turn - 1) + (1 - far) * ((8 - turn) % 8)


def spread():
    pairs = []
    for source in range(4**3 * 4):
        zh, zl, yh, core, yl = source // 64, source // 16 % 4, source // 4 % 4, source // 2 % 2, source % 2
        target_yl, rank = y_target(zl, yh, yl)
        target = ((rank + 2 * core + zl) % 4 * 4 + zh) * 4 + zl
        pairs.append((source, (target * 2 + core) * 2 + target_yl))
    return pairs


def around(size, near):
    return [((i + near) % size, i) for i in range(size)]


def two_away():
    near = [2, -2]
    return [
        ((i + near[core]) % PLANES * 2 + core, i * 2 + core) for i in range(PLANES) for core in range(2)
    ]


def local(a_tiles, p_tiles, a_mask, p_mask):
    z = ("zh", "zl")
    mine = stripes(p_tiles, p_mask)
    slab = trim(lax.ppermute(mine, z + ("yh", "core", "yl"), spread()))
    a_tiles, mine = lax.optimization_barrier((a_tiles, mine))
    own = masked_operator(a_tiles, a_mask)
    after = [lax.ppermute(half, "x", around(4, 1)) for half in own]
    before = [lax.ppermute(half, "x", around(4, -1)) for half in own]

    above, below = [lax.ppermute(slab, z, around(PLANES, turn)) for turn in (1, -1)]
    slabs = [slab, above, below, lax.ppermute(slab, z + ("core",), two_away())]
    across = [
        lax.ppermute(after[0], "x", around(4, 1)),
        lax.ppermute(before[1], "x", around(4, -1)),
    ]
    blocks = [*own, *after, *across, *before]

    theirs = lax.ppermute(product(slabs, blocks, 1), "core", [(0, 1), (1, 0)])
    coded = encode(product(slabs, blocks, 0), theirs)
    coded = lax.all_to_all(coded, "yh", 0, 0, tiled=True)
    coded = lax.all_to_all(coarse_parts(coded, p_tiles, p_mask), z, 0, 0, tiled=True)
    return summed(coded).T


def solution(mesh):
    fine = Mesh(mesh.devices.reshape(4, 4, 4, 4, 2, 2), ("zh", "zl", "x", "yh", "core", "yl"))
    z, col = ("zh", "zl"), ("x", "yh", "core")
    return jax.shard_map(
        local,
        mesh=fine,
        in_specs=(P(z, col), P(z, None), P(z, col), P(z, None)),
        out_specs=P(z, col + ("yl",)),
        check_vma=False,
    )
```

```python
import functools

import jax
import jax.numpy as jnp
from jax import lax
from jax.experimental import pallas as pl
from jax.experimental.pallas import tpu as pltpu
from jax.sharding import Mesh
from jax.sharding import PartitionSpec as P

TILE = 192
WIDE = 48
ROWS = 768
HALF = 384
COARSE = 3072
PLANES = 16
LIMIT = 32766.0
STEPS = 128.0
EMPTY = 16
LEAST = 1e-33
GROUPS = ROWS // 128
CODED = 80
VMEM = 16 * 1024 * 1024
MOST_VMEM = 57 * 1024 * 1024
F32 = jnp.float32
BF16 = jnp.bfloat16


def params():
    return pltpu.CompilerParams(vmem_limit_bytes=VMEM)


def dot_last(left, right):
    return lax.dot_general(left, right, (((1,), (1,)), ((), ())), preferred_element_type=F32)


def stripes_kernel(mask_in, tiles, out, window, mask, arrived, mask_arrived):
    core, x = lax.axis_index("core"), lax.axis_index("x")
    yl = y_target(lax.axis_index("zl"), lax.axis_index("yh"), lax.axis_index("yl"))
    mask_copy = pltpu.make_async_copy(mask_in, mask, mask_arrived)
    mask_copy.start()
    copies = []
    for n in range(2):
        rows = pl.ds(pl.multiple_of(core * HALF, HALF), HALF)
        columns = pl.ds(pl.multiple_of((2 * x + n) * HALF, HALF), HALF)
        copies.append(pltpu.make_async_copy(tiles.at[rows, columns], window.at[n], arrived.at[n]))
        copies[n].start()
    row = lax.broadcasted_iota(jnp.int32, (WIDE, HALF), 0)
    lane = lax.broadcasted_iota(jnp.int32, (WIDE, HALF), 1)
    picks = [(lane == row + (2 * s + yl) * WIDE).astype(F32).astype(BF16) for s in range(4)]
    pick = jnp.concatenate(picks, axis=0)
    fine = lax.broadcasted_iota(jnp.int32, (1, HALF), 1)
    out[8 * WIDE :, :] = jnp.zeros((EMPTY, HALF), BF16)
    mask_copy.wait()
    for n in range(2):
        copies[n].wait()
        picked = dot_last(pick, window[n])
        for m in range(2):
            tile = 4 * x + 2 * n + m
            upper, lower = mask[2 * core, tile], mask[2 * core + 1, tile]
            present = jnp.where(fine < TILE, upper.astype(F32), lower.astype(F32))
            part = picked[2 * WIDE * m : 2 * WIDE * (m + 1)]
            first = 2 * WIDE * (2 * n + m)
            out[first : first + 2 * WIDE, :] = (part * present).astype(BF16)


def stripes(p_tiles, p_mask):
    return pl.pallas_call(
        stripes_kernel,
        out_shape=jax.ShapeDtypeStruct((8 * WIDE + EMPTY, HALF), BF16),
        in_specs=[pl.BlockSpec(memory_space=pl.ANY)] * 2,
        out_specs=pl.BlockSpec(memory_space=pltpu.VMEM),
        scratch_shapes=[
            pltpu.VMEM((2, HALF, HALF), BF16),
            pltpu.SMEM(p_mask.shape, jnp.int32),
            pltpu.SemaphoreType.DMA((2,)),
            pltpu.SemaphoreType.DMA,
        ],
        compiler_params=pltpu.CompilerParams(vmem_limit_bytes=MOST_VMEM),
        name="stripes",
    )(p_mask, p_tiles)


def mask_rows(mask, tiles, out, first):
    height, width = tiles.shape
    lane = lax.broadcasted_iota(jnp.int32, (1, width), 1)
    for i in range(height // TILE):
        present = jnp.zeros((1, width), F32)
        for k in range(width // TILE):
            inside = (lane >= k * TILE) & (lane < (k + 1) * TILE)
            present = jnp.where(inside, mask(i, first + k).astype(F32), present)
        rows = slice(i * TILE, (i + 1) * TILE)
        out[rows, :] = tiles[rows, :] * present.astype(BF16)


def operator_kernel(mask, tiles, upper, lower):
    for half, out in enumerate((upper, lower)):
        rows = tiles[half * HALF : (half + 1) * HALF, :]
        mask_rows(lambda i, k: mask[k, 2 * half + i], rows, out, 0)


def masked_operator(a_tiles, a_mask):
    return pl.pallas_call(
        operator_kernel,
        out_shape=[jax.ShapeDtypeStruct((HALF, HALF), BF16)] * 2,
        in_specs=[pl.BlockSpec(memory_space=pltpu.SMEM), pl.BlockSpec(memory_space=pltpu.VMEM)],
        out_specs=[pl.BlockSpec(memory_space=pltpu.VMEM)] * 2,
        compiler_params=params(),
        name="masked_operator",
    )(a_mask.T, a_tiles)


def trim_kernel(padded, out):
    out[...] = padded[: 8 * WIDE, :]


def trim(padded):
    return pl.pallas_call(
        trim_kernel,
        out_shape=jax.ShapeDtypeStruct((8 * WIDE, HALF), BF16),
        in_specs=[pl.BlockSpec(memory_space=pltpu.VMEM)],
        out_specs=pl.BlockSpec(memory_space=pltpu.VMEM),
        compiler_params=params(),
        name="trim",
    )(padded)


def product_kernel(other, *refs):
    slabs, blocks, out, columns = refs[:4], refs[4:12], refs[12], refs[13]
    x, zl, yh = lax.axis_index("x"), lax.axis_index("zl"), lax.axis_index("yh")
    core = (lax.axis_index("core") + other) % 2
    for n, slab in zip((0, 1, 3, 2), slabs):
        block = block_of(yh, (zl + n) % 4)
        for y in range(4):
            rows = pl.ds(pl.multiple_of((2 * y + core) * WIDE, WIDE), WIDE)
            columns[block, y * WIDE : (y + 1) * WIDE] = slab[rows, :]
    for half in range(2):
        total = dot_last(columns[x], blocks[half][...])
        for n in range(1, 4):
            total = total + dot_last(columns[(x + n) % 4], blocks[2 * n + half][...])
        out[:, :, half * HALF : (half + 1) * HALF] = total.reshape(4, WIDE, HALF)


def product(slabs, blocks, other):
    return pl.pallas_call(
        functools.partial(product_kernel, other),
        out_shape=jax.ShapeDtypeStruct((4, WIDE, ROWS), F32),
        in_specs=[pl.BlockSpec(memory_space=pltpu.VMEM)] * 12,
        out_specs=pl.BlockSpec(memory_space=pltpu.VMEM),
        scratch_shapes=[pltpu.VMEM((4, 4 * WIDE, HALF), BF16)],
        compiler_params=params(),
        name="product_for_other" if other else "product",
    )(*slabs, *blocks)


def scale_code(most):
    return jnp.ceil(jnp.log2(jnp.maximum(most, LEAST)) * STEPS) + 1.0


def encode_kernel(mine, theirs, out):
    for n in range(4):
        codes = []
        for g in range(GROUPS):
            lanes = slice(g * 128, (g + 1) * 128)
            values = mine[n, :, lanes] + theirs[n, :, lanes]
            codes.append(scale_code(jnp.max(jnp.abs(values), axis=0, keepdims=True)))
            values = jnp.round(values * (LIMIT * jnp.exp2(codes[g] * (-1.0 / STEPS))))
            out[n, g * WIDE : (g + 1) * WIDE, :] = values.astype(jnp.int32).astype(jnp.int16)
        codes = jnp.concatenate(codes + [jnp.zeros((8 - GROUPS, 128), F32)], axis=0)
        out[n, GROUPS * WIDE :, :] = codes.astype(jnp.int32).astype(jnp.int16)


def encode(mine, theirs):
    return pl.pallas_call(
        encode_kernel,
        out_shape=jax.ShapeDtypeStruct((4, GROUPS * WIDE + 8, 128), jnp.int16),
        in_specs=[pl.BlockSpec(memory_space=pltpu.VMEM)] * 2,
        out_specs=pl.BlockSpec(memory_space=pltpu.VMEM),
        compiler_params=params(),
        name="encode",
    )(mine, theirs)


def decoded_sum(coded):
    total = [jnp.zeros((WIDE, 128), F32)] * GROUPS
    for n in range(4):
        codes = coded[n, GROUPS * WIDE :, :].astype(jnp.int32).astype(F32)
        scales = jnp.exp2(codes * (1.0 / STEPS)) * (1.0 / LIMIT)
        for g in range(GROUPS):
            values = coded[n, g * WIDE : (g + 1) * WIDE, :].astype(jnp.int32).astype(F32)
            total[g] = total[g] + values * scales[g : g + 1]
    return jnp.concatenate(total, axis=1)


def pack(values):
    tail = values[:, 128:]
    return jnp.concatenate(
        [values[:, :128], jnp.concatenate([tail[:24], tail[24:]], axis=1)], axis=0
    )


def coarse_kernel(mask, parts, tiles, out, present):
    whole = decoded_sum(parts)
    high = whole.astype(BF16)
    terms = jnp.concatenate([high, (whole - high.astype(F32)).astype(BF16)], axis=0)
    width = present.shape[1]
    for n in range(COARSE // width):
        first = n * (width // TILE)
        block = tiles.at[:, n * width : (n + 1) * width]
        mask_rows(lambda i, k: mask[i, k], block, present, first)
        full = jnp.dot(terms, present[...], preferred_element_type=F32)
        full = full[:WIDE] + full[WIDE:]
        for k in range(width // TILE):
            chunk = full[:, k * TILE : (k + 1) * TILE]
            code = scale_code(jnp.max(jnp.abs(chunk), axis=0, keepdims=True))
            factor = LIMIT * jnp.exp2(code * (-1.0 / STEPS))
            values = pack(jnp.round(chunk * factor))
            scales = pack(jnp.broadcast_to(code, (WIDE, TILE)))
            empty = jnp.zeros((6, 128), F32)
            coded = jnp.concatenate([values, scales[:1], scales[48:49], empty], axis=0)
            out[first + k] = coded.astype(jnp.int32).astype(jnp.int16)


def coarse_parts(parts, p_tiles, p_mask):
    vmem = pl.BlockSpec(memory_space=pltpu.VMEM)
    return pl.pallas_call(
        coarse_kernel,
        out_shape=jax.ShapeDtypeStruct((PLANES, CODED, 128), jnp.int16),
        in_specs=[pl.BlockSpec(memory_space=pltpu.SMEM), vmem, vmem],
        out_specs=vmem,
        scratch_shapes=[pltpu.VMEM((ROWS, COARSE // 4), BF16)],
        compiler_params=params(),
        name="coarse_parts",
    )(p_mask, parts, p_tiles)


def sum_kernel(coded, out):
    total = jnp.zeros((72, 128), F32)
    for z in range(PLANES):
        block = coded[z].astype(jnp.int32).astype(F32)
        scale = jnp.exp2(block[72:80] * (1.0 / STEPS)) * (1.0 / LIMIT)
        factor = jnp.concatenate(
            [jnp.broadcast_to(scale[:1], (48, 128)), jnp.broadcast_to(scale[1:2], (24, 128))], axis=0
        )
        total = total + block[:72] * factor
    out[:, :128] = total[:48]
    out[:24, 128:] = total[48:, :64]
    out[24:, 128:] = total[48:, 64:]


def summed(coded):
    return pl.pallas_call(
        sum_kernel,
        out_shape=jax.ShapeDtypeStruct((WIDE, TILE), F32),
        in_specs=[pl.BlockSpec(memory_space=pltpu.VMEM)],
        out_specs=pl.BlockSpec(memory_space=pltpu.VMEM),
        compiler_params=params(),
        name="summed",
    )(coded)


PLACE = ((0, 1, 2, 3), (2, 0, 1, 3), (1, 3, 0, 2), (3, 2, 1, 0))
TURNS = (
    0x8D28D637, 0x778E1D82, 0xD87D2782, 0x22D4B87D,
    0x2D8278D7, 0x727D88D2, 0x7D8E1782, 0x7872D1E8,
    0x8D24EB17, 0xDD8722B4, 0x8D28D727, 0x82D8771E,
    0x8728D72D, 0x72D788D2, 0x287D287D, 0xD2D78368,
)


def block_of(yh, zl):
    block = jnp.int32(0)
    for y in range(4):
        for n in range(4):
            block = jnp.where((yh == y) & (zl == PLACE[y][n]), n, block)
    return block


def y_target(zl, yh, yl):
    return ((2 * yh + yl + 8 - 2 * zl) % 8 + 3) // 4 % 2


def spread():
    pairs = []
    for source in range(4**3 * 4):
        zh, zl, yh, core, yl = source // 64, source // 16 % 4, source // 4 % 4, source // 2 % 2, source % 2
        target_yl = y_target(zl, yh, yl)
        turn = TURNS[zh * 4 + zl] >> (yh * 8 + yl * 4 + core * 2) & 3
        target = (turn * 4 + PLACE[zl][zh]) * 4 + zl
        pairs.append((source, (target * 2 + core) * 2 + target_yl))
    return pairs


def around(size, near):
    return [((i + near) % size, i) for i in range(size)]


def two_away():
    near = [2, -2]
    return [
        ((i + near[core]) % PLANES * 2 + core, i * 2 + core) for i in range(PLANES) for core in range(2)
    ]


def local(a_tiles, p_tiles, a_mask, p_mask):
    z = ("zh", "zl")
    mine = stripes(p_tiles, p_mask)
    slab = trim(lax.ppermute(mine, z + ("yh", "core", "yl"), spread()))
    a_tiles, mine = lax.optimization_barrier((a_tiles, mine))
    own = masked_operator(a_tiles, a_mask)
    after = [lax.ppermute(half, "x", around(4, 1)) for half in own]
    before = [lax.ppermute(half, "x", around(4, -1)) for half in own]

    above, below = [lax.ppermute(slab, z, around(PLANES, turn)) for turn in (1, -1)]
    slabs = [slab, above, below, lax.ppermute(slab, z + ("core",), two_away())]
    across = [
        lax.ppermute(after[0], "x", around(4, 1)),
        lax.ppermute(before[1], "x", around(4, -1)),
    ]
    blocks = [*own, *after, *across, *before]

    theirs = lax.ppermute(product(slabs, blocks, 1), "core", [(0, 1), (1, 0)])
    coded = encode(product(slabs, blocks, 0), theirs)
    coded = lax.all_to_all(coded, "yh", 0, 0, tiled=True)
    coded = lax.all_to_all(coarse_parts(coded, p_tiles, p_mask), z, 0, 0, tiled=True)
    return summed(coded).T


def solution(mesh):
    fine = Mesh(mesh.devices.reshape(4, 4, 4, 4, 2, 2), ("zh", "zl", "x", "yh", "core", "yl"))
    z, col = ("zh", "zl"), ("x", "yh", "core")
    return jax.shard_map(
        local,
        mesh=fine,
        in_specs=(P(z, col), P(z, None), P(z, col), P(z, None)),
        out_specs=P(z, col + ("yl",)),
        check_vma=False,
    )
```

```python
import functools

import jax
import jax.numpy as jnp
from jax import lax
from jax.experimental import pallas as pl
from jax.experimental.pallas import tpu as pltpu
from jax.sharding import Mesh
from jax.sharding import PartitionSpec as P

TILE = 192
WIDE = 48
ROWS = 768
HALF = 384
COARSE = 3072
PLANES = 16
LIMIT = 32766.0
STEPS = 128.0
EMPTY = 16
LEAST = 1e-33
GROUPS = ROWS // 128
CODED = 80
VMEM = 16 * 1024 * 1024
MOST_VMEM = 57 * 1024 * 1024
F32 = jnp.float32
BF16 = jnp.bfloat16


def params():
    return pltpu.CompilerParams(vmem_limit_bytes=VMEM)


def dot_last(left, right):
    return lax.dot_general(left, right, (((1,), (1,)), ((), ())), preferred_element_type=F32)


def stripes_kernel(mask_in, tiles, out, window, mask, arrived, mask_arrived):
    core, x = lax.axis_index("core"), lax.axis_index("x")
    yl = y_target(lax.axis_index("zl"), lax.axis_index("yh"), lax.axis_index("yl"))
    mask_copy = pltpu.make_async_copy(mask_in, mask, mask_arrived)
    mask_copy.start()
    copies = []
    for n in range(2):
        rows = pl.ds(pl.multiple_of(core * HALF, HALF), HALF)
        columns = pl.ds(pl.multiple_of((2 * x + n) * HALF, HALF), HALF)
        copies.append(pltpu.make_async_copy(tiles.at[rows, columns], window.at[n], arrived.at[n]))
        copies[n].start()
    row = lax.broadcasted_iota(jnp.int32, (WIDE, HALF), 0)
    lane = lax.broadcasted_iota(jnp.int32, (WIDE, HALF), 1)
    picks = [(lane == row + (2 * s + yl) * WIDE).astype(F32).astype(BF16) for s in range(4)]
    pick = jnp.concatenate(picks, axis=0)
    fine = lax.broadcasted_iota(jnp.int32, (1, HALF), 1)
    out[8 * WIDE :, :] = jnp.zeros((EMPTY, HALF), BF16)
    mask_copy.wait()
    for n in range(2):
        copies[n].wait()
        picked = dot_last(pick, window[n])
        for m in range(2):
            tile = 4 * x + 2 * n + m
            upper, lower = mask[2 * core, tile], mask[2 * core + 1, tile]
            present = jnp.where(fine < TILE, upper.astype(F32), lower.astype(F32))
            part = picked[2 * WIDE * m : 2 * WIDE * (m + 1)]
            first = 2 * WIDE * (2 * n + m)
            out[first : first + 2 * WIDE, :] = (part * present).astype(BF16)


def stripes(p_tiles, p_mask):
    return pl.pallas_call(
        stripes_kernel,
        out_shape=jax.ShapeDtypeStruct((8 * WIDE + EMPTY, HALF), BF16),
        in_specs=[pl.BlockSpec(memory_space=pl.ANY)] * 2,
        out_specs=pl.BlockSpec(memory_space=pltpu.VMEM),
        scratch_shapes=[
            pltpu.VMEM((2, HALF, HALF), BF16),
            pltpu.SMEM(p_mask.shape, jnp.int32),
            pltpu.SemaphoreType.DMA((2,)),
            pltpu.SemaphoreType.DMA,
        ],
        compiler_params=pltpu.CompilerParams(vmem_limit_bytes=MOST_VMEM),
        name="stripes",
    )(p_mask, p_tiles)


def mask_rows(mask, tiles, out, first):
    height, width = tiles.shape
    lane = lax.broadcasted_iota(jnp.int32, (1, width), 1)
    for i in range(height // TILE):
        present = jnp.zeros((1, width), F32)
        for k in range(width // TILE):
            inside = (lane >= k * TILE) & (lane < (k + 1) * TILE)
            present = jnp.where(inside, mask(i, first + k).astype(F32), present)
        rows = slice(i * TILE, (i + 1) * TILE)
        out[rows, :] = tiles[rows, :] * present.astype(BF16)


def operator_kernel(mask, tiles, upper, lower):
    for half, out in enumerate((upper, lower)):
        rows = tiles[half * HALF : (half + 1) * HALF, :]
        mask_rows(lambda i, k: mask[k, 2 * half + i], rows, out, 0)


def masked_operator(a_tiles, a_mask):
    return pl.pallas_call(
        operator_kernel,
        out_shape=[jax.ShapeDtypeStruct((HALF, HALF), BF16)] * 2,
        in_specs=[pl.BlockSpec(memory_space=pltpu.SMEM), pl.BlockSpec(memory_space=pltpu.VMEM)],
        out_specs=[pl.BlockSpec(memory_space=pltpu.VMEM)] * 2,
        compiler_params=params(),
        name="masked_operator",
    )(a_mask.T, a_tiles)


def trim_kernel(padded, out):
    out[...] = padded[: 8 * WIDE, :]


def trim(padded):
    return pl.pallas_call(
        trim_kernel,
        out_shape=jax.ShapeDtypeStruct((8 * WIDE, HALF), BF16),
        in_specs=[pl.BlockSpec(memory_space=pltpu.VMEM)],
        out_specs=pl.BlockSpec(memory_space=pltpu.VMEM),
        compiler_params=params(),
        name="trim",
    )(padded)


def product_kernel(other, *refs):
    slabs, blocks, out, columns = refs[:4], refs[4:12], refs[12], refs[13]
    x, zl, yh = lax.axis_index("x"), lax.axis_index("zl"), lax.axis_index("yh")
    core = (lax.axis_index("core") + other) % 2
    for n, slab in zip((0, 1, 3, 2), slabs):
        block = block_of(yh, (zl + n) % 4)
        for y in range(4):
            rows = pl.ds(pl.multiple_of((2 * y + core) * WIDE, WIDE), WIDE)
            columns[block, y * WIDE : (y + 1) * WIDE] = slab[rows, :]
    for half in range(2):
        total = dot_last(columns[x], blocks[half][...])
        for n in range(1, 4):
            total = total + dot_last(columns[(x + n) % 4], blocks[2 * n + half][...])
        out[:, :, half * HALF : (half + 1) * HALF] = total.reshape(4, WIDE, HALF)


def product(slabs, blocks, other):
    return pl.pallas_call(
        functools.partial(product_kernel, other),
        out_shape=jax.ShapeDtypeStruct((4, WIDE, ROWS), F32),
        in_specs=[pl.BlockSpec(memory_space=pltpu.VMEM)] * 12,
        out_specs=pl.BlockSpec(memory_space=pltpu.VMEM),
        scratch_shapes=[pltpu.VMEM((4, 4 * WIDE, HALF), BF16)],
        compiler_params=params(),
        name="product_for_other" if other else "product",
    )(*slabs, *blocks)


def scale_code(most):
    return jnp.ceil(jnp.log2(jnp.maximum(most, LEAST)) * STEPS) + 1.0


def encode_kernel(mine, theirs, out):
    for n in range(4):
        codes = []
        for g in range(GROUPS):
            lanes = slice(g * 128, (g + 1) * 128)
            values = mine[n, :, lanes] + theirs[n, :, lanes]
            codes.append(scale_code(jnp.max(jnp.abs(values), axis=0, keepdims=True)))
            values = jnp.round(values * (LIMIT * jnp.exp2(codes[g] * (-1.0 / STEPS))))
            out[n, g * WIDE : (g + 1) * WIDE, :] = values.astype(jnp.int32).astype(jnp.int16)
        codes = jnp.concatenate(codes + [jnp.zeros((8 - GROUPS, 128), F32)], axis=0)
        out[n, GROUPS * WIDE :, :] = codes.astype(jnp.int32).astype(jnp.int16)


def encode(mine, theirs):
    return pl.pallas_call(
        encode_kernel,
        out_shape=jax.ShapeDtypeStruct((4, GROUPS * WIDE + 8, 128), jnp.int16),
        in_specs=[pl.BlockSpec(memory_space=pltpu.VMEM)] * 2,
        out_specs=pl.BlockSpec(memory_space=pltpu.VMEM),
        compiler_params=params(),
        name="encode",
    )(mine, theirs)


def decoded_sum(coded):
    total = [jnp.zeros((WIDE, 128), F32)] * GROUPS
    for n in range(4):
        codes = coded[n, GROUPS * WIDE :, :].astype(jnp.int32).astype(F32)
        scales = jnp.exp2(codes * (1.0 / STEPS)) * (1.0 / LIMIT)
        for g in range(GROUPS):
            values = coded[n, g * WIDE : (g + 1) * WIDE, :].astype(jnp.int32).astype(F32)
            total[g] = total[g] + values * scales[g : g + 1]
    return jnp.concatenate(total, axis=1)


def pack(values):
    tail = values[:, 128:]
    return jnp.concatenate(
        [values[:, :128], jnp.concatenate([tail[:24], tail[24:]], axis=1)], axis=0
    )


def coarse_kernel(mask, parts, tiles, out, present):
    whole = decoded_sum(parts)
    high = whole.astype(BF16)
    terms = jnp.concatenate([high, (whole - high.astype(F32)).astype(BF16)], axis=0)
    width = present.shape[1]
    for n in range(COARSE // width):
        first = n * (width // TILE)
        block = tiles.at[:, n * width : (n + 1) * width]
        mask_rows(lambda i, k: mask[i, k], block, present, first)
        full = jnp.dot(terms, present[...], preferred_element_type=F32)
        full = full[:WIDE] + full[WIDE:]
        for k in range(width // TILE):
            chunk = full[:, k * TILE : (k + 1) * TILE]
            code = scale_code(jnp.max(jnp.abs(chunk), axis=0, keepdims=True))
            factor = LIMIT * jnp.exp2(code * (-1.0 / STEPS))
            values = pack(jnp.round(chunk * factor))
            scales = pack(jnp.broadcast_to(code, (WIDE, TILE)))
            empty = jnp.zeros((6, 128), F32)
            coded = jnp.concatenate([values, scales[:1], scales[48:49], empty], axis=0)
            out[first + k] = coded.astype(jnp.int32).astype(jnp.int16)


def coarse_parts(parts, p_tiles, p_mask):
    vmem = pl.BlockSpec(memory_space=pltpu.VMEM)
    return pl.pallas_call(
        coarse_kernel,
        out_shape=jax.ShapeDtypeStruct((PLANES, CODED, 128), jnp.int16),
        in_specs=[pl.BlockSpec(memory_space=pltpu.SMEM), vmem, vmem],
        out_specs=vmem,
        scratch_shapes=[pltpu.VMEM((ROWS, COARSE // 4), BF16)],
        compiler_params=params(),
        name="coarse_parts",
    )(p_mask, parts, p_tiles)


def sum_kernel(coded, out):
    total = jnp.zeros((72, 128), F32)
    for z in range(PLANES):
        block = coded[z].astype(jnp.int32).astype(F32)
        scale = jnp.exp2(block[72:80] * (1.0 / STEPS)) * (1.0 / LIMIT)
        factor = jnp.concatenate(
            [jnp.broadcast_to(scale[:1], (48, 128)), jnp.broadcast_to(scale[1:2], (24, 128))], axis=0
        )
        total = total + block[:72] * factor
    out[:, :128] = total[:48]
    out[:24, 128:] = total[48:, :64]
    out[24:, 128:] = total[48:, 64:]


def summed(coded):
    return pl.pallas_call(
        sum_kernel,
        out_shape=jax.ShapeDtypeStruct((WIDE, TILE), F32),
        in_specs=[pl.BlockSpec(memory_space=pltpu.VMEM)],
        out_specs=pl.BlockSpec(memory_space=pltpu.VMEM),
        compiler_params=params(),
        name="summed",
    )(coded)


PLACE = ((0, 1, 2, 3), (2, 0, 1, 3), (1, 3, 0, 2), (3, 2, 1, 0))
TURNS = (
    0x8D28D637, 0x778E1D82, 0xD87D2782, 0x22D4B87D,
    0x2D8278D7, 0x727D88D2, 0x7D8E1782, 0x7872D1E8,
    0x8D24EB17, 0xDD8722B4, 0x8D28D727, 0x82D8771E,
    0x8728D72D, 0x72D788D2, 0x287D287D, 0xD2D78368,
)


def block_of(yh, zl):
    block = jnp.int32(0)
    for y in range(4):
        for n in range(4):
            block = jnp.where((yh == y) & (zl == PLACE[y][n]), n, block)
    return block


def y_target(zl, yh, yl):
    return ((2 * yh + yl + 8 - 2 * zl) % 8 + 3) // 4 % 2


def spread():
    pairs = []
    for source in range(4**3 * 4):
        zh, zl, yh, core, yl = source // 64, source // 16 % 4, source // 4 % 4, source // 2 % 2, source % 2
        target_yl = y_target(zl, yh, yl)
        turn = TURNS[zh * 4 + zl] >> (yh * 8 + yl * 4 + core * 2) & 3
        target = (turn * 4 + PLACE[zl][zh]) * 4 + zl
        pairs.append((source, (target * 2 + core) * 2 + target_yl))
    return pairs


def around(size, near):
    return [((i + near) % size, i) for i in range(size)]


def two_away():
    near = [2, -2]
    return [
        ((i + near[core]) % PLANES * 2 + core, i * 2 + core) for i in range(PLANES) for core in range(2)
    ]


def local(a_tiles, p_tiles, a_mask, p_mask):
    z = ("zh", "zl")
    mine = stripes(p_tiles, p_mask)
    padded = lax.ppermute(mine, z + ("yh", "core", "yl"), spread())
    a_tiles, mine = lax.optimization_barrier((a_tiles, mine))
    own = masked_operator(a_tiles, a_mask)
    after = [lax.ppermute(half, "x", around(4, 1)) for half in own]
    before = [lax.ppermute(half, "x", around(4, -1)) for half in own]

    slab = trim(padded)
    above, below = [lax.ppermute(slab, z, around(PLANES, turn)) for turn in (1, -1)]
    slabs = [slab, above, below, lax.ppermute(padded, z + ("core",), two_away())]
    across = [
        lax.ppermute(after[0], "x", around(4, 1)),
        lax.ppermute(before[1], "x", around(4, -1)),
    ]
    blocks = [*own, *after, *across, *before]

    theirs = lax.ppermute(product(slabs, blocks, 1), "core", [(0, 1), (1, 0)])
    coded = encode(product(slabs, blocks, 0), theirs)
    coded = lax.all_to_all(coded, "yh", 0, 0, tiled=True)
    coded = lax.all_to_all(coarse_parts(coded, p_tiles, p_mask), z, 0, 0, tiled=True)
    return summed(coded).T


def solution(mesh):
    fine = Mesh(mesh.devices.reshape(4, 4, 4, 4, 2, 2), ("zh", "zl", "x", "yh", "core", "yl"))
    z, col = ("zh", "zl"), ("x", "yh", "core")
    return jax.shard_map(
        local,
        mesh=fine,
        in_specs=(P(z, col), P(z, None), P(z, col), P(z, None)),
        out_specs=P(z, col + ("yl",)),
        check_vma=False,
    )
```

```python
import functools

import jax
import jax.numpy as jnp
from jax import lax
from jax.experimental import pallas as pl
from jax.experimental.pallas import tpu as pltpu
from jax.sharding import Mesh
from jax.sharding import PartitionSpec as P

TILE = 192
WIDE = 48
ROWS = 768
HALF = 384
COARSE = 3072
PLANES = 16
LIMIT = 32766.0
STEPS = 128.0
EMPTY = 16
LEAST = 1e-33
GROUPS = ROWS // 128
CODED = 80
VMEM = 16 * 1024 * 1024
MOST_VMEM = 57 * 1024 * 1024
F32 = jnp.float32
BF16 = jnp.bfloat16


def params():
    return pltpu.CompilerParams(vmem_limit_bytes=VMEM)


def dot_last(left, right):
    return lax.dot_general(left, right, (((1,), (1,)), ((), ())), preferred_element_type=F32)


def stripes_kernel(mask_in, tiles, out, window, mask, arrived, mask_arrived):
    core, x = lax.axis_index("core"), lax.axis_index("x")
    yl = y_target(lax.axis_index("zl"), lax.axis_index("yh"), lax.axis_index("yl"))
    mask_copy = pltpu.make_async_copy(mask_in, mask, mask_arrived)
    mask_copy.start()
    copies = []
    for n in range(2):
        rows = pl.ds(pl.multiple_of(core * HALF, HALF), HALF)
        columns = pl.ds(pl.multiple_of((2 * x + n) * HALF, HALF), HALF)
        copies.append(pltpu.make_async_copy(tiles.at[rows, columns], window.at[n], arrived.at[n]))
        copies[n].start()
    row = lax.broadcasted_iota(jnp.int32, (WIDE, HALF), 0)
    lane = lax.broadcasted_iota(jnp.int32, (WIDE, HALF), 1)
    picks = [(lane == row + (2 * s + yl) * WIDE).astype(F32).astype(BF16) for s in range(4)]
    pick = jnp.concatenate(picks, axis=0)
    fine = lax.broadcasted_iota(jnp.int32, (1, HALF), 1)
    out[8 * WIDE :, :] = jnp.zeros((EMPTY, HALF), BF16)
    mask_copy.wait()
    for n in range(2):
        copies[n].wait()
        picked = dot_last(pick, window[n])
        for m in range(2):
            tile = 4 * x + 2 * n + m
            upper, lower = mask[2 * core, tile], mask[2 * core + 1, tile]
            present = jnp.where(fine < TILE, upper.astype(F32), lower.astype(F32))
            part = picked[2 * WIDE * m : 2 * WIDE * (m + 1)]
            first = 2 * WIDE * (2 * n + m)
            out[first : first + 2 * WIDE, :] = (part * present).astype(BF16)


def stripes(p_tiles, p_mask):
    return pl.pallas_call(
        stripes_kernel,
        out_shape=jax.ShapeDtypeStruct((8 * WIDE + EMPTY, HALF), BF16),
        in_specs=[pl.BlockSpec(memory_space=pl.ANY)] * 2,
        out_specs=pl.BlockSpec(memory_space=pltpu.VMEM),
        scratch_shapes=[
            pltpu.VMEM((2, HALF, HALF), BF16),
            pltpu.SMEM(p_mask.shape, jnp.int32),
            pltpu.SemaphoreType.DMA((2,)),
            pltpu.SemaphoreType.DMA,
        ],
        compiler_params=pltpu.CompilerParams(vmem_limit_bytes=MOST_VMEM),
        name="stripes",
    )(p_mask, p_tiles)


def mask_rows(mask, tiles, out, first):
    height, width = tiles.shape
    lane = lax.broadcasted_iota(jnp.int32, (1, width), 1)
    for i in range(height // TILE):
        present = jnp.zeros((1, width), F32)
        for k in range(width // TILE):
            inside = (lane >= k * TILE) & (lane < (k + 1) * TILE)
            present = jnp.where(inside, mask(i, first + k).astype(F32), present)
        rows = slice(i * TILE, (i + 1) * TILE)
        out[rows, :] = tiles[rows, :] * present.astype(BF16)


def operator_kernel(mask, tiles, whole, upper, lower):
    mask_rows(lambda i, k: mask[k, i], tiles, whole, 0)
    upper[...], lower[...] = whole[:HALF], whole[HALF:]


def masked_operator(a_tiles, a_mask):
    return pl.pallas_call(
        operator_kernel,
        out_shape=[jax.ShapeDtypeStruct((n * HALF, HALF), BF16) for n in (2, 1, 1)],
        in_specs=[pl.BlockSpec(memory_space=pltpu.SMEM), pl.BlockSpec(memory_space=pltpu.VMEM)],
        out_specs=[pl.BlockSpec(memory_space=pltpu.VMEM)] * 3,
        compiler_params=params(),
        name="masked_operator",
    )(a_mask.T, a_tiles)


def trim_kernel(padded, out):
    out[...] = padded[: 8 * WIDE, :]


def trim(padded):
    return pl.pallas_call(
        trim_kernel,
        out_shape=jax.ShapeDtypeStruct((8 * WIDE, HALF), BF16),
        in_specs=[pl.BlockSpec(memory_space=pltpu.VMEM)],
        out_specs=pl.BlockSpec(memory_space=pltpu.VMEM),
        compiler_params=params(),
        name="trim",
    )(padded)


def product_kernel(other, *refs):
    slabs, (own, behind), halves, out, columns = refs[:4], refs[4:6], refs[6:10], refs[10], refs[11]
    x, zl, yh = lax.axis_index("x"), lax.axis_index("zl"), lax.axis_index("yh")
    core = (lax.axis_index("core") + other) % 2
    for n, slab in zip((0, 1, 3, 2), slabs):
        block = block_of(yh, (zl + n) % 4)
        for y in range(4):
            rows = pl.ds(pl.multiple_of((2 * y + core) * WIDE, WIDE), WIDE)
            columns[block, y * WIDE : (y + 1) * WIDE] = slab[rows, :]
    for half in range(2):
        rows = slice(half * HALF, (half + 1) * HALF)
        total = dot_last(columns[x], own[rows, :])
        total = total + dot_last(columns[(x + 1) % 4], halves[half][...])
        total = total + dot_last(columns[(x + 2) % 4], halves[2 + half][...])
        total = total + dot_last(columns[(x + 3) % 4], behind[rows, :])
        out[:, :, rows] = total.reshape(4, WIDE, HALF)


def product(slabs, blocks, other):
    return pl.pallas_call(
        functools.partial(product_kernel, other),
        out_shape=jax.ShapeDtypeStruct((4, WIDE, ROWS), F32),
        in_specs=[pl.BlockSpec(memory_space=pltpu.VMEM)] * 10,
        out_specs=pl.BlockSpec(memory_space=pltpu.VMEM),
        scratch_shapes=[pltpu.VMEM((4, 4 * WIDE, HALF), BF16)],
        compiler_params=params(),
        name="product_for_other" if other else "product",
    )(*slabs, *blocks)


def scale_code(most):
    return jnp.ceil(jnp.log2(jnp.maximum(most, LEAST)) * STEPS) + 1.0


def encode_kernel(mine, theirs, out):
    for n in range(4):
        codes = []
        for g in range(GROUPS):
            lanes = slice(g * 128, (g + 1) * 128)
            values = mine[n, :, lanes] + theirs[n, :, lanes]
            codes.append(scale_code(jnp.max(jnp.abs(values), axis=0, keepdims=True)))
            values = jnp.round(values * (LIMIT * jnp.exp2(codes[g] * (-1.0 / STEPS))))
            out[n, g * WIDE : (g + 1) * WIDE, :] = values.astype(jnp.int32).astype(jnp.int16)
        codes = jnp.concatenate(codes + [jnp.zeros((8 - GROUPS, 128), F32)], axis=0)
        out[n, GROUPS * WIDE :, :] = codes.astype(jnp.int32).astype(jnp.int16)


def encode(mine, theirs):
    return pl.pallas_call(
        encode_kernel,
        out_shape=jax.ShapeDtypeStruct((4, GROUPS * WIDE + 8, 128), jnp.int16),
        in_specs=[pl.BlockSpec(memory_space=pltpu.VMEM)] * 2,
        out_specs=pl.BlockSpec(memory_space=pltpu.VMEM),
        compiler_params=params(),
        name="encode",
    )(mine, theirs)


def decoded_sum(coded):
    total = [jnp.zeros((WIDE, 128), F32)] * GROUPS
    for n in range(4):
        codes = coded[n, GROUPS * WIDE :, :].astype(jnp.int32).astype(F32)
        scales = jnp.exp2(codes * (1.0 / STEPS)) * (1.0 / LIMIT)
        for g in range(GROUPS):
            values = coded[n, g * WIDE : (g + 1) * WIDE, :].astype(jnp.int32).astype(F32)
            total[g] = total[g] + values * scales[g : g + 1]
    return jnp.concatenate(total, axis=1)


def pack(values):
    tail = values[:, 128:]
    return jnp.concatenate(
        [values[:, :128], jnp.concatenate([tail[:24], tail[24:]], axis=1)], axis=0
    )


def coarse_kernel(mask, parts, tiles, out, present):
    whole = decoded_sum(parts)
    high = whole.astype(BF16)
    terms = jnp.concatenate([high, (whole - high.astype(F32)).astype(BF16)], axis=0)
    width = present.shape[1]
    for n in range(COARSE // width):
        first = n * (width // TILE)
        block = tiles.at[:, n * width : (n + 1) * width]
        mask_rows(lambda i, k: mask[i, k], block, present, first)
        full = jnp.dot(terms, present[...], preferred_element_type=F32)
        full = full[:WIDE] + full[WIDE:]
        for k in range(width // TILE):
            chunk = full[:, k * TILE : (k + 1) * TILE]
            code = scale_code(jnp.max(jnp.abs(chunk), axis=0, keepdims=True))
            factor = LIMIT * jnp.exp2(code * (-1.0 / STEPS))
            values = pack(jnp.round(chunk * factor))
            scales = pack(jnp.broadcast_to(code, (WIDE, TILE)))
            empty = jnp.zeros((6, 128), F32)
            coded = jnp.concatenate([values, scales[:1], scales[48:49], empty], axis=0)
            out[first + k] = coded.astype(jnp.int32).astype(jnp.int16)


def coarse_parts(parts, p_tiles, p_mask):
    vmem = pl.BlockSpec(memory_space=pltpu.VMEM)
    return pl.pallas_call(
        coarse_kernel,
        out_shape=jax.ShapeDtypeStruct((PLANES, CODED, 128), jnp.int16),
        in_specs=[pl.BlockSpec(memory_space=pltpu.SMEM), vmem, vmem],
        out_specs=vmem,
        scratch_shapes=[pltpu.VMEM((ROWS, COARSE // 4), BF16)],
        compiler_params=params(),
        name="coarse_parts",
    )(p_mask, parts, p_tiles)


def sum_kernel(coded, out):
    total = jnp.zeros((72, 128), F32)
    for z in range(PLANES):
        block = coded[z].astype(jnp.int32).astype(F32)
        scale = jnp.exp2(block[72:80] * (1.0 / STEPS)) * (1.0 / LIMIT)
        factor = jnp.concatenate(
            [jnp.broadcast_to(scale[:1], (48, 128)), jnp.broadcast_to(scale[1:2], (24, 128))], axis=0
        )
        total = total + block[:72] * factor
    out[:, :128] = total[:48]
    out[:24, 128:] = total[48:, :64]
    out[24:, 128:] = total[48:, 64:]


def summed(coded):
    return pl.pallas_call(
        sum_kernel,
        out_shape=jax.ShapeDtypeStruct((WIDE, TILE), F32),
        in_specs=[pl.BlockSpec(memory_space=pltpu.VMEM)],
        out_specs=pl.BlockSpec(memory_space=pltpu.VMEM),
        compiler_params=params(),
        name="summed",
    )(coded)


PLACE = ((0, 1, 2, 3), (2, 0, 1, 3), (1, 3, 0, 2), (3, 2, 1, 0))
TURNS = (
    0x8D28D637, 0x778E1D82, 0xD87D2782, 0x22D4B87D,
    0x2D8278D7, 0x727D88D2, 0x7D8E1782, 0x7872D1E8,
    0x8D24EB17, 0xDD8722B4, 0x8D28D727, 0x82D8771E,
    0x8728D72D, 0x72D788D2, 0x287D287D, 0xD2D78368,
)


def block_of(yh, zl):
    block = jnp.int32(0)
    for y in range(4):
        for n in range(4):
            block = jnp.where((yh == y) & (zl == PLACE[y][n]), n, block)
    return block


def y_target(zl, yh, yl):
    return ((2 * yh + yl + 8 - 2 * zl) % 8 + 3) // 4 % 2


def spread():
    pairs = []
    for source in range(4**3 * 4):
        zh, zl, yh, core, yl = source // 64, source // 16 % 4, source // 4 % 4, source // 2 % 2, source % 2
        target_yl = y_target(zl, yh, yl)
        turn = TURNS[zh * 4 + zl] >> (yh * 8 + yl * 4 + core * 2) & 3
        target = (turn * 4 + PLACE[zl][zh]) * 4 + zl
        pairs.append((source, (target * 2 + core) * 2 + target_yl))
    return pairs


def around(size, near):
    return [((i + near) % size, i) for i in range(size)]


def two_away():
    near = [2, -2]
    return [
        ((i + near[core]) % PLANES * 2 + core, i * 2 + core) for i in range(PLANES) for core in range(2)
    ]


def local(a_tiles, p_tiles, a_mask, p_mask):
    z = ("zh", "zl")
    mine = stripes(p_tiles, p_mask)
    slab = trim(lax.ppermute(mine, z + ("yh", "core", "yl"), spread()))
    a_tiles, mine = lax.optimization_barrier((a_tiles, mine))
    own, *own_halves = masked_operator(a_tiles, a_mask)
    after = [lax.ppermute(half, "x", around(4, 1)) for half in own_halves]
    before = lax.ppermute(own, "x", around(4, -1))

    above, below = [lax.ppermute(slab, z, around(PLANES, turn)) for turn in (1, -1)]
    slabs = [slab, above, below, lax.ppermute(slab, z + ("core",), two_away())]
    across = [lax.ppermute(half, "x", around(4, 1)) for half in after]
    blocks = [own, before, *after, *across]

    theirs = lax.ppermute(product(slabs, blocks, 1), "core", [(0, 1), (1, 0)])
    coded = encode(product(slabs, blocks, 0), theirs)
    coded = lax.all_to_all(coded, "yh", 0, 0, tiled=True)
    coded = lax.all_to_all(coarse_parts(coded, p_tiles, p_mask), z, 0, 0, tiled=True)
    return summed(coded).T


def solution(mesh):
    fine = Mesh(mesh.devices.reshape(4, 4, 4, 4, 2, 2), ("zh", "zl", "x", "yh", "core", "yl"))
    z, col = ("zh", "zl"), ("x", "yh", "core")
    return jax.shard_map(
        local,
        mesh=fine,
        in_specs=(P(z, col), P(z, None), P(z, col), P(z, None)),
        out_specs=P(z, col + ("yl",)),
        check_vma=False,
    )
```

```python
import functools

import jax
import jax.numpy as jnp
from jax import lax
from jax.experimental import pallas as pl
from jax.experimental.pallas import tpu as pltpu
from jax.sharding import Mesh
from jax.sharding import PartitionSpec as P

TILE = 192
WIDE = 48
ROWS = 768
HALF = 384
COARSE = 3072
PLANES = 16
LIMIT = 32766.0
STEPS = 128.0
EMPTY = 16
LEAST = 1e-33
GROUPS = ROWS // 128
CODED = 80
VMEM = 16 * 1024 * 1024
MOST_VMEM = 57 * 1024 * 1024
F32 = jnp.float32
BF16 = jnp.bfloat16


def params():
    return pltpu.CompilerParams(vmem_limit_bytes=VMEM)


def dot_last(left, right):
    return lax.dot_general(left, right, (((1,), (1,)), ((), ())), preferred_element_type=F32)


def stripes_kernel(mask_in, tiles, out, window, mask, arrived, mask_arrived):
    core, x = lax.axis_index("core"), lax.axis_index("x")
    yl = y_target(lax.axis_index("zl"), lax.axis_index("yh"), lax.axis_index("yl"))
    mask_copy = pltpu.make_async_copy(mask_in, mask, mask_arrived)
    mask_copy.start()
    copies = []
    for n in range(2):
        rows = pl.ds(pl.multiple_of(core * HALF, HALF), HALF)
        columns = pl.ds(pl.multiple_of((2 * x + n) * HALF, HALF), HALF)
        copies.append(pltpu.make_async_copy(tiles.at[rows, columns], window.at[n], arrived.at[n]))
        copies[n].start()
    row = lax.broadcasted_iota(jnp.int32, (WIDE, HALF), 0)
    lane = lax.broadcasted_iota(jnp.int32, (WIDE, HALF), 1)
    picks = [(lane == row + (2 * s + yl) * WIDE).astype(F32).astype(BF16) for s in range(4)]
    pick = jnp.concatenate(picks, axis=0)
    fine = lax.broadcasted_iota(jnp.int32, (1, HALF), 1)
    out[8 * WIDE :, :] = jnp.zeros((EMPTY, HALF), BF16)
    mask_copy.wait()
    for n in range(2):
        copies[n].wait()
        picked = dot_last(pick, window[n])
        for m in range(2):
            tile = 4 * x + 2 * n + m
            upper, lower = mask[2 * core, tile], mask[2 * core + 1, tile]
            present = jnp.where(fine < TILE, upper.astype(F32), lower.astype(F32))
            part = picked[2 * WIDE * m : 2 * WIDE * (m + 1)]
            first = 2 * WIDE * (2 * n + m)
            out[first : first + 2 * WIDE, :] = (part * present).astype(BF16)


def stripes(p_tiles, p_mask):
    return pl.pallas_call(
        stripes_kernel,
        out_shape=jax.ShapeDtypeStruct((8 * WIDE + EMPTY, HALF), BF16),
        in_specs=[pl.BlockSpec(memory_space=pl.ANY)] * 2,
        out_specs=pl.BlockSpec(memory_space=pltpu.VMEM),
        scratch_shapes=[
            pltpu.VMEM((2, HALF, HALF), BF16),
            pltpu.SMEM(p_mask.shape, jnp.int32),
            pltpu.SemaphoreType.DMA((2,)),
            pltpu.SemaphoreType.DMA,
        ],
        compiler_params=pltpu.CompilerParams(vmem_limit_bytes=MOST_VMEM),
        name="stripes",
    )(p_mask, p_tiles)


def mask_rows(mask, tiles, out, first):
    height, width = tiles.shape
    lane = lax.broadcasted_iota(jnp.int32, (1, width), 1)
    for i in range(height // TILE):
        present = jnp.zeros((1, width), F32)
        for k in range(width // TILE):
            inside = (lane >= k * TILE) & (lane < (k + 1) * TILE)
            present = jnp.where(inside, mask(i, first + k).astype(F32), present)
        rows = slice(i * TILE, (i + 1) * TILE)
        out[rows, :] = tiles[rows, :] * present.astype(BF16)


def operator_kernel(mask, tiles, out):
    mask_rows(lambda i, k: mask[k, i], tiles, out.at[0], 0)
    for n in range(1, 4):
        out[n] = out[0]


def masked_operator(a_tiles, a_mask):
    return pl.pallas_call(
        operator_kernel,
        out_shape=jax.ShapeDtypeStruct((4,) + a_tiles.shape, BF16),
        in_specs=[pl.BlockSpec(memory_space=pltpu.SMEM), pl.BlockSpec(memory_space=pltpu.VMEM)],
        out_specs=pl.BlockSpec(memory_space=pltpu.VMEM),
        compiler_params=params(),
        name="masked_operator",
    )(a_mask.T, a_tiles)


def trim_kernel(padded, out):
    out[...] = padded[: 8 * WIDE, :]


def trim(padded):
    return pl.pallas_call(
        trim_kernel,
        out_shape=jax.ShapeDtypeStruct((8 * WIDE, HALF), BF16),
        in_specs=[pl.BlockSpec(memory_space=pltpu.VMEM)],
        out_specs=pl.BlockSpec(memory_space=pltpu.VMEM),
        compiler_params=params(),
        name="trim",
    )(padded)


def product_kernel(other, *refs):
    slabs, blocks, out, columns = refs[:4], refs[4], refs[5], refs[6]
    zl, yh = lax.axis_index("zl"), lax.axis_index("yh")
    core = (lax.axis_index("core") + other) % 2
    for n, slab in zip((0, 1, 3, 2), slabs):
        block = block_of(yh, (zl + n) % 4)
        for y in range(4):
            rows = pl.ds(pl.multiple_of((2 * y + core) * WIDE, WIDE), WIDE)
            columns[block, y * WIDE : (y + 1) * WIDE] = slab[rows, :]
    total = dot_last(columns[0], blocks[0])
    for n in range(1, 4):
        total = total + dot_last(columns[n], blocks[n])
    out[...] = total.reshape(4, WIDE, ROWS)


def product(slabs, blocks, other):
    return pl.pallas_call(
        functools.partial(product_kernel, other),
        out_shape=jax.ShapeDtypeStruct((4, WIDE, ROWS), F32),
        in_specs=[pl.BlockSpec(memory_space=pltpu.VMEM)] * 5,
        out_specs=pl.BlockSpec(memory_space=pltpu.VMEM),
        scratch_shapes=[pltpu.VMEM((4, 4 * WIDE, HALF), BF16)],
        compiler_params=params(),
        name="product_for_other" if other else "product",
    )(*slabs, blocks)


def scale_code(most):
    return jnp.ceil(jnp.log2(jnp.maximum(most, LEAST)) * STEPS) + 1.0


def encode_kernel(mine, theirs, out):
    for n in range(4):
        codes = []
        for g in range(GROUPS):
            lanes = slice(g * 128, (g + 1) * 128)
            values = mine[n, :, lanes] + theirs[n, :, lanes]
            codes.append(scale_code(jnp.max(jnp.abs(values), axis=0, keepdims=True)))
            values = jnp.round(values * (LIMIT * jnp.exp2(codes[g] * (-1.0 / STEPS))))
            out[n, g * WIDE : (g + 1) * WIDE, :] = values.astype(jnp.int32).astype(jnp.int16)
        codes = jnp.concatenate(codes + [jnp.zeros((8 - GROUPS, 128), F32)], axis=0)
        out[n, GROUPS * WIDE :, :] = codes.astype(jnp.int32).astype(jnp.int16)


def encode(mine, theirs):
    return pl.pallas_call(
        encode_kernel,
        out_shape=jax.ShapeDtypeStruct((4, GROUPS * WIDE + 8, 128), jnp.int16),
        in_specs=[pl.BlockSpec(memory_space=pltpu.VMEM)] * 2,
        out_specs=pl.BlockSpec(memory_space=pltpu.VMEM),
        compiler_params=params(),
        name="encode",
    )(mine, theirs)


def decoded_sum(coded):
    total = [jnp.zeros((WIDE, 128), F32)] * GROUPS
    for n in range(4):
        codes = coded[n, GROUPS * WIDE :, :].astype(jnp.int32).astype(F32)
        scales = jnp.exp2(codes * (1.0 / STEPS)) * (1.0 / LIMIT)
        for g in range(GROUPS):
            values = coded[n, g * WIDE : (g + 1) * WIDE, :].astype(jnp.int32).astype(F32)
            total[g] = total[g] + values * scales[g : g + 1]
    return jnp.concatenate(total, axis=1)


def pack(values):
    tail = values[:, 128:]
    return jnp.concatenate(
        [values[:, :128], jnp.concatenate([tail[:24], tail[24:]], axis=1)], axis=0
    )


def coarse_kernel(mask, parts, tiles, out, present):
    whole = decoded_sum(parts)
    high = whole.astype(BF16)
    terms = jnp.concatenate([high, (whole - high.astype(F32)).astype(BF16)], axis=0)
    width = present.shape[1]
    for n in range(COARSE // width):
        first = n * (width // TILE)
        block = tiles.at[:, n * width : (n + 1) * width]
        mask_rows(lambda i, k: mask[i, k], block, present, first)
        full = jnp.dot(terms, present[...], preferred_element_type=F32)
        full = full[:WIDE] + full[WIDE:]
        for k in range(width // TILE):
            chunk = full[:, k * TILE : (k + 1) * TILE]
            code = scale_code(jnp.max(jnp.abs(chunk), axis=0, keepdims=True))
            factor = LIMIT * jnp.exp2(code * (-1.0 / STEPS))
            values = pack(jnp.round(chunk * factor))
            scales = pack(jnp.broadcast_to(code, (WIDE, TILE)))
            empty = jnp.zeros((6, 128), F32)
            coded = jnp.concatenate([values, scales[:1], scales[48:49], empty], axis=0)
            out[first + k] = coded.astype(jnp.int32).astype(jnp.int16)


def coarse_parts(parts, p_tiles, p_mask):
    vmem = pl.BlockSpec(memory_space=pltpu.VMEM)
    return pl.pallas_call(
        coarse_kernel,
        out_shape=jax.ShapeDtypeStruct((PLANES, CODED, 128), jnp.int16),
        in_specs=[pl.BlockSpec(memory_space=pltpu.SMEM), vmem, vmem],
        out_specs=vmem,
        scratch_shapes=[pltpu.VMEM((ROWS, COARSE // 4), BF16)],
        compiler_params=params(),
        name="coarse_parts",
    )(p_mask, parts, p_tiles)


def sum_kernel(coded, out):
    total = jnp.zeros((72, 128), F32)
    for z in range(PLANES):
        block = coded[z].astype(jnp.int32).astype(F32)
        scale = jnp.exp2(block[72:80] * (1.0 / STEPS)) * (1.0 / LIMIT)
        factor = jnp.concatenate(
            [jnp.broadcast_to(scale[:1], (48, 128)), jnp.broadcast_to(scale[1:2], (24, 128))], axis=0
        )
        total = total + block[:72] * factor
    out[:, :128] = total[:48]
    out[:24, 128:] = total[48:, :64]
    out[24:, 128:] = total[48:, 64:]


def summed(coded):
    return pl.pallas_call(
        sum_kernel,
        out_shape=jax.ShapeDtypeStruct((WIDE, TILE), F32),
        in_specs=[pl.BlockSpec(memory_space=pltpu.VMEM)],
        out_specs=pl.BlockSpec(memory_space=pltpu.VMEM),
        compiler_params=params(),
        name="summed",
    )(coded)


PLACE = ((0, 1, 2, 3), (2, 0, 1, 3), (1, 3, 0, 2), (3, 2, 1, 0))
TURNS = (
    0x8D28D637, 0x778E1D82, 0xD87D2782, 0x22D4B87D,
    0x2D8278D7, 0x727D88D2, 0x7D8E1782, 0x7872D1E8,
    0x8D24EB17, 0xDD8722B4, 0x8D28D727, 0x82D8771E,
    0x8728D72D, 0x72D788D2, 0x287D287D, 0xD2D78368,
)


def block_of(yh, zl):
    block = jnp.int32(0)
    for y in range(4):
        for n in range(4):
            block = jnp.where((yh == y) & (zl == PLACE[y][n]), n, block)
    return block


def y_target(zl, yh, yl):
    return ((2 * yh + yl + 8 - 2 * zl) % 8 + 3) // 4 % 2


def spread():
    pairs = []
    for source in range(4**3 * 4):
        zh, zl, yh, core, yl = source // 64, source // 16 % 4, source // 4 % 4, source // 2 % 2, source % 2
        target_yl = y_target(zl, yh, yl)
        turn = TURNS[zh * 4 + zl] >> (yh * 8 + yl * 4 + core * 2) & 3
        target = (turn * 4 + PLACE[zl][zh]) * 4 + zl
        pairs.append((source, (target * 2 + core) * 2 + target_yl))
    return pairs


def around(size, near):
    return [((i + near) % size, i) for i in range(size)]


def two_away():
    near = [2, -2]
    return [
        ((i + near[core]) % PLANES * 2 + core, i * 2 + core) for i in range(PLANES) for core in range(2)
    ]


def local(a_tiles, p_tiles, a_mask, p_mask):
    z = ("zh", "zl")
    mine = stripes(p_tiles, p_mask)
    slab = trim(lax.ppermute(mine, z + ("yh", "core", "yl"), spread()))
    a_tiles, mine = lax.optimization_barrier((a_tiles, mine))
    blocks = lax.all_to_all(masked_operator(a_tiles, a_mask), "x", 0, 0, tiled=True)

    above, below = [lax.ppermute(slab, z, around(PLANES, turn)) for turn in (1, -1)]
    slabs = [slab, above, below, lax.ppermute(slab, z + ("core",), two_away())]

    theirs = lax.ppermute(product(slabs, blocks, 1), "core", [(0, 1), (1, 0)])
    coded = encode(product(slabs, blocks, 0), theirs)
    coded = lax.all_to_all(coded, "yh", 0, 0, tiled=True)
    coded = lax.all_to_all(coarse_parts(coded, p_tiles, p_mask), z, 0, 0, tiled=True)
    return summed(coded).T


def solution(mesh):
    fine = Mesh(mesh.devices.reshape(4, 4, 4, 4, 2, 2), ("zh", "zl", "x", "yh", "core", "yl"))
    z, col = ("zh", "zl"), ("x", "yh", "core")
    return jax.shard_map(
        local,
        mesh=fine,
        in_specs=(P(z, col), P(z, None), P(z, col), P(z, None)),
        out_specs=P(z, col + ("yl",)),
        check_vma=False,
    )
```

```python
import functools

import jax
import jax.numpy as jnp
from jax import lax
from jax.experimental import pallas as pl
from jax.experimental.pallas import tpu as pltpu
from jax.sharding import Mesh
from jax.sharding import PartitionSpec as P

TILE = 192
WIDE = 48
ROWS = 768
HALF = 384
COARSE = 3072
PLANES = 16
LIMIT = 32766.0
STEPS = 128.0
EMPTY = 16
LEAST = 1e-33
GROUPS = ROWS // 128
CODED = 80
VMEM = 16 * 1024 * 1024
MOST_VMEM = 57 * 1024 * 1024
F32 = jnp.float32
BF16 = jnp.bfloat16


def params():
    return pltpu.CompilerParams(vmem_limit_bytes=VMEM)


def dot_last(left, right):
    return lax.dot_general(left, right, (((1,), (1,)), ((), ())), preferred_element_type=F32)


def stripes_kernel(mask_in, tiles, out, window, mask, arrived, mask_arrived):
    core, x = lax.axis_index("core"), lax.axis_index("x")
    yl = y_target(lax.axis_index("zl"), lax.axis_index("yh"), lax.axis_index("yl"))
    mask_copy = pltpu.make_async_copy(mask_in, mask, mask_arrived)
    mask_copy.start()
    copies = []
    for n in range(2):
        rows = pl.ds(pl.multiple_of(core * HALF, HALF), HALF)
        columns = pl.ds(pl.multiple_of((2 * x + n) * HALF, HALF), HALF)
        copies.append(pltpu.make_async_copy(tiles.at[rows, columns], window.at[n], arrived.at[n]))
        copies[n].start()
    row = lax.broadcasted_iota(jnp.int32, (WIDE, HALF), 0)
    lane = lax.broadcasted_iota(jnp.int32, (WIDE, HALF), 1)
    picks = [(lane == row + (2 * s + yl) * WIDE).astype(F32).astype(BF16) for s in range(4)]
    pick = jnp.concatenate(picks, axis=0)
    fine = lax.broadcasted_iota(jnp.int32, (1, HALF), 1)
    out[8 * WIDE :, :] = jnp.zeros((EMPTY, HALF), BF16)
    mask_copy.wait()
    for n in range(2):
        copies[n].wait()
        picked = dot_last(pick, window[n])
        for m in range(2):
            tile = 4 * x + 2 * n + m
            upper, lower = mask[2 * core, tile], mask[2 * core + 1, tile]
            present = jnp.where(fine < TILE, upper.astype(F32), lower.astype(F32))
            part = picked[2 * WIDE * m : 2 * WIDE * (m + 1)]
            first = 2 * WIDE * (2 * n + m)
            out[first : first + 2 * WIDE, :] = (part * present).astype(BF16)


def stripes(p_tiles, p_mask):
    return pl.pallas_call(
        stripes_kernel,
        out_shape=jax.ShapeDtypeStruct((8 * WIDE + EMPTY, HALF), BF16),
        in_specs=[pl.BlockSpec(memory_space=pl.ANY)] * 2,
        out_specs=pl.BlockSpec(memory_space=pltpu.VMEM),
        scratch_shapes=[
            pltpu.VMEM((2, HALF, HALF), BF16),
            pltpu.SMEM(p_mask.shape, jnp.int32),
            pltpu.SemaphoreType.DMA((2,)),
            pltpu.SemaphoreType.DMA,
        ],
        compiler_params=pltpu.CompilerParams(vmem_limit_bytes=MOST_VMEM),
        name="stripes",
    )(p_mask, p_tiles)


def mask_rows(mask, tiles, out, first):
    height, width = tiles.shape
    lane = lax.broadcasted_iota(jnp.int32, (1, width), 1)
    for i in range(height // TILE):
        present = jnp.zeros((1, width), F32)
        for k in range(width // TILE):
            inside = (lane >= k * TILE) & (lane < (k + 1) * TILE)
            present = jnp.where(inside, mask(i, first + k).astype(F32), present)
        rows = slice(i * TILE, (i + 1) * TILE)
        out[rows, :] = tiles[rows, :] * present.astype(BF16)


def operator_kernel(mask, tiles, upper, lower):
    for half, out in enumerate((upper, lower)):
        rows = tiles[half * HALF : (half + 1) * HALF, :]
        mask_rows(lambda i, k: mask[k, 2 * half + i], rows, out, 0)


def masked_operator(a_tiles, a_mask):
    return pl.pallas_call(
        operator_kernel,
        out_shape=[jax.ShapeDtypeStruct((HALF, HALF), BF16)] * 2,
        in_specs=[pl.BlockSpec(memory_space=pltpu.SMEM), pl.BlockSpec(memory_space=pltpu.VMEM)],
        out_specs=[pl.BlockSpec(memory_space=pltpu.VMEM)] * 2,
        compiler_params=params(),
        name="masked_operator",
    )(a_mask.T, a_tiles)


def trim_kernel(padded, out):
    out[...] = padded[: 8 * WIDE, :]


def trim(padded):
    return pl.pallas_call(
        trim_kernel,
        out_shape=jax.ShapeDtypeStruct((8 * WIDE, HALF), BF16),
        in_specs=[pl.BlockSpec(memory_space=pltpu.VMEM)],
        out_specs=pl.BlockSpec(memory_space=pltpu.VMEM),
        compiler_params=params(),
        name="trim",
    )(padded)


def add_terms(total, left, blocks, number, x):
    for n in range(4):

        @pl.when((number - x + 4) % 4 == n)
        def _():
            for half in range(2):
                lanes = slice(half * HALF, (half + 1) * HALF)
                total[:, lanes] += dot_last(left, blocks[2 * n + half][...])


def early_kernel(slab, two_away, *refs):
    blocks, out = refs[:8], refs[8]
    x, zl, yh = lax.axis_index("x"), lax.axis_index("zl"), lax.axis_index("yh")
    out[...] = jnp.zeros_like(out)
    add_terms(out, slab[...], blocks, block_of(yh, zl), x)
    add_terms(out, two_away[: 8 * WIDE, :], blocks, block_of(yh, (zl + 2) % 4), x)


def early_terms(slab, two_away, blocks):
    vmem = pl.BlockSpec(memory_space=pltpu.VMEM)
    return pl.pallas_call(
        early_kernel,
        out_shape=jax.ShapeDtypeStruct((8 * WIDE, ROWS), F32),
        in_specs=[vmem] * 10,
        out_specs=vmem,
        compiler_params=params(),
        name="early_terms",
    )(slab, two_away, *blocks)


def product_kernel(other, early, above, below, *refs):
    blocks, out, left, total = refs[:8], refs[8], refs[9], refs[10]
    x, zl, yh = lax.axis_index("x"), lax.axis_index("zl"), lax.axis_index("yh")
    core = (lax.axis_index("core") + other) % 2
    for y in range(4):
        rows = pl.ds(pl.multiple_of((2 * y + core) * WIDE, WIDE), WIDE)
        into = slice(y * WIDE, (y + 1) * WIDE)
        left[0, into], left[1, into], total[into] = above[rows, :], below[rows, :], early[rows, :]
    add_terms(total, left[0], blocks, block_of(yh, (zl + 1) % 4), x)
    add_terms(total, left[1], blocks, block_of(yh, (zl + 3) % 4), x)
    out[...] = total[...].reshape(4, WIDE, ROWS)


def product(early, above, below, blocks, other):
    return pl.pallas_call(
        functools.partial(product_kernel, other),
        out_shape=jax.ShapeDtypeStruct((4, WIDE, ROWS), F32),
        in_specs=[pl.BlockSpec(memory_space=pltpu.VMEM)] * 11,
        out_specs=pl.BlockSpec(memory_space=pltpu.VMEM),
        scratch_shapes=[pltpu.VMEM((2, 4 * WIDE, HALF), BF16), pltpu.VMEM((4 * WIDE, ROWS), F32)],
        compiler_params=params(),
        name="product_for_other" if other else "product",
    )(early, above, below, *blocks)


def scale_code(most):
    return jnp.ceil(jnp.log2(jnp.maximum(most, LEAST)) * STEPS) + 1.0


def encode_kernel(mine, theirs, out):
    for n in range(4):
        codes = []
        for g in range(GROUPS):
            lanes = slice(g * 128, (g + 1) * 128)
            values = mine[n, :, lanes] + theirs[n, :, lanes]
            codes.append(scale_code(jnp.max(jnp.abs(values), axis=0, keepdims=True)))
            values = jnp.round(values * (LIMIT * jnp.exp2(codes[g] * (-1.0 / STEPS))))
            out[n, g * WIDE : (g + 1) * WIDE, :] = values.astype(jnp.int32).astype(jnp.int16)
        codes = jnp.concatenate(codes + [jnp.zeros((8 - GROUPS, 128), F32)], axis=0)
        out[n, GROUPS * WIDE :, :] = codes.astype(jnp.int32).astype(jnp.int16)


def encode(mine, theirs):
    return pl.pallas_call(
        encode_kernel,
        out_shape=jax.ShapeDtypeStruct((4, GROUPS * WIDE + 8, 128), jnp.int16),
        in_specs=[pl.BlockSpec(memory_space=pltpu.VMEM)] * 2,
        out_specs=pl.BlockSpec(memory_space=pltpu.VMEM),
        compiler_params=params(),
        name="encode",
    )(mine, theirs)


def decoded_sum(coded):
    total = [jnp.zeros((WIDE, 128), F32)] * GROUPS
    for n in range(4):
        codes = coded[n, GROUPS * WIDE :, :].astype(jnp.int32).astype(F32)
        scales = jnp.exp2(codes * (1.0 / STEPS)) * (1.0 / LIMIT)
        for g in range(GROUPS):
            values = coded[n, g * WIDE : (g + 1) * WIDE, :].astype(jnp.int32).astype(F32)
            total[g] = total[g] + values * scales[g : g + 1]
    return jnp.concatenate(total, axis=1)


def pack(values):
    tail = values[:, 128:]
    return jnp.concatenate(
        [values[:, :128], jnp.concatenate([tail[:24], tail[24:]], axis=1)], axis=0
    )


def coarse_kernel(mask, parts, tiles, out, present):
    whole = decoded_sum(parts)
    high = whole.astype(BF16)
    terms = jnp.concatenate([high, (whole - high.astype(F32)).astype(BF16)], axis=0)
    width = present.shape[1]
    for n in range(COARSE // width):
        first = n * (width // TILE)
        block = tiles.at[:, n * width : (n + 1) * width]
        mask_rows(lambda i, k: mask[i, k], block, present, first)
        full = jnp.dot(terms, present[...], preferred_element_type=F32)
        full = full[:WIDE] + full[WIDE:]
        for k in range(width // TILE):
            chunk = full[:, k * TILE : (k + 1) * TILE]
            code = scale_code(jnp.max(jnp.abs(chunk), axis=0, keepdims=True))
            factor = LIMIT * jnp.exp2(code * (-1.0 / STEPS))
            values = pack(jnp.round(chunk * factor))
            scales = pack(jnp.broadcast_to(code, (WIDE, TILE)))
            empty = jnp.zeros((6, 128), F32)
            coded = jnp.concatenate([values, scales[:1], scales[48:49], empty], axis=0)
            out[first + k] = coded.astype(jnp.int32).astype(jnp.int16)


def coarse_parts(parts, p_tiles, p_mask):
    vmem = pl.BlockSpec(memory_space=pltpu.VMEM)
    return pl.pallas_call(
        coarse_kernel,
        out_shape=jax.ShapeDtypeStruct((PLANES, CODED, 128), jnp.int16),
        in_specs=[pl.BlockSpec(memory_space=pltpu.SMEM), vmem, vmem],
        out_specs=vmem,
        scratch_shapes=[pltpu.VMEM((ROWS, COARSE // 4), BF16)],
        compiler_params=params(),
        name="coarse_parts",
    )(p_mask, parts, p_tiles)


def sum_kernel(coded, out):
    total = jnp.zeros((72, 128), F32)
    for z in range(PLANES):
        block = coded[z].astype(jnp.int32).astype(F32)
        scale = jnp.exp2(block[72:80] * (1.0 / STEPS)) * (1.0 / LIMIT)
        factor = jnp.concatenate(
            [jnp.broadcast_to(scale[:1], (48, 128)), jnp.broadcast_to(scale[1:2], (24, 128))], axis=0
        )
        total = total + block[:72] * factor
    out[:, :128] = total[:48]
    out[:24, 128:] = total[48:, :64]
    out[24:, 128:] = total[48:, 64:]


def summed(coded):
    return pl.pallas_call(
        sum_kernel,
        out_shape=jax.ShapeDtypeStruct((WIDE, TILE), F32),
        in_specs=[pl.BlockSpec(memory_space=pltpu.VMEM)],
        out_specs=pl.BlockSpec(memory_space=pltpu.VMEM),
        compiler_params=params(),
        name="summed",
    )(coded)


PLACE = ((0, 1, 2, 3), (2, 0, 1, 3), (1, 3, 0, 2), (3, 2, 1, 0))
TURNS = (
    0x8D28D637, 0x778E1D82, 0xD87D2782, 0x22D4B87D,
    0x2D8278D7, 0x727D88D2, 0x7D8E1782, 0x7872D1E8,
    0x8D24EB17, 0xDD8722B4, 0x8D28D727, 0x82D8771E,
    0x8728D72D, 0x72D788D2, 0x287D287D, 0xD2D78368,
)


def block_of(yh, zl):
    block = jnp.int32(0)
    for y in range(4):
        for n in range(4):
            block = jnp.where((yh == y) & (zl == PLACE[y][n]), n, block)
    return block


def y_target(zl, yh, yl):
    return ((2 * yh + yl + 8 - 2 * zl) % 8 + 3) // 4 % 2


def spread():
    pairs = []
    for source in range(4**3 * 4):
        zh, zl, yh, core, yl = source // 64, source // 16 % 4, source // 4 % 4, source // 2 % 2, source % 2
        target_yl = y_target(zl, yh, yl)
        turn = TURNS[zh * 4 + zl] >> (yh * 8 + yl * 4 + core * 2) & 3
        target = (turn * 4 + PLACE[zl][zh]) * 4 + zl
        pairs.append((source, (target * 2 + core) * 2 + target_yl))
    return pairs


def around(size, near):
    return [((i + near) % size, i) for i in range(size)]


def two_away():
    near = [2, -2]
    return [
        ((i + near[core]) % PLANES * 2 + core, i * 2 + core) for i in range(PLANES) for core in range(2)
    ]


def local(a_tiles, p_tiles, a_mask, p_mask):
    z = ("zh", "zl")
    mine = stripes(p_tiles, p_mask)
    slab = trim(lax.ppermute(mine, z + ("yh", "core", "yl"), spread()))
    a_tiles, mine = lax.optimization_barrier((a_tiles, mine))
    own = masked_operator(a_tiles, a_mask)
    after = [lax.ppermute(half, "x", around(4, 1)) for half in own]
    before = [lax.ppermute(half, "x", around(4, -1)) for half in own]

    above, below = [lax.ppermute(slab, z, around(PLANES, turn)) for turn in (1, -1)]
    far = lax.ppermute(slab, z + ("core",), two_away())
    across = [
        lax.ppermute(after[0], "x", around(4, 1)),
        lax.ppermute(before[1], "x", around(4, -1)),
    ]
    blocks = [*own, *after, *across, *before]

    early = early_terms(slab, far, blocks)
    theirs = lax.ppermute(product(early, above, below, blocks, 1), "core", [(0, 1), (1, 0)])
    coded = encode(product(early, above, below, blocks, 0), theirs)
    coded = lax.all_to_all(coded, "yh", 0, 0, tiled=True)
    coded = lax.all_to_all(coarse_parts(coded, p_tiles, p_mask), z, 0, 0, tiled=True)
    return summed(coded).T


def solution(mesh):
    fine = Mesh(mesh.devices.reshape(4, 4, 4, 4, 2, 2), ("zh", "zl", "x", "yh", "core", "yl"))
    z, col = ("zh", "zl"), ("x", "yh", "core")
    return jax.shard_map(
        local,
        mesh=fine,
        in_specs=(P(z, col), P(z, None), P(z, col), P(z, None)),
        out_specs=P(z, col + ("yl",)),
        check_vma=False,
    )
```

```python
import functools

import jax
import jax.numpy as jnp
from jax import lax
from jax.experimental import pallas as pl
from jax.experimental.pallas import tpu as pltpu
from jax.sharding import Mesh
from jax.sharding import PartitionSpec as P

TILE = 192
WIDE = 48
ROWS = 768
HALF = 384
COARSE = 3072
PLANES = 16
LIMIT = 32766.0
STEPS = 128.0
EMPTY = 16
LEAST = 1e-33
GROUPS = ROWS // 128
CODED = 80
VMEM = 16 * 1024 * 1024
MOST_VMEM = 57 * 1024 * 1024
F32 = jnp.float32
BF16 = jnp.bfloat16


def params():
    return pltpu.CompilerParams(vmem_limit_bytes=VMEM)


def dot_last(left, right):
    return lax.dot_general(left, right, (((1,), (1,)), ((), ())), preferred_element_type=F32)


def stripes_kernel(mask_in, tiles, out, window, mask, arrived, mask_arrived):
    core, x = lax.axis_index("core"), lax.axis_index("x")
    yl = y_target(lax.axis_index("zl"), lax.axis_index("yh"), lax.axis_index("yl"))
    mask_copy = pltpu.make_async_copy(mask_in, mask, mask_arrived)
    mask_copy.start()
    copies = []
    for n in range(2):
        rows = pl.ds(pl.multiple_of(core * HALF, HALF), HALF)
        columns = pl.ds(pl.multiple_of((2 * x + n) * HALF, HALF), HALF)
        copies.append(pltpu.make_async_copy(tiles.at[rows, columns], window.at[n], arrived.at[n]))
        copies[n].start()
    row = lax.broadcasted_iota(jnp.int32, (WIDE, HALF), 0)
    lane = lax.broadcasted_iota(jnp.int32, (WIDE, HALF), 1)
    picks = [(lane == row + (2 * s + yl) * WIDE).astype(F32).astype(BF16) for s in range(4)]
    pick = jnp.concatenate(picks, axis=0)
    fine = lax.broadcasted_iota(jnp.int32, (1, HALF), 1)
    out[8 * WIDE :, :] = jnp.zeros((EMPTY, HALF), BF16)
    mask_copy.wait()
    for n in range(2):
        copies[n].wait()
        picked = dot_last(pick, window[n])
        for m in range(2):
            tile = 4 * x + 2 * n + m
            upper, lower = mask[2 * core, tile], mask[2 * core + 1, tile]
            present = jnp.where(fine < TILE, upper.astype(F32), lower.astype(F32))
            part = picked[2 * WIDE * m : 2 * WIDE * (m + 1)]
            first = 2 * WIDE * (2 * n + m)
            out[first : first + 2 * WIDE, :] = (part * present).astype(BF16)


def stripes(p_tiles, p_mask):
    return pl.pallas_call(
        stripes_kernel,
        out_shape=jax.ShapeDtypeStruct((8 * WIDE + EMPTY, HALF), BF16),
        in_specs=[pl.BlockSpec(memory_space=pl.ANY)] * 2,
        out_specs=pl.BlockSpec(memory_space=pltpu.VMEM),
        scratch_shapes=[
            pltpu.VMEM((2, HALF, HALF), BF16),
            pltpu.SMEM(p_mask.shape, jnp.int32),
            pltpu.SemaphoreType.DMA((2,)),
            pltpu.SemaphoreType.DMA,
        ],
        compiler_params=pltpu.CompilerParams(vmem_limit_bytes=MOST_VMEM),
        name="stripes",
    )(p_mask, p_tiles)


def mask_rows(mask, tiles, out, first):
    height, width = tiles.shape
    lane = lax.broadcasted_iota(jnp.int32, (1, width), 1)
    for i in range(height // TILE):
        present = jnp.zeros((1, width), F32)
        for k in range(width // TILE):
            inside = (lane >= k * TILE) & (lane < (k + 1) * TILE)
            present = jnp.where(inside, mask(i, first + k).astype(F32), present)
        rows = slice(i * TILE, (i + 1) * TILE)
        out[rows, :] = tiles[rows, :] * present.astype(BF16)


def operator_kernel(mask, tiles, upper, lower):
    for half, out in enumerate((upper, lower)):
        rows = tiles[half * HALF : (half + 1) * HALF, :]
        mask_rows(lambda i, k: mask[k, 2 * half + i], rows, out, 0)


def masked_operator(a_tiles, a_mask):
    return pl.pallas_call(
        operator_kernel,
        out_shape=[jax.ShapeDtypeStruct((HALF, HALF), BF16)] * 2,
        in_specs=[pl.BlockSpec(memory_space=pltpu.SMEM), pl.BlockSpec(memory_space=pltpu.VMEM)],
        out_specs=[pl.BlockSpec(memory_space=pltpu.VMEM)] * 2,
        compiler_params=params(),
        name="masked_operator",
    )(a_mask.T, a_tiles)


def trim_kernel(padded, out):
    out[...] = padded[: 8 * WIDE, :]


def trim(padded):
    return pl.pallas_call(
        trim_kernel,
        out_shape=jax.ShapeDtypeStruct((8 * WIDE, HALF), BF16),
        in_specs=[pl.BlockSpec(memory_space=pltpu.VMEM)],
        out_specs=pl.BlockSpec(memory_space=pltpu.VMEM),
        compiler_params=params(),
        name="trim",
    )(padded)


def product_kernel(other, *refs):
    slabs, blocks, out, columns = refs[:4], refs[4:12], refs[12], refs[13]
    x, zl, yh = lax.axis_index("x"), lax.axis_index("zl"), lax.axis_index("yh")
    core = (lax.axis_index("core") + other) % 2
    for n, slab in zip((0, 1, 3, 2), slabs):
        block = block_of(yh, (zl + n) % 4)
        for y in range(4):
            rows = pl.ds(pl.multiple_of((2 * y + core) * WIDE, WIDE), WIDE)
            columns[block, y * WIDE : (y + 1) * WIDE] = slab[rows, :]
    for half in range(2):
        total = dot_last(columns[x], blocks[half][...])
        for n in range(1, 4):
            total = total + dot_last(columns[(x + n) % 4], blocks[2 * n + half][...])
        out[:, :, half * HALF : (half + 1) * HALF] = total.reshape(4, WIDE, HALF)


def product(slabs, blocks, other):
    return pl.pallas_call(
        functools.partial(product_kernel, other),
        out_shape=jax.ShapeDtypeStruct((4, WIDE, ROWS), F32),
        in_specs=[pl.BlockSpec(memory_space=pltpu.VMEM)] * 12,
        out_specs=pl.BlockSpec(memory_space=pltpu.VMEM),
        scratch_shapes=[pltpu.VMEM((4, 4 * WIDE, HALF), BF16)],
        compiler_params=params(),
        name="product_for_other" if other else "product",
    )(*slabs, *blocks)


def scale_code(most):
    return jnp.ceil(jnp.log2(jnp.maximum(most, LEAST)) * STEPS) + 1.0


def encode_kernel(mine, theirs, out):
    for n in range(4):
        codes = []
        for g in range(GROUPS):
            lanes = slice(g * 128, (g + 1) * 128)
            values = mine[n, :, lanes] + theirs[n, :, lanes]
            codes.append(scale_code(jnp.max(jnp.abs(values), axis=0, keepdims=True)))
            values = jnp.round(values * (LIMIT * jnp.exp2(codes[g] * (-1.0 / STEPS))))
            out[n, g * WIDE : (g + 1) * WIDE, :] = values.astype(jnp.int32).astype(jnp.int16)
        codes = jnp.concatenate(codes + [jnp.zeros((8 - GROUPS, 128), F32)], axis=0)
        out[n, GROUPS * WIDE :, :] = codes.astype(jnp.int32).astype(jnp.int16)


def encode(mine, theirs):
    return pl.pallas_call(
        encode_kernel,
        out_shape=jax.ShapeDtypeStruct((4, GROUPS * WIDE + 8, 128), jnp.int16),
        in_specs=[pl.BlockSpec(memory_space=pltpu.VMEM)] * 2,
        out_specs=pl.BlockSpec(memory_space=pltpu.VMEM),
        compiler_params=params(),
        name="encode",
    )(mine, theirs)


def decoded_sum(coded):
    total = [jnp.zeros((WIDE, 128), F32)] * GROUPS
    for n in range(4):
        codes = coded[n, GROUPS * WIDE :, :].astype(jnp.int32).astype(F32)
        scales = jnp.exp2(codes * (1.0 / STEPS)) * (1.0 / LIMIT)
        for g in range(GROUPS):
            values = coded[n, g * WIDE : (g + 1) * WIDE, :].astype(jnp.int32).astype(F32)
            total[g] = total[g] + values * scales[g : g + 1]
    return jnp.concatenate(total, axis=1)


def pack(values):
    tail = values[:, 128:]
    return jnp.concatenate(
        [values[:, :128], jnp.concatenate([tail[:24], tail[24:]], axis=1)], axis=0
    )


def prolongator_kernel(mask, tiles, out):
    width = COARSE // 4
    for n in range(4):
        columns = slice(n * width, (n + 1) * width)
        first = n * (width // TILE)
        mask_rows(lambda i, k: mask[i, k], tiles.at[:, columns], out.at[:, columns], first)


def masked_prolongator(p_tiles, p_mask):
    vmem = pl.BlockSpec(memory_space=pltpu.VMEM)
    return pl.pallas_call(
        prolongator_kernel,
        out_shape=jax.ShapeDtypeStruct(p_tiles.shape, BF16),
        in_specs=[pl.BlockSpec(memory_space=pltpu.SMEM), vmem],
        out_specs=vmem,
        compiler_params=params(),
        name="masked_prolongator",
    )(p_mask, p_tiles)


def coarse_kernel(parts, tiles, out):
    whole = decoded_sum(parts)
    high = whole.astype(BF16)
    terms = jnp.concatenate([high, (whole - high.astype(F32)).astype(BF16)], axis=0)
    width = COARSE // 4
    for n in range(4):
        first = n * (width // TILE)
        block = tiles[:, n * width : (n + 1) * width]
        full = jnp.dot(terms, block, preferred_element_type=F32)
        full = full[:WIDE] + full[WIDE:]
        for k in range(width // TILE):
            chunk = full[:, k * TILE : (k + 1) * TILE]
            code = scale_code(jnp.max(jnp.abs(chunk), axis=0, keepdims=True))
            factor = LIMIT * jnp.exp2(code * (-1.0 / STEPS))
            values = pack(jnp.round(chunk * factor))
            scales = pack(jnp.broadcast_to(code, (WIDE, TILE)))
            empty = jnp.zeros((6, 128), F32)
            coded = jnp.concatenate([values, scales[:1], scales[48:49], empty], axis=0)
            out[first + k] = coded.astype(jnp.int32).astype(jnp.int16)


def coarse_parts(parts, p_masked):
    return pl.pallas_call(
        coarse_kernel,
        out_shape=jax.ShapeDtypeStruct((PLANES, CODED, 128), jnp.int16),
        in_specs=[pl.BlockSpec(memory_space=pltpu.VMEM)] * 2,
        out_specs=pl.BlockSpec(memory_space=pltpu.VMEM),
        compiler_params=params(),
        name="coarse_parts",
    )(parts, p_masked)


def sum_kernel(coded, out):
    total = jnp.zeros((72, 128), F32)
    for z in range(PLANES):
        block = coded[z].astype(jnp.int32).astype(F32)
        scale = jnp.exp2(block[72:80] * (1.0 / STEPS)) * (1.0 / LIMIT)
        factor = jnp.concatenate(
            [jnp.broadcast_to(scale[:1], (48, 128)), jnp.broadcast_to(scale[1:2], (24, 128))], axis=0
        )
        total = total + block[:72] * factor
    out[:, :128] = total[:48]
    out[:24, 128:] = total[48:, :64]
    out[24:, 128:] = total[48:, 64:]


def summed(coded):
    return pl.pallas_call(
        sum_kernel,
        out_shape=jax.ShapeDtypeStruct((WIDE, TILE), F32),
        in_specs=[pl.BlockSpec(memory_space=pltpu.VMEM)],
        out_specs=pl.BlockSpec(memory_space=pltpu.VMEM),
        compiler_params=params(),
        name="summed",
    )(coded)


PLACE = ((0, 1, 2, 3), (2, 0, 1, 3), (1, 3, 0, 2), (3, 2, 1, 0))
TURNS = (
    0x8D28D637, 0x778E1D82, 0xD87D2782, 0x22D4B87D,
    0x2D8278D7, 0x727D88D2, 0x7D8E1782, 0x7872D1E8,
    0x8D24EB17, 0xDD8722B4, 0x8D28D727, 0x82D8771E,
    0x8728D72D, 0x72D788D2, 0x287D287D, 0xD2D78368,
)


def block_of(yh, zl):
    block = jnp.int32(0)
    for y in range(4):
        for n in range(4):
            block = jnp.where((yh == y) & (zl == PLACE[y][n]), n, block)
    return block


def y_target(zl, yh, yl):
    return ((2 * yh + yl + 8 - 2 * zl) % 8 + 3) // 4 % 2


def spread():
    pairs = []
    for source in range(4**3 * 4):
        zh, zl, yh, core, yl = source // 64, source // 16 % 4, source // 4 % 4, source // 2 % 2, source % 2
        target_yl = y_target(zl, yh, yl)
        turn = TURNS[zh * 4 + zl] >> (yh * 8 + yl * 4 + core * 2) & 3
        target = (turn * 4 + PLACE[zl][zh]) * 4 + zl
        pairs.append((source, (target * 2 + core) * 2 + target_yl))
    return pairs


def around(size, near):
    return [((i + near) % size, i) for i in range(size)]


def two_away():
    near = [2, -2]
    return [
        ((i + near[core]) % PLANES * 2 + core, i * 2 + core) for i in range(PLANES) for core in range(2)
    ]


def local(a_tiles, p_tiles, a_mask, p_mask):
    z = ("zh", "zl")
    mine = stripes(p_tiles, p_mask)
    slab = trim(lax.ppermute(mine, z + ("yh", "core", "yl"), spread()))
    a_tiles, mine = lax.optimization_barrier((a_tiles, mine))
    own = masked_operator(a_tiles, a_mask)
    after = [lax.ppermute(half, "x", around(4, 1)) for half in own]
    before = [lax.ppermute(half, "x", around(4, -1)) for half in own]

    above, below = [lax.ppermute(slab, z, around(PLANES, turn)) for turn in (1, -1)]
    slabs = [slab, above, below, lax.ppermute(slab, z + ("core",), two_away())]
    across = [
        lax.ppermute(after[0], "x", around(4, 1)),
        lax.ppermute(before[1], "x", around(4, -1)),
    ]
    blocks = [*own, *after, *across, *before]

    theirs = lax.ppermute(product(slabs, blocks, 1), "core", [(0, 1), (1, 0)])
    coded = encode(product(slabs, blocks, 0), theirs)
    p_tiles, theirs = lax.optimization_barrier((p_tiles, theirs))
    p_masked = masked_prolongator(p_tiles, p_mask)
    coded = lax.all_to_all(coded, "yh", 0, 0, tiled=True)
    coded = lax.all_to_all(coarse_parts(coded, p_masked), z, 0, 0, tiled=True)
    return summed(coded).T


def solution(mesh):
    fine = Mesh(mesh.devices.reshape(4, 4, 4, 4, 2, 2), ("zh", "zl", "x", "yh", "core", "yl"))
    z, col = ("zh", "zl"), ("x", "yh", "core")
    return jax.shard_map(
        local,
        mesh=fine,
        in_specs=(P(z, col), P(z, None), P(z, col), P(z, None)),
        out_specs=P(z, col + ("yl",)),
        check_vma=False,
    )
```
